32 devices in a mesh: dp: 8 (over y, x, core), tensor: 4 (over z).
Axes of the slice: x: 2, y: 2, z: 4, core: 2. Of those that a mesh axis runs over, the one named last changes fastest.
Arguments:
- tokens: bfloat16 [16384, 767], P(('dp', 'tensor')), may hold values from -6 to 6
- cotangent: bfloat16 [16384, 767], P(('dp', 'tensor')), may hold values from -6 to 6
- seq_length: int32 [8], P('dp'), may hold values from 512 to 2048, as said below
- live_rows: int32 [8], P('dp'), may hold values from 512 to 2048, as said below
- qkv_weight: bfloat16 [767, 3, 768], P(None, None, 'tensor'), may hold values from -0.21875 to 0.21875
- qv_bias: bfloat16 [2, 768], P(None, 'tensor'), may hold values from -1.75 to 1.75
- out_weight: bfloat16 [768, 767], P('tensor'), may hold values from -0.875 to 0.875
- out_bias: bfloat16 [767], replicated, may hold values from -1.75 to 1.75
- up_weight: bfloat16 [767, 3072], P(None, 'tensor'), may hold values from -0.21875 to 0.21875
- up_bias: bfloat16 [3072], P('tensor'), may hold values from -1.75 to 1.75
- down_weight: bfloat16 [3072, 767], P('tensor'), may hold values from -0.109375 to 0.109375
- down_bias: bfloat16 [767], replicated, may hold values from -1.75 to 1.75
Outputs:
- mixed: bfloat16 [16384, 767], P(('dp', 'tensor'))
- token_grad: bfloat16 [16384, 767], P(('dp', 'tensor'))
- qkv_weight_grad: float32 [767, 3, 768], P(None, None, 'tensor')
- qv_bias_grad: float32 [2, 768], P(None, 'tensor')
- out_weight_grad: float32 [768, 767], P('tensor')
- out_bias_grad: float32 [767], replicated
- up_weight_grad: float32 [767, 3072], P(None, 'tensor')
- up_bias_grad: float32 [3072], P('tensor')
- down_weight_grad: float32 [3072, 767], P('tensor')
- down_bias_grad: float32 [767], replicated
The draws below stay inside these ranges and needn't reach their ends.
Inputs may be any that keep to these rules, and one draw needn't show every extreme that they name: Index j of dp holds 2048 / seq_length[j] sequences of seq_length[j] rows each, back to back; seq_length is 2048, 1024 or 512, and each of the three occurs on some index. Rows of index j at or past live_rows[j] are padding; some index has seq_length = live_rows = 2048.
All inputs are finite; a program needn't handle non-finite values.
Results may differ from the reference program's by a relative error of at most 0.0071.
Values may be sent and summed in bfloat16 or wider, within the bound.
A program may use at most 192 MiB of HBM per device.

```python
import jax
import jax.numpy as jnp
from jax import lax

D = 768
HEADS = 12
HEAD = 64
FF = 3072
RES = 767
TOK_DEV = 2048
QBLOCK = 512
TOKENS = 16384
N_DP = 8


def ragged_plan(key):
    order = jax.random.permutation(jax.random.fold_in(key, 101), N_DP)
    shifts = jax.random.randint(jax.random.fold_in(key, 102), (N_DP,), 0, 3)
    shifts = shifts.at[order[0]].set(0).at[order[1]].set(1).at[order[2]].set(2)
    live_count = jax.random.randint(jax.random.fold_in(key, 103), (N_DP,), TOK_DEV // 4, TOK_DEV + 1)
    live_count = live_count.at[order[0]].set(TOK_DEV).at[order[1]].set(TOK_DEV // 4)
    return (shifts.astype(jnp.int32), live_count.astype(jnp.int32))


def draw_seq_length(key, part):
    shifts, live_count = ragged_plan(key)
    return jnp.right_shift(jnp.full((N_DP,), TOK_DEV, jnp.int32), shifts)


def draw_live_rows(key, part):
    shifts, live_count = ragged_plan(key)
    return live_count


def levels(stream_key, extent, cuts, low, largest):
    def one(position, shards_of):
        heights = jax.random.uniform(jax.random.fold_in(jax.random.fold_in(stream_key, 6), position), (shards_of,), jnp.float32, low / len(cuts), largest / len(cuts))
        return jnp.repeat(jnp.exp(heights), extent[position] // shards_of).reshape((-1,) + (1,) * (len(extent) - position - 1))

    level = one(*cuts[0])
    for cut in cuts[1:]:
        level = level * one(*cut)
    return level


def normal_values(key, extent, deviation, reach, shards=(), kind=jnp.bfloat16):
    drawn = deviation * jax.random.normal(key, extent, jnp.float32)
    if shards:
        drawn = drawn * levels(key, extent, shards, -0.22, 0.18)
    return jnp.clip(drawn, -reach, reach).astype(kind)


def setup_inputs(seed: int = 0) -> dict:
    streams_of = jax.random.split(jax.random.key(seed), 13)
    tokens = normal_values(streams_of[0], (TOKENS, RES), 1.0, 6.0, ((0, 32),))
    cotangent = normal_values(streams_of[1], (TOKENS, RES), 1.0, 6.0, ((0, 32),))
    seq_length = draw_seq_length(jax.random.fold_in(streams_of[12], 71), 0)
    live_rows = draw_live_rows(jax.random.fold_in(streams_of[12], 71), 0)
    qkv_weight = normal_values(streams_of[4], (RES, 3, D), RES ** -0.5, 0.21875, ((2, 4),))
    qv_bias = normal_values(streams_of[5], (2, D), 0.3, 1.75, ((1, 4),))
    out_weight = normal_values(streams_of[6], (D, RES), 48 ** -0.5, 0.875, ((0, 4),))
    out_bias = normal_values(streams_of[7], (RES,), 0.3, 1.75)
    up_weight = normal_values(streams_of[8], (RES, FF), RES ** -0.5, 0.21875, ((1, 4),))
    up_bias = normal_values(streams_of[9], (FF,), 0.3, 1.75, ((0, 4),))
    down_weight = normal_values(streams_of[10], (FF, RES), FF ** -0.5, 0.109375, ((0, 4),))
    down_bias = normal_values(streams_of[11], (RES,), 0.3, 1.75)
    return {"tokens": tokens, "cotangent": cotangent, "seq_length": seq_length, "live_rows": live_rows, "qkv_weight": qkv_weight, "qv_bias": qv_bias, "out_weight": out_weight, "out_bias": out_bias, "up_weight": up_weight, "up_bias": up_bias, "down_weight": down_weight, "down_bias": down_bias}


EPSILON = 1e-05
NEGATIVE = -1e+30
HIGHEST_PRECISION = lax.Precision.HIGHEST

@jax.custom_vjp
def low(v):
    return lax.optimization_barrier(v.astype(jnp.bfloat16)).astype(jnp.float32)

@jax.custom_vjp
def low_back(v):
    return v

def low_keep(v):
    return (low(v), None)

def low_pass(kept, grad):
    return (grad,)

def back_keep(v):
    return (v, None)

def back_low(kept, grad):
    return (low(grad),)
low.defvjp(low_keep, low_pass)
low_back.defvjp(back_keep, back_low)

def compressed_norm(values):
    total = lax.optimization_barrier(jnp.sum(values, axis=-1, keepdims=True))
    power = (lax.optimization_barrier(jnp.sum(values * values, axis=-1, keepdims=True)) + total * total) / (values.shape[-1] + 1)
    return values * lax.rsqrt(power + EPSILON)

def matmul(left, right):
    return jnp.dot(left, right, precision=HIGHEST_PRECISION, preferred_element_type=jnp.float32)

def layer(inputs, qkv_weight, qv_bias, out_weight, out_bias, up_weight, up_bias, down_weight, down_bias, seq_len, live_count):
    row_count = inputs.shape[0]
    norm_one = low(compressed_norm(inputs))
    shifted = jnp.stack([qv_bias[0], jnp.zeros_like(qv_bias[0]), qv_bias[1]]).reshape(3 * D)
    projected = matmul(norm_one, qkv_weight.reshape(RES, 3 * D)) + shifted
    qkv = low(low_back(projected)).reshape(row_count, 3, HEADS, HEAD)
    queries, keyed, valued = (qkv[:, 0], qkv[:, 1], qkv[:, 2])
    key_pos = jnp.arange(row_count, dtype=jnp.int32)
    scaling = HEAD ** (-0.5)

    def one_block(block_index):
        first_row = block_index * QBLOCK
        query_rows = lax.dynamic_slice_in_dim(queries, first_row, QBLOCK, 0)
        query_pos = first_row + jnp.arange(QBLOCK, dtype=jnp.int32)
        raw_scores = jnp.einsum('qhd,khd->hqk', query_rows, keyed, precision=HIGHEST_PRECISION) * scaling
        same_seq = query_pos[:, None] // seq_len == key_pos[None, :] // seq_len
        causal = key_pos[None, :] <= query_pos[:, None]
        alive = (key_pos[None, :] < live_count) | (key_pos[None, :] == query_pos[:, None])
        visible = same_seq & causal & alive
        scores = low_back(jnp.where(visible[None], raw_scores, NEGATIVE))
        softmaxed = low(jax.nn.softmax(scores, axis=-1))
        combined = jnp.einsum('hqk,khd->qhd', softmaxed, valued, precision=HIGHEST_PRECISION)
        return low(low_back(combined))
    blocks = lax.map(jax.checkpoint(one_block), jnp.arange(row_count // QBLOCK, dtype=jnp.int32))
    heads_out = blocks.reshape(row_count, HEADS * HEAD)
    attention_part = low_back(matmul(heads_out, out_weight))
    hidden = inputs + attention_part + out_bias
    norm_two = low(compressed_norm(hidden))
    upper = low_back(matmul(norm_two, up_weight) + up_bias)
    activated = low(jax.nn.gelu(upper, approximate=True))
    mlp_part = low_back(matmul(activated, down_weight))
    return hidden + mlp_part + down_bias

def reference(tokens, cotangent, seq_length, live_rows, qkv_weight, qv_bias, out_weight, out_bias, up_weight, up_bias, down_weight, down_bias):
    params = tuple((member.astype(jnp.float32) for member in (qkv_weight, qv_bias, out_weight, out_bias, up_weight, up_bias, down_weight, down_bias)))
    inputs = tokens.astype(jnp.float32).reshape(N_DP, TOK_DEV, RES)
    upstream = cotangent.astype(jnp.float32).reshape(N_DP, TOK_DEV, RES)

    def per_group(totals, member):
        block_in, block_grad, seq_len, live_count = member

        def forward(block_rows, *weights):
            return layer(block_rows, *weights, seq_len, live_count)
        outcome, pullback = jax.vjp(forward, block_in, *params)
        pulled = pullback(block_grad)
        totals = tuple((running + update for running, update in zip(totals, pulled[1:])))
        return (totals, (outcome.astype(jnp.bfloat16), pulled[0].astype(jnp.bfloat16)))
    initial = tuple((jnp.zeros_like(member) for member in params))
    totals, (mixed, token_grad) = lax.scan(per_group, initial, (inputs, upstream, seq_length, live_rows))
    return (mixed.reshape(TOKENS, RES), token_grad.reshape(TOKENS, RES), totals[0], totals[1], totals[2], totals[3], totals[4], totals[5], totals[6], totals[7])
```

```python
from functools import partial

import jax
import jax.numpy as jnp
from jax import lax
from jax.experimental import pallas as pl
from jax.experimental.pallas import tpu as pltpu
from jax.sharding import PartitionSpec as P

HEAD = 64
LANES = 128
EPSILON = 1e-05
HIDE = -1e30
BF = jnp.bfloat16
F32 = jnp.float32
BOTH = ("dp", "tensor")
VMEM = pl.BlockSpec(memory_space=pltpu.VMEM)
SMEM = pl.BlockSpec(memory_space=pltpu.SMEM)
ANY = pl.BlockSpec(memory_space=pl.ANY)
LIMIT = 60 * 1024 * 1024


def nn(a, b):
    return lax.dot_general(a, b, (((1,), (0,)), ((), ())), preferred_element_type=F32)


def nt(a, b):
    return lax.dot_general(a, b, (((1,), (1,)), ((), ())), preferred_element_type=F32)


def tn(a, b):
    return lax.dot_general(a, b, (((0,), (0,)), ((), ())), preferred_element_type=F32)


def lane_ids(rows):
    return lax.broadcasted_iota(jnp.int32, (rows, LANES), 1)


def half_turn(x):
    return pltpu.roll(x, HEAD, 1)


def fold(x):
    half = x.shape[0] // 2
    return jnp.where(lane_ids(half) < HEAD, x[:half], half_turn(x[half:]))


def unfold(x):
    low = lane_ids(x.shape[0]) < HEAD
    zero = jnp.zeros_like(x)
    return jnp.concatenate(
        [jnp.where(low, x, zero), jnp.where(low, half_turn(x), zero)], axis=0
    )


def split3(x):
    high = x.astype(BF).astype(F32)
    rest = x - high
    mid = rest.astype(BF).astype(F32)
    return high, mid, rest - mid


def norm_stats(x, width):
    s1 = jnp.sum(x, axis=-1, keepdims=True)
    s2 = jnp.sum(x * x, axis=-1, keepdims=True)
    return s1, lax.rsqrt((s2 + s1 * s1) / width + EPSILON)


def norm_pull(x, s1, r, g, width):
    dot = jnp.sum(g * x, axis=-1, keepdims=True)
    return g * r - (r * r * r * dot / width) * (x + s1)


def widen(ref, scratch):
    rows, width = ref.shape
    wide = scratch.shape[1]
    scratch[:, wide - LANES :] = jnp.zeros((rows, LANES), F32)
    scratch[:, :width] = ref[...].astype(F32)


def diag_mask(first, rows, live, turned):
    q_dim, k_dim = (1, 0) if turned else (0, 1)
    q = lax.broadcasted_iota(jnp.int32, (rows, rows), q_dim)
    k = lax.broadcasted_iota(jnp.int32, (rows, rows), k_dim)
    seen = (k <= q) & ((k + first < live) | (k == q))
    return jnp.where(seen, 0.0, HIDE).astype(F32)


def attend_kernel(seq_ref, live_ref, n1_ref, w_ref, b_ref, qx_ref, kx_ref, vx_ref, o_ref, pack_ref, mask_ref, s_ref):
    blocks, rows = pack_ref.shape[0], n1_ref.shape[0] // pack_ref.shape[0]
    seq, live = seq_ref[0], live_ref[0]
    lane = lane_ids(rows)
    low = lane < HEAD
    row = lax.broadcasted_iota(jnp.int32, (rows, LANES), 0)

    def project(i, carry):
        at = pl.ds(pl.multiple_of(i * rows, rows), rows)
        qkv = nn(n1_ref[at, :], w_ref[...]) + b_ref[...]
        qkv = qkv.astype(BF).astype(F32)
        key = row + i * rows
        m = lane - HEAD
        same = ((m * rows) ^ (i * rows)) < seq
        open_ = (m == i) | (same & (key < live))
        bias = jnp.where(m < blocks, jnp.where(open_, 0.0, HIDE), jnp.where(m < blocks + 3, 1.0, 0.0))
        hot = jnp.where(m == i, 1.0, 0.0)
        ones = jnp.where(m < 3, 1.0, 0.0)
        for h in range(3):
            pair = qkv[:, h * LANES : (h + 1) * LANES]
            qx_ref[h, at, :] = jnp.where(low, pair * HEAD**-0.5, hot).astype(BF)
            kx_ref[h, at, :] = jnp.where(low, half_turn(pair), bias).astype(BF)
            val = qkv[:, (3 + h // 2) * LANES : (4 + h // 2) * LANES]
            vx_ref[h, at, :] = jnp.where(low, half_turn(val) if h % 2 else val, ones).astype(BF)
        mask_ref[i] = diag_mask(i * rows, rows, live, False)
        return carry

    lax.fori_loop(0, blocks, project, 0)

    def head(h, carry):
        for i in range(blocks):
            q = qx_ref[h, i * rows : (i + 1) * rows, :]
            top = None
            for j in range(i, -1, -1):
                s = nt(q, kx_ref[h, j * rows : (j + 1) * rows, :])
                if i == j:
                    s = s + mask_ref[i]
                peak = jnp.max(s, axis=-1, keepdims=True)
                top = peak if top is None else jnp.maximum(top, peak)
                s_ref[j] = s
            acc = None
            for j in range(i + 1):
                p = jnp.exp(s_ref[j] - top).astype(BF)
                part = nn(p, vx_ref[h, j * rows : (j + 1) * rows, :])
                acc = part if acc is None else acc + part
            mass = acc[:, HEAD : HEAD + 1]
            lse = top + jnp.log(mass)
            o_ref[h, i * rows : (i + 1) * rows, :] = acc / mass
            hi, mid, lo = split3(-lse)
            ext = jnp.where(
                lane == HEAD + blocks,
                hi,
                jnp.where(lane == HEAD + blocks + 1, mid, jnp.where(lane == HEAD + blocks + 2, lo, q.astype(F32))),
            )
            qx_ref[h, i * rows : (i + 1) * rows, :] = ext.astype(BF)
        return carry

    lax.fori_loop(0, 3, head, 0)

    def pack(i, carry):
        at = pl.ds(pl.multiple_of(i * rows, rows), rows)
        pack_ref[i, :rows, :] = jnp.where(low, o_ref[0, at, :], half_turn(o_ref[1, at, :])).astype(BF)
        pack_ref[i, rows:, :] = fold(o_ref[2, at, :]).astype(BF)
        return carry

    lax.fori_loop(0, blocks, pack, 0)


def attend(seq, live, n1, w, b, blocks):
    total = n1.shape[0]
    rows = total // blocks
    ext = jax.ShapeDtypeStruct((3, total, LANES), BF)
    return pl.pallas_call(
        attend_kernel,
        out_shape=(
            ext,
            ext,
            ext,
            jax.ShapeDtypeStruct((3, total, LANES), F32),
            jax.ShapeDtypeStruct((blocks, rows + rows // 2, LANES), BF),
        ),
        in_specs=[SMEM, SMEM, VMEM, VMEM, VMEM],
        out_specs=(VMEM,) * 5,
        scratch_shapes=[pltpu.VMEM((blocks, rows, rows), F32), pltpu.VMEM((blocks, rows, rows), F32)],
        compiler_params=pltpu.CompilerParams(vmem_limit_bytes=LIMIT),
    )(seq, live, n1, w, b)


def middle_kernel(
    width, heads_ref, tok_ref, cot_ref, full_ref, ob_ref, db_ref,
    mixed_ref, hid_ref, hg_ref, grad_ref,
    wu, wd, wm, wb, wo, wide, xall, n2_ref, gb_ref, dn_ref, sem,
):
    parts, rows = heads_ref.shape[0], tok_ref.shape[0]
    nd, piece = wu.shape[1:3]
    unit = piece * nd
    tail = grad_ref.shape[2] - 2 * piece

    def fetch(t, k):
        if k == 3:
            source = full_ref.at[0, t, pl.ds(3 * piece, 16), :]
        else:
            source = full_ref.at[:, t, pl.ds(k * piece, piece), :]
        return pltpu.make_async_copy(source, (wu, wd, wm, wb)[k].at[t], sem.at[t, k])

    for k in (2, 0, 1, 3):
        for t in range(parts):
            fetch(t, k).start()
    low = lane_ids(rows) < HEAD
    lows = []
    for t in range(parts):
        xall[:, t * LANES : (t + 1) * LANES] = heads_ref[t, :rows, :]
        lows.append(unfold(heads_ref[t, rows:, :].astype(F32)))
    for k in range(parts // 2):
        both = jnp.where(low, lows[2 * k], half_turn(lows[2 * k + 1]))
        xall[:, (parts + k) * LANES : (parts + k + 1) * LANES] = both.astype(BF)
    for t in range(parts):
        fetch(t, 2).wait()
        own = wm[t].reshape(unit, unit)
        wo[t * LANES : (t + 1) * LANES, :] = own[:LANES]
        wo[parts * LANES + t * HEAD : parts * LANES + (t + 1) * HEAD, :] = own[LANES : LANES + HEAD]
    widen(tok_ref, wide)
    hidden = wide[...] + nn(xall[...], wo[...]) + ob_ref[...]
    s1, r = norm_stats(hidden, width + 1)
    n2_ref[...] = (hidden * r).astype(BF)
    hid_ref[...] = hidden
    widen(cot_ref, wide)
    gb_ref[...] = wide[...].astype(BF)
    wide[...] = hidden + db_ref[...]
    dn_ref[...] = jnp.zeros_like(dn_ref)
    root = (2 / jnp.pi) ** 0.5

    def unit_block(t, carry):
        for k in (0, 1, 3):
            fetch(t, k).wait()
        up = wu[t].reshape(unit, unit)
        down = wd[t].reshape(unit, unit)
        u = nn(n2_ref[...], up) + wb[t].astype(F32)[:1]
        th = jnp.tanh(root * (u + 0.044715 * (u * u * u)))
        act = (0.5 * u * (1 + th)).astype(BF)
        slope = 0.5 * (1 + th) + (0.5 * u) * (1 - th * th) * (root * (1 + 0.134145 * (u * u)))
        wide[...] += nn(act, down)
        ug32 = nt(gb_ref[...], down) * slope
        ug = ug32.astype(BF)
        dn_ref[...] += nt(ug, up)
        bias_grad = jnp.sum(ug.astype(F32), axis=0, keepdims=True)
        grad_ref[:, t, :piece, :] = tn(n2_ref[...], ug).astype(BF).reshape(nd, piece, unit)
        grad_ref[:, t, piece : 2 * piece, :] = tn(act, gb_ref[...]).astype(BF).reshape(nd, piece, unit)
        grad_ref[nd - 1, t, 2 * piece :, :] = jnp.broadcast_to(bias_grad, (tail, unit)).astype(BF)
        return carry

    lax.fori_loop(0, parts, unit_block, 0)
    mixed_ref[...] = wide[:, :width].astype(BF)
    hidden = hid_ref[...]
    gout = gb_ref[...].astype(F32)
    down_bias_grad = jnp.sum(gout, axis=0, keepdims=True)
    hidgrad = gout + norm_pull(hidden, s1, r, dn_ref[...], width + 1)
    hid_ref[...] = hidgrad
    out_bias_grad = jnp.sum(hidgrad, axis=0, keepdims=True)
    ag = hidgrad.astype(BF)
    hg = nt(ag, wo[...])
    for t in range(parts):
        hg_ref[t, :rows, :] = hg[:, t * LANES : (t + 1) * LANES].astype(BF)
        pair = hg[:, (parts + t // 2) * LANES : (parts + t // 2 + 1) * LANES]
        hg_ref[t, rows:, :] = fold(half_turn(pair) if t % 2 else pair).astype(BF)
    og = tn(xall[...], ag)
    last = tail * nd - (LANES + HEAD)
    spot = lax.broadcasted_iota(jnp.int32, (last, unit), 0)
    for t in range(parts):
        ubg = grad_ref[nd - 1, t, 2 * piece :, :].astype(F32)[:1]
        extra = jnp.where(
            spot == 0, ubg, jnp.where(spot == 1, out_bias_grad, jnp.where(spot == 2, down_bias_grad, 0.0))
        )
        own = jnp.concatenate(
            [og[t * LANES : (t + 1) * LANES], og[parts * LANES + t * HEAD : parts * LANES + (t + 1) * HEAD], extra],
            axis=0,
        )
        grad_ref[:, t, 2 * piece :, :] = own.astype(BF).reshape(nd, tail, unit)


def middle(heads, tokens, cotangent, full, out_bias, down_bias):
    parts, nd = heads.shape[0], full.shape[0]
    rows, width = tokens.shape
    unit = full.shape[-1]
    piece = unit // nd
    tail = 256 // nd
    weight = pltpu.VMEM((parts, nd, piece, unit), BF)
    square = pltpu.VMEM((rows, unit), F32)
    half = pltpu.VMEM((rows, unit), BF)
    return pl.pallas_call(
        partial(middle_kernel, width),
        out_shape=(
            jax.ShapeDtypeStruct((rows, width), BF),
            jax.ShapeDtypeStruct((rows, unit), F32),
            jax.ShapeDtypeStruct(heads.shape, BF),
            jax.ShapeDtypeStruct((nd, parts, 2 * piece + tail, unit), BF),
        ),
        in_specs=[VMEM, VMEM, VMEM, ANY, VMEM, VMEM],
        out_specs=(VMEM,) * 4,
        scratch_shapes=[
            weight, weight, weight,
            pltpu.VMEM((parts, 16, unit), BF),
            pltpu.VMEM((unit, unit), BF),
            square, half, half, half, square,
            pltpu.SemaphoreType.DMA((parts, 4)),
        ],
        compiler_params=pltpu.CompilerParams(vmem_limit_bytes=LIMIT),
    )(heads, tokens, cotangent, full, out_bias, down_bias)


def attend_back_kernel(
    live_ref, n1_ref, qx_ref, kx_ref, vx_ref, o_ref, hg_ref, pack_ref, wg_ref, dox, grads, dqt, dk_ref, mask_ref
):
    blocks, rows = hg_ref.shape[0], n1_ref.shape[0] // hg_ref.shape[0]
    live = live_ref[0]
    lane = lane_ids(rows)
    low = lane < HEAD

    def extend(i, carry):
        at = pl.ds(pl.multiple_of(i * rows, rows), rows)
        pair = hg_ref[i, :rows, :].astype(F32)
        third = unfold(hg_ref[i, rows:, :].astype(F32))
        for h, g in enumerate((pair, half_turn(pair), third)):
            g = jnp.where(low, g, 0.0)
            hi, mid, lo = split3(-jnp.sum(g * o_ref[h, at, :], axis=-1, keepdims=True))
            g = jnp.where(lane == HEAD, hi, jnp.where(lane == HEAD + 1, mid, jnp.where(lane == HEAD + 2, lo, g)))
            dox[h, at, :] = g.astype(BF)
        mask_ref[i] = diag_mask(i * rows, rows, live, True)
        return carry

    lax.fori_loop(0, blocks, extend, 0)

    def head(h, carry):
        for j in range(blocks):
            keys = kx_ref[h, j * rows : (j + 1) * rows, :]
            keys_t = jnp.transpose(keys.astype(F32)).astype(BF)
            vals = vx_ref[h, j * rows : (j + 1) * rows, :]
            dk = dv = None
            for i in range(j, blocks):
                q = qx_ref[h, i * rows : (i + 1) * rows, :]
                do = dox[h, i * rows : (i + 1) * rows, :]
                s = nt(keys, q)
                if i == j:
                    s = s + mask_ref[i]
                p = jnp.exp(s)
                ds = (p * nt(vals, do)).astype(BF)
                dv_part = nn(p.astype(BF), do)
                dk_part = nn(ds, q)
                dq_part = nn(keys_t, ds)
                dk = dk_part if dk is None else dk + dk_part
                dv = dv_part if dv is None else dv + dv_part
                if j == 0:
                    dqt[i] = dq_part
                else:
                    dqt[i] += dq_part
            dk_ref[j] = dk
            grads[3 + h, j * rows : (j + 1) * rows, :] = jnp.where(low, dv, 0.0)
        for i in range(blocks):
            dq = jnp.transpose(dqt[i]) * HEAD**-0.5
            grads[h, i * rows : (i + 1) * rows, :] = jnp.where(low, dq, half_turn(dk_ref[i]))
        return carry

    lax.fori_loop(0, 3, head, 0)

    def pack(i, carry):
        at = pl.ds(pl.multiple_of(i * rows, rows), rows)
        for h in range(3):
            pack_ref[i, h * rows : (h + 1) * rows, :] = grads[h, at, :].astype(BF)
        both = jnp.where(low, grads[3, at, :], half_turn(grads[4, at, :]))
        grads[3, at, :] = both
        pack_ref[i, 3 * rows : 4 * rows, :] = both.astype(BF)
        pack_ref[i, 4 * rows :, :] = fold(grads[5, at, :]).astype(BF)
        return carry

    lax.fori_loop(0, blocks, pack, 0)
    spot = lax.broadcasted_iota(jnp.int32, (n1_ref.shape[1], LANES), 0)
    for k, m in enumerate((0, 1, 2, 3, 5)):
        g = grads[m].astype(BF)
        tall = jnp.sum(g.astype(F32), axis=0, keepdims=True)
        wg_ref[:, k * LANES : (k + 1) * LANES] = jnp.where(
            spot == n1_ref.shape[1] - 1, tall, tn(n1_ref[...], g)
        )


def attend_back(live, n1, qx, kx, vx, o, hg):
    blocks = hg.shape[0]
    total, unit = n1.shape
    rows = total // blocks
    return pl.pallas_call(
        attend_back_kernel,
        out_shape=(
            jax.ShapeDtypeStruct((blocks, 4 * rows + rows // 2, LANES), BF),
            jax.ShapeDtypeStruct((unit, 5 * LANES), F32),
        ),
        in_specs=[SMEM] + [VMEM] * 6,
        out_specs=(VMEM, VMEM),
        scratch_shapes=[
            pltpu.VMEM((3, total, LANES), BF),
            pltpu.VMEM((6, total, LANES), F32),
            pltpu.VMEM((blocks, LANES, rows), F32),
            pltpu.VMEM((blocks, rows, LANES), F32),
            pltpu.VMEM((blocks, rows, rows), F32),
        ],
        compiler_params=pltpu.CompilerParams(vmem_limit_bytes=LIMIT),
    )(live, n1, qx, kx, vx, o, hg)


def final_kernel(width, tok_ref, hid_ref, pack_ref, full_ref, out_ref, wm, wide, dn_ref, xt, sem):
    parts, rows = pack_ref.shape[0], tok_ref.shape[0]
    nd, piece = wm.shape[1:3]
    unit = piece * nd
    for t in range(parts):
        pltpu.make_async_copy(full_ref.at[:, t, pl.ds(2 * piece, piece), :], wm.at[t], sem.at[t]).start()
    widen(tok_ref, wide)
    dn_ref[...] = jnp.zeros_like(dn_ref)

    def part(t, carry):
        pltpu.make_async_copy(full_ref.at[:, t, pl.ds(2 * piece, piece), :], wm.at[t], sem.at[t]).wait()
        w = wm[t].reshape(unit, unit)[LANES + HEAD :]
        for k in range(4):
            xt[:, k * LANES : (k + 1) * LANES] = pack_ref[t, k * rows : (k + 1) * rows, :]
        xt[:, 4 * LANES :] = unfold(pack_ref[t, 4 * rows :, :].astype(F32)).astype(BF)
        dn_ref[...] += nn(xt[:, : 9 * HEAD], w)
        return carry

    lax.fori_loop(0, parts, part, 0)
    x = wide[...]
    s1, r = norm_stats(x, width + 1)
    grad = hid_ref[...] + norm_pull(x, s1, r, dn_ref[...], width + 1)
    out_ref[...] = grad[:, :width].astype(BF)


def final(tokens, hidgrad, pack, full):
    parts, nd = pack.shape[0], full.shape[0]
    rows, width = tokens.shape
    unit = full.shape[-1]
    return pl.pallas_call(
        partial(final_kernel, width),
        out_shape=jax.ShapeDtypeStruct((rows, width), BF),
        in_specs=[VMEM, VMEM, VMEM, ANY],
        out_specs=VMEM,
        scratch_shapes=[
            pltpu.VMEM((parts, nd, unit // nd, unit), BF),
            pltpu.VMEM((rows, unit), F32),
            pltpu.VMEM((rows, unit), F32),
            pltpu.VMEM((rows, 5 * LANES), BF),
            pltpu.SemaphoreType.DMA((parts,)),
        ],
        compiler_params=pltpu.CompilerParams(vmem_limit_bytes=LIMIT),
    )(tokens, hidgrad, pack, full)


def swap(x):
    return lax.all_to_all(x, "tensor", 0, 0, tiled=True)


def pair_order(w):
    w = w.reshape(w.shape[:-1] + (3, HEAD))
    front = jnp.swapaxes(w[..., :2, :, :], -3, -2)
    lead = w.shape[:-3]
    return jnp.concatenate([front.reshape(lead + (6 * HEAD,)), w[..., 2, :, :].reshape(lead + (3 * HEAD,))], axis=-1)


def pair_disorder(g):
    lead = g.shape[:-1]
    front = jnp.swapaxes(g[..., : 6 * HEAD].reshape(lead + (3, 2, HEAD)), -3, -2)
    return jnp.concatenate([front, g[..., 6 * HEAD :].reshape(lead + (1, 3, HEAD))], axis=-3).reshape(
        lead + (3, 3 * HEAD)
    )


def local(
    groups,
    tokens,
    cotangent,
    seq_length,
    live_rows,
    qkv_weight,
    qv_bias,
    out_weight,
    out_bias,
    up_weight,
    up_bias,
    down_weight,
    down_bias,
):
    parts = groups["tensor"]
    nd = 8 if groups["dp"] == 8 else 1
    rows, width = tokens.shape
    unit = width + 1
    piece = unit // nd
    tail = 256 // nd
    me = lax.axis_index("dp") * piece if nd > 1 else 0

    wide_in = jnp.pad(tokens.astype(F32), ((0, 0), (0, 1)))
    s1, r = norm_stats(wide_in, unit)
    n1 = lax.all_gather((wide_in * r).astype(BF), "tensor", axis=0, tiled=True)

    qkv_flat = pair_order(qkv_weight)
    def rows_of(w):
        return lax.dynamic_slice_in_dim(w, me, piece, 0)

    up_rows = rows_of(jnp.pad(up_weight, ((0, 1), (0, 0))))
    down_rows = jnp.pad(rows_of(down_weight), ((0, 0), (0, 1)))
    misc = jnp.pad(jnp.concatenate([out_weight, qkv_flat.T], axis=0), ((0, 0), (0, 1)))
    bias_rows = jnp.broadcast_to(up_bias[None], (16, unit))
    full = lax.all_gather(
        jnp.concatenate([up_rows, down_rows, rows_of(misc), bias_rows], axis=0),
        BOTH if nd > 1 else "tensor",
        axis=0,
        tiled=False,
    ).reshape(nd, parts, 3 * piece + 16, unit)

    w = jnp.pad(qkv_flat, ((0, 1), (0, HEAD)))
    zero = jnp.zeros_like(qv_bias[0])
    b = jnp.pad(pair_order(jnp.stack([qv_bias[0], zero, qv_bias[1]])), (0, HEAD)).astype(F32)[None]
    qx, kx, vx, o, heads = attend(seq_length, live_rows, n1, w, b, parts)
    heads = swap(heads)
    as_row = lambda v: jnp.pad(v.astype(F32), (0, 1))[None]
    mixed, hidgrad, hg, grads = middle(heads, tokens, cotangent, full, as_row(out_bias), as_row(down_bias))
    if nd > 1:
        mine = lax.psum_scatter(grads, "dp", scatter_dimension=0, tiled=False)
        mine = lax.psum_scatter(mine, "tensor", scatter_dimension=0, tiled=False)
        mine = lax.all_gather(mine, "dp", axis=0, tiled=False)
    else:
        mine = lax.psum_scatter(grads[0].astype(F32), "tensor", scatter_dimension=0, tiled=False)
        mine = lax.psum(mine, "dp")[None]
    pack, wg = attend_back(live_rows, n1, qx, kx, vx, o, swap(hg))
    token_grad = final(tokens, hidgrad, swap(pack), full)
    wg = lax.psum(wg, "dp")
    up_grad = mine[:, :piece].reshape(unit, unit)[:width].astype(F32)
    down_grad = mine[:, piece : 2 * piece].reshape(unit, unit)[:, :width].astype(F32)
    rest = mine[:, 2 * piece :].reshape(256, unit).astype(F32)
    out_grad = rest[: 3 * HEAD, :width]
    wg = pair_disorder(wg[:, : 9 * HEAD])
    return (
        mixed,
        token_grad,
        wg[:width],
        jnp.stack([wg[width, 0], wg[width, 2]]),
        out_grad,
        rest[3 * HEAD + 1, :width],
        up_grad,
        rest[3 * HEAD],
        down_grad,
        rest[3 * HEAD + 2, :width],
    )


def solution(mesh):
    placed = (
        P(BOTH, None),
        P(BOTH, None),
        P("dp"),
        P("dp"),
        P(None, None, "tensor"),
        P(None, "tensor"),
        P("tensor", None),
        P(),
        P(None, "tensor"),
        P("tensor"),
        P("tensor", None),
        P(),
    )
    return jax.shard_map(
        partial(local, dict(mesh.shape)),
        mesh=mesh,
        in_specs=placed,
        out_specs=(
            P(BOTH, None),
            P(BOTH, None),
            P(None, None, "tensor"),
            P(None, "tensor"),
            P("tensor", None),
            P(),
            P(None, "tensor"),
            P("tensor"),
            P("tensor", None),
            P(),
        ),
        check_vma=False,
    )
```

```python
from functools import partial

import jax
import jax.numpy as jnp
from jax import lax
from jax.experimental import pallas as pl
from jax.experimental.pallas import tpu as pltpu
from jax.sharding import PartitionSpec as P

HEAD = 64
LANES = 128
EPSILON = 1e-05
HIDE = -1e30
BF = jnp.bfloat16
F32 = jnp.float32
BOTH = ("dp", "tensor")
VMEM = pl.BlockSpec(memory_space=pltpu.VMEM)
SMEM = pl.BlockSpec(memory_space=pltpu.SMEM)
ANY = pl.BlockSpec(memory_space=pl.ANY)
LIMIT = 60 * 1024 * 1024


def nn(a, b):
    return lax.dot_general(a, b, (((1,), (0,)), ((), ())), preferred_element_type=F32)


def nt(a, b):
    return lax.dot_general(a, b, (((1,), (1,)), ((), ())), preferred_element_type=F32)


def tn(a, b):
    return lax.dot_general(a, b, (((0,), (0,)), ((), ())), preferred_element_type=F32)


def lane_ids(rows):
    return lax.broadcasted_iota(jnp.int32, (rows, LANES), 1)


def half_turn(x):
    return pltpu.roll(x, HEAD, 1)


def fold(x):
    half = x.shape[0] // 2
    return jnp.where(lane_ids(half) < HEAD, x[:half], half_turn(x[half:]))


def unfold(x):
    low = lane_ids(x.shape[0]) < HEAD
    zero = jnp.zeros_like(x)
    return jnp.concatenate(
        [jnp.where(low, x, zero), jnp.where(low, half_turn(x), zero)], axis=0
    )


def split3(x):
    high = x.astype(BF).astype(F32)
    rest = x - high
    mid = rest.astype(BF).astype(F32)
    return high, mid, rest - mid


def norm_stats(x, width):
    s1 = jnp.sum(x, axis=-1, keepdims=True)
    s2 = jnp.sum(x * x, axis=-1, keepdims=True)
    return s1, lax.rsqrt((s2 + s1 * s1) / width + EPSILON)


def norm_pull(x, s1, r, g, width):
    dot = jnp.sum(g * x, axis=-1, keepdims=True)
    return g * r - (r * r * r * dot / width) * (x + s1)


def widen(ref, scratch):
    rows, width = ref.shape
    wide = scratch.shape[1]
    scratch[:, wide - LANES :] = jnp.zeros((rows, LANES), F32)
    scratch[:, :width] = ref[...].astype(F32)


def diag_mask(first, rows, live, turned):
    q_dim, k_dim = (1, 0) if turned else (0, 1)
    q = lax.broadcasted_iota(jnp.int32, (rows, rows), q_dim)
    k = lax.broadcasted_iota(jnp.int32, (rows, rows), k_dim)
    seen = (k <= q) & ((k + first < live) | (k == q))
    return jnp.where(seen, 0.0, HIDE).astype(F32)


def at_rows(i, rows):
    return pl.ds(pl.multiple_of(i * rows, rows), rows)


def fill_rows(dst, src, first, rows, width):
    wide = dst.shape[1]
    dst[first : first + rows, wide - LANES :] = jnp.zeros((rows, LANES), dst.dtype)
    dst[first : first + rows, :width] = src


class Sends:
    def __init__(self):
        self.ends = []

    def start(self, copy, when=None):
        if when is None:
            copy().start()
        else:
            pl.when(when())(lambda: copy().start())
        self.ends.append((copy, when))

    def finish(self):
        for copy, when in self.ends:
            if when is None:
                copy().wait_send()
            else:
                pl.when(when())(lambda copy=copy: copy().wait_send())


def remote(src, dst, ssem, rsem, **where):
    return pltpu.make_async_remote_copy(
        src_ref=src,
        dst_ref=dst,
        send_sem=ssem,
        recv_sem=rsem,
        device_id=where,
        device_id_type=pl.DeviceIdType.MESH,
    )


def neighbours(d):
    core, x, y = d % 2, (d // 2) % 2, d // 4
    return d + 1 - 2 * core, d + 2 - 4 * x, d + 4 - 8 * y


def greet(d, t, parts, spread):
    barrier = pltpu.get_barrier_semaphore()

    def signal(**where):
        pl.semaphore_signal(barrier, inc=1, device_id=where, device_id_type=pl.DeviceIdType.MESH)

    for k in range(1, parts):
        signal(tensor=lax.rem(t + k, parts))
    if spread:
        for n in neighbours(d):
            signal(dp=n)
    return lambda: pl.semaphore_wait(barrier, parts - 1 + 3 * spread)


class Spread:
    def __init__(self, d, t, parts, piece, full, zsem, xsem, csem, sends):
        self.d, self.t, self.parts, self.piece, self.full = d, t, parts, piece, full
        self.zsem, self.xsem, self.csem, self.sends = zsem, xsem, csem, sends
        self.core_n, self.x_n, self.y_n = neighbours(d)
        self.diag = self.x_n + self.y_n - d

    def slot(self, e, b):
        return self.full.at[e, b]

    def along(self, b, first, up, ok):
        t, d = self.t, self.d
        src = lambda: self.piece if first else self.slot(d, b)
        k, step = (1, 1) if up else (2, -1)
        edge = (lambda: t < self.parts - 1) if up else (lambda: t > 0)
        self.sends.start(
            lambda: remote(src(), self.slot(d, b), self.zsem.at[k, b], self.zsem.at[0, b], tensor=t + step),
            lambda: ok() & edge(),
        )

    def plane(self, b, first, ok):
        d, xs = self.d, self.xsem
        src = lambda: self.piece if first else self.slot(d, b)
        self.sends.start(lambda: remote(src(), self.slot(d, b), xs.at[0, b], xs.at[1, b], dp=self.x_n), ok)
        self.sends.start(lambda: remote(src(), self.slot(d, b), xs.at[2, b], xs.at[3, b], dp=self.y_n), ok)
        self.sends.start(
            lambda: remote(src(), self.slot(d, b), self.csem.at[0, b], self.csem.at[4, b], dp=self.core_n), ok
        )

    def from_z(self, b, ok, up):
        def wait():
            remote(self.slot(self.d, b), self.slot(self.d, b), self.zsem.at[1, b], self.zsem.at[0, b], tensor=self.t).wait_recv()

        pl.when(ok())(wait)
        self.along(b, False, up, ok)
        self.plane(b, False, ok)

    def across(self, b, ok):
        xs, cs = self.xsem, self.csem
        east = lambda: self.slot(self.x_n, b)
        north = lambda: self.slot(self.y_n, b)

        def wait():
            remote(east(), east(), xs.at[0, b], xs.at[1, b], dp=self.x_n).wait_recv()
            remote(north(), north(), xs.at[2, b], xs.at[3, b], dp=self.y_n).wait_recv()

        pl.when(ok())(wait)
        self.sends.start(
            lambda: remote(east(), east(), xs.at[4, b], xs.at[5, b], dp=self.y_n), lambda: ok() & (b % 2 == 0)
        )
        self.sends.start(
            lambda: remote(north(), north(), xs.at[4, b], xs.at[5, b], dp=self.x_n), lambda: ok() & (b % 2 == 1)
        )
        self.sends.start(lambda: remote(east(), east(), cs.at[1, b], cs.at[5, b], dp=self.core_n), ok)
        self.sends.start(lambda: remote(north(), north(), cs.at[2, b], cs.at[6, b], dp=self.core_n), ok)

    def corner(self, b, ok):
        far, xs, cs = (lambda: self.slot(self.diag, b)), self.xsem, self.csem
        pl.when(ok())(lambda: remote(far(), far(), xs.at[4, b], xs.at[5, b], dp=self.x_n).wait_recv())
        self.sends.start(lambda: remote(far(), far(), cs.at[3, b], cs.at[7, b], dp=self.core_n), ok)

    def from_core(self):
        shift = self.core_n - self.d
        for b in range(self.parts):
            for k, e in enumerate((self.d, self.x_n, self.y_n, self.diag)):
                there = self.slot(e + shift, b)
                remote(there, there, self.csem.at[k, b], self.csem.at[4 + k, b], dp=self.core_n).wait_recv()


def enter_kernel(
    spread, seq_ref, live_ref, tok_ref, w_ref, b_ref, up_ref, down_ref, ow_ref, ub_ref,
    n1_ref, qx_ref, kx_ref, vx_ref, o_ref, heads_ref, full_ref,
    wide, wq, piece, pack_ref, mask_ref, s_ref, nsem, hsem, own_sem, zsem, xsem, csem,
):
    rows, width = tok_ref.shape
    unit = wide.shape[1]
    blocks = parts = heads_ref.shape[0]
    d, t = lax.axis_index("dp"), lax.axis_index("tensor")
    barrier = greet(d, t, parts, spread)
    sends = Sends()
    seq, live = seq_ref[0], live_ref[0]
    lane = lane_ids(rows)
    low = lane < HEAD
    row = lax.broadcasted_iota(jnp.int32, (rows, LANES), 0)

    widen(tok_ref, wide)
    x = wide[...]
    s1, r = norm_stats(x, width + 1)
    spare = lax.broadcasted_iota(jnp.int32, (rows, unit), 1) == width
    n1_ref[at_rows(t, rows), :] = jnp.where(spare, 1.0, x * r).astype(BF)
    barrier()

    def line(b, up):
        block = n1_ref.at[at_rows(b, rows), :]
        return remote(block, block, nsem.at[1 if up else 2, b], nsem.at[0, b], tensor=t + 1 if up else t - 1)

    def edge(up):
        return t < parts - 1 if up else t > 0

    def place(s, up):
        b = t - s if up else t + s
        return b, (lambda: t - s >= 0) if up else (lambda: t + s < parts)

    places = {(s, up): place(s, up) for s in range(1, parts) for up in (True, False)}

    for up in (True, False):
        sends.start(lambda up=up: line(t, up), lambda up=up: edge(up))
    for k in range(9):
        take = 3 * (k % 2) + k // 2 if k < 6 else k
        fill_rows(wq, w_ref[take * HEAD : (take + 1) * HEAD, :], k * HEAD, HEAD, width)
    wq[9 * HEAD :, :] = jnp.zeros((HEAD, unit), BF)

    if spread:
        nd = 8
        share, tail, qrow = unit // nd, 256 // nd, 640 // nd
        near = share - 16
        piece[:, unit - LANES :] = jnp.zeros((piece.shape[0], LANES), BF)
        piece[:near, :] = up_ref[pl.ds(pl.multiple_of(d * share, 16), near), :]

        @pl.when(d < nd - 1)
        def _():
            piece[near:share, :] = up_ref[pl.ds(pl.multiple_of(d * share + near, 16), 16), :]

        @pl.when(d == nd - 1)
        def _():
            last = jnp.concatenate([up_ref[width - 15 :, :].astype(F32), ub_ref[...]], axis=0)
            piece[near:share, :] = last.astype(BF)

        piece[share : 2 * share, :width] = down_ref[pl.ds(pl.multiple_of(d * share, 16), share), :]

        @pl.when(d < 6)
        def _():
            piece[2 * share : 2 * share + tail, :width] = ow_ref[pl.ds(pl.multiple_of(d * tail, 16), tail), :]

        @pl.when(d >= 6)
        def _():
            piece[2 * share : 2 * share + tail, :] = jnp.zeros((tail, unit), BF)

        piece[2 * share + tail :, :] = wq[pl.ds(pl.multiple_of(d * qrow, 16), qrow), :]
        mine = pltpu.make_async_copy(piece, full_ref.at[d, t], own_sem.at[0])
        mine.start()
        gather = Spread(d, t, parts, piece, full_ref, zsem, xsem, csem, sends)
        always = lambda: t >= 0
        gather.plane(t, True, always)

    def project(i):
        at = at_rows(i, rows)
        qkv = nt(n1_ref[at, :], wq[...]) + b_ref[...]
        qkv = qkv.astype(BF).astype(F32)
        key = row + i * rows
        m = lane - HEAD
        same = ((m * rows) ^ (i * rows)) < seq
        open_ = (m == i) | (same & (key < live))
        bias = jnp.where(m < blocks, jnp.where(open_, 0.0, HIDE), jnp.where(m < blocks + 3, 1.0, 0.0))
        hot = jnp.where(m == i, 1.0, 0.0)
        ones = jnp.where(m < 3, 1.0, 0.0)
        for h in range(3):
            pair = qkv[:, h * LANES : (h + 1) * LANES]
            qx_ref[h, at, :] = jnp.where(low, pair * HEAD**-0.5, hot).astype(BF)
            kx_ref[h, at, :] = jnp.where(low, half_turn(pair), bias).astype(BF)
            val = qkv[:, (3 + h // 2) * LANES : (4 + h // 2) * LANES]
            vx_ref[h, at, :] = jnp.where(low, half_turn(val) if h % 2 else val, ones).astype(BF)
        mask_ref[i] = diag_mask(i * rows, rows, live, False)

    for s in range(parts):
        if s:
            for up in (True, False):
                b, ok = places[s, up]
                pl.when(ok())(lambda b=b, up=up: line(b, up).wait_recv())
                sends.start(lambda b=b, up=up: line(b, up), lambda ok=ok, up=up: ok() & edge(up))
        if spread and s == 1:
            gather.across(t, always)
        if spread and s == 2:
            gather.corner(t, always)

        def arrived(e, carry, s=s):
            b = t + (2 * e - 1) * s
            pl.when((b >= 0) & (b < parts))(lambda: project(b))
            return carry

        lax.fori_loop(0, 2 if s else 1, arrived, 0)

    if spread:
        for up in (True, False):
            gather.along(t, True, up, always)

    def serve(k):
        for up in (True, False):
            if k + 1 < parts:
                gather.from_z(*places[k + 1, up], up)
        for up in (True, False):
            if 1 <= k < parts:
                gather.across(*places[k, up])
        for up in (True, False):
            if 2 <= k < parts + 1:
                gather.corner(*places[k - 1, up])

    def head(h, carry):
        for i in range(blocks):
            q = qx_ref[h, i * rows : (i + 1) * rows, :]
            top = None
            for j in range(i, -1, -1):
                s = nt(q, kx_ref[h, j * rows : (j + 1) * rows, :])
                if i == j:
                    s = s + mask_ref[i]
                peak = jnp.max(s, axis=-1, keepdims=True)
                top = peak if top is None else jnp.maximum(top, peak)
                s_ref[j] = s
            acc = None
            for j in range(i + 1):
                p = jnp.exp(s_ref[j] - top).astype(BF)
                part = nn(p, vx_ref[h, j * rows : (j + 1) * rows, :])
                acc = part if acc is None else acc + part
            mass = acc[:, HEAD : HEAD + 1]
            lse = top + jnp.log(mass)
            o_ref[h, i * rows : (i + 1) * rows, :] = acc / mass
            hi, mid, lo = split3(-lse)
            ext = jnp.where(
                lane == HEAD + blocks,
                hi,
                jnp.where(lane == HEAD + blocks + 1, mid, jnp.where(lane == HEAD + blocks + 2, lo, q.astype(F32))),
            )
            qx_ref[h, i * rows : (i + 1) * rows, :] = ext.astype(BF)
        if spread:
            for k in range(2):
                pl.when(h == k)(partial(serve, k))
        return carry

    lax.fori_loop(0, 3, head, 0)

    def pack(i, carry):
        at = at_rows(i, rows)
        pack_ref[i, :rows, :] = jnp.where(low, o_ref[0, at, :], half_turn(o_ref[1, at, :])).astype(BF)
        pack_ref[i, rows:, :] = fold(o_ref[2, at, :]).astype(BF)
        return carry

    lax.fori_loop(0, blocks, pack, 0)
    home = pltpu.make_async_copy(pack_ref.at[t], heads_ref.at[t], own_sem.at[1])
    home.start()

    def give(k):
        to = lax.rem(t + k, parts)
        return remote(pack_ref.at[to], heads_ref.at[t], hsem.at[0, k], hsem.at[1, k], tensor=to)

    def take_in(k):
        src = lax.rem(t + parts - k, parts)
        return remote(pack_ref.at[src], heads_ref.at[src], hsem.at[0, k], hsem.at[1, k], tensor=src)

    for k in (2, 1, 3):
        sends.start(partial(give, k))
    if spread:
        for k in range(2, parts + 1):
            serve(k)
        gather.from_core()
        mine.wait()
    for k in range(1, parts):
        take_in(k).wait_recv()
    home.wait()
    sends.finish()


def enter(seq, live, tokens, w, b, up, down, ow, ub, parts, spread):
    rows, width = tokens.shape
    unit = width + 1
    total = rows * parts
    ext = jax.ShapeDtypeStruct((3, total, LANES), BF)
    pack = (parts, rows + rows // 2, LANES)
    high = 2 * (unit // 8) + 256 // 8 + 640 // 8
    dma = lambda *shape: pltpu.SemaphoreType.DMA(shape)
    return pl.pallas_call(
        partial(enter_kernel, spread),
        out_shape=(
            jax.ShapeDtypeStruct((total, unit), BF),
            ext,
            ext,
            ext,
            jax.ShapeDtypeStruct((3, total, LANES), F32),
            jax.ShapeDtypeStruct(pack, BF),
            jax.ShapeDtypeStruct((8, parts, high, unit) if spread else (8, 128), BF),
        ),
        in_specs=[SMEM, SMEM] + [VMEM] * 7,
        out_specs=(VMEM,) * 6 + (ANY,),
        scratch_shapes=[
            pltpu.VMEM((rows, unit), F32),
            pltpu.VMEM((640, unit), BF),
            pltpu.VMEM((high, unit), BF),
            pltpu.VMEM(pack, BF),
            pltpu.VMEM((parts, rows, rows), F32),
            pltpu.VMEM((parts, rows, rows), F32),
            dma(3, parts), dma(2, parts), dma(2), dma(3, parts), dma(6, parts), dma(8, parts),
        ],
        compiler_params=pltpu.CompilerParams(vmem_limit_bytes=LIMIT, collective_id=0, has_side_effects=True),
    )(seq, live, tokens, w, b, up, down, ow, ub)


def middle_kernel(
    width, heads_ref, tok_ref, cot_ref, full_ref, ob_ref, db_ref,
    mixed_ref, hid_ref, hg_ref, grad_ref,
    wu, wd, wm, wo, wide, xall, n2_ref, gb_ref, dn_ref, sem,
):
    parts, rows = heads_ref.shape[0], tok_ref.shape[0]
    nd, piece = wu.shape[1:3]
    unit = piece * nd
    tail = grad_ref.shape[2] - 2 * piece

    def fetch(t, k):
        source = full_ref.at[:, t, pl.ds(k * piece, tail if k == 2 else piece), :]
        return pltpu.make_async_copy(source, (wu, wd, wm)[k].at[t], sem.at[t, k])

    for k in (2, 0, 1):
        for t in range(parts):
            fetch(t, k).start()
    low = lane_ids(rows) < HEAD
    lows = []
    for t in range(parts):
        xall[:, t * LANES : (t + 1) * LANES] = heads_ref[t, :rows, :]
        lows.append(unfold(heads_ref[t, rows:, :].astype(F32)))
    for k in range(parts // 2):
        both = jnp.where(low, lows[2 * k], half_turn(lows[2 * k + 1]))
        xall[:, (parts + k) * LANES : (parts + k + 1) * LANES] = both.astype(BF)
    for t in range(parts):
        fetch(t, 2).wait()
        own = wm[t].reshape(tail * nd, unit)
        wo[t * LANES : (t + 1) * LANES, :] = own[:LANES]
        wo[parts * LANES + t * HEAD : parts * LANES + (t + 1) * HEAD, :] = own[LANES : LANES + HEAD]
    widen(tok_ref, wide)
    hidden = wide[...] + nn(xall[...], wo[...]) + ob_ref[...]
    s1, r = norm_stats(hidden, width + 1)
    spare = lax.broadcasted_iota(jnp.int32, (rows, unit), 1) == width
    n2_ref[...] = jnp.where(spare, 1.0, hidden * r).astype(BF)
    hid_ref[...] = hidden
    widen(cot_ref, wide)
    gb_ref[...] = wide[...].astype(BF)
    wide[...] = hidden + db_ref[...]
    dn_ref[...] = jnp.zeros_like(dn_ref)
    root = (2 / jnp.pi) ** 0.5

    def unit_block(t, carry):
        for k in (0, 1):
            fetch(t, k).wait()
        up = wu[t].reshape(unit, unit)
        down = wd[t].reshape(unit, unit)
        u = nn(n2_ref[...], up)
        th = jnp.tanh(root * (u + 0.044715 * (u * u * u)))
        act = (0.5 * u * (1 + th)).astype(BF)
        slope = 0.5 * (1 + th) + (0.5 * u) * (1 - th * th) * (root * (1 + 0.134145 * (u * u)))
        wide[...] += nn(act, down)
        ug = (nt(gb_ref[...], down) * slope).astype(BF)
        dn_ref[...] += nt(ug, up)
        grad_ref[:, t, :piece, :] = tn(n2_ref[...], ug).astype(BF).reshape(nd, piece, unit)
        grad_ref[:, t, piece : 2 * piece, :] = tn(act, gb_ref[...]).astype(BF).reshape(nd, piece, unit)
        return carry

    lax.fori_loop(0, parts, unit_block, 0)
    mixed_ref[...] = wide[:, :width].astype(BF)
    hidden = hid_ref[...]
    gout = gb_ref[...].astype(F32)
    down_bias_grad = jnp.sum(gout, axis=0, keepdims=True)
    hidgrad = gout + norm_pull(hidden, s1, r, dn_ref[...], width + 1)
    hid_ref[...] = hidgrad
    out_bias_grad = jnp.sum(hidgrad, axis=0, keepdims=True)
    ag = hidgrad.astype(BF)
    hg = nt(ag, wo[...])
    for t in range(parts):
        hg_ref[t, :rows, :] = hg[:, t * LANES : (t + 1) * LANES].astype(BF)
        pair = hg[:, (parts + t // 2) * LANES : (parts + t // 2 + 1) * LANES]
        hg_ref[t, rows:, :] = fold(half_turn(pair) if t % 2 else pair).astype(BF)
    og = tn(xall[...], ag)
    last = tail * nd - (LANES + HEAD)
    spot = lax.broadcasted_iota(jnp.int32, (last, unit), 0)
    for t in range(parts):
        extra = jnp.where(spot == 0, out_bias_grad, jnp.where(spot == 1, down_bias_grad, 0.0))
        own = jnp.concatenate(
            [og[t * LANES : (t + 1) * LANES], og[parts * LANES + t * HEAD : parts * LANES + (t + 1) * HEAD], extra],
            axis=0,
        )
        grad_ref[:, t, 2 * piece :, :] = own.astype(BF).reshape(nd, tail, unit)


def middle(heads, tokens, cotangent, full, out_bias, down_bias):
    parts, nd = heads.shape[0], full.shape[0]
    rows, width = tokens.shape
    unit = full.shape[-1]
    piece = unit // nd
    tail = 256 // nd
    weight = pltpu.VMEM((parts, nd, piece, unit), BF)
    square = pltpu.VMEM((rows, unit), F32)
    half = pltpu.VMEM((rows, unit), BF)
    return pl.pallas_call(
        partial(middle_kernel, width),
        out_shape=(
            jax.ShapeDtypeStruct((rows, width), BF),
            jax.ShapeDtypeStruct((rows, unit), F32),
            jax.ShapeDtypeStruct(heads.shape, BF),
            jax.ShapeDtypeStruct((nd, parts, 2 * piece + tail, unit), BF),
        ),
        in_specs=[VMEM, VMEM, VMEM, ANY, VMEM, VMEM],
        out_specs=(VMEM,) * 4,
        scratch_shapes=[
            weight, weight,
            pltpu.VMEM((parts, nd, tail, unit), BF),
            pltpu.VMEM((unit, unit), BF),
            square, half, half, half, square,
            pltpu.SemaphoreType.DMA((parts, 3)),
        ],
        compiler_params=pltpu.CompilerParams(vmem_limit_bytes=LIMIT),
    )(heads, tokens, cotangent, full, out_bias, down_bias)


def attend_back_kernel(
    live_ref, n1_ref, qx_ref, kx_ref, vx_ref, o_ref, hg_ref, pack_ref, wg_ref, dox, grads, dqt, dk_ref, mask_ref
):
    blocks, rows = hg_ref.shape[0], n1_ref.shape[0] // hg_ref.shape[0]
    live = live_ref[0]
    lane = lane_ids(rows)
    low = lane < HEAD

    def extend(i, carry):
        at = pl.ds(pl.multiple_of(i * rows, rows), rows)
        pair = hg_ref[i, :rows, :].astype(F32)
        third = unfold(hg_ref[i, rows:, :].astype(F32))
        for h, g in enumerate((pair, half_turn(pair), third)):
            g = jnp.where(low, g, 0.0)
            hi, mid, lo = split3(-jnp.sum(g * o_ref[h, at, :], axis=-1, keepdims=True))
            g = jnp.where(lane == HEAD, hi, jnp.where(lane == HEAD + 1, mid, jnp.where(lane == HEAD + 2, lo, g)))
            dox[h, at, :] = g.astype(BF)
        mask_ref[i] = diag_mask(i * rows, rows, live, True)
        return carry

    lax.fori_loop(0, blocks, extend, 0)

    def head(h, carry):
        for j in range(blocks):
            keys = kx_ref[h, j * rows : (j + 1) * rows, :]
            keys_t = jnp.transpose(keys.astype(F32)).astype(BF)
            vals = vx_ref[h, j * rows : (j + 1) * rows, :]
            dk = dv = None
            for i in range(j, blocks):
                q = qx_ref[h, i * rows : (i + 1) * rows, :]
                do = dox[h, i * rows : (i + 1) * rows, :]
                s = nt(keys, q)
                if i == j:
                    s = s + mask_ref[i]
                p = jnp.exp(s)
                ds = (p * nt(vals, do)).astype(BF)
                dv_part = nn(p.astype(BF), do)
                dk_part = nn(ds, q)
                dq_part = nn(keys_t, ds)
                dk = dk_part if dk is None else dk + dk_part
                dv = dv_part if dv is None else dv + dv_part
                if j == 0:
                    dqt[i] = dq_part
                else:
                    dqt[i] += dq_part
            dk_ref[j] = dk
            grads[3 + h, j * rows : (j + 1) * rows, :] = jnp.where(low, dv, 0.0)
        for i in range(blocks):
            dq = jnp.transpose(dqt[i]) * HEAD**-0.5
            grads[h, i * rows : (i + 1) * rows, :] = jnp.where(low, dq, half_turn(dk_ref[i]))
        return carry

    lax.fori_loop(0, 3, head, 0)

    def pack(i, carry):
        at = pl.ds(pl.multiple_of(i * rows, rows), rows)
        for h in range(3):
            pack_ref[i, h * rows : (h + 1) * rows, :] = grads[h, at, :].astype(BF)
        both = jnp.where(low, grads[3, at, :], half_turn(grads[4, at, :]))
        grads[3, at, :] = both
        pack_ref[i, 3 * rows : 4 * rows, :] = both.astype(BF)
        pack_ref[i, 4 * rows :, :] = fold(grads[5, at, :]).astype(BF)
        return carry

    lax.fori_loop(0, blocks, pack, 0)
    for k, m in enumerate((0, 1, 2, 3, 5)):
        wg_ref[k * LANES : (k + 1) * LANES, :] = tn(grads[m].astype(BF), n1_ref[...])


def attend_back(live, n1, qx, kx, vx, o, hg):
    blocks = hg.shape[0]
    total, unit = n1.shape
    rows = total // blocks
    return pl.pallas_call(
        attend_back_kernel,
        out_shape=(
            jax.ShapeDtypeStruct((blocks, 4 * rows + rows // 2, LANES), BF),
            jax.ShapeDtypeStruct((5 * LANES, unit), F32),
        ),
        in_specs=[SMEM] + [VMEM] * 6,
        out_specs=(VMEM, VMEM),
        scratch_shapes=[
            pltpu.VMEM((3, total, LANES), BF),
            pltpu.VMEM((6, total, LANES), F32),
            pltpu.VMEM((blocks, LANES, rows), F32),
            pltpu.VMEM((blocks, rows, LANES), F32),
            pltpu.VMEM((blocks, rows, rows), F32),
        ],
        compiler_params=pltpu.CompilerParams(vmem_limit_bytes=LIMIT),
    )(live, n1, qx, kx, vx, o, hg)


def final_kernel(width, tok_ref, hid_ref, pack_ref, full_ref, out_ref, wm, wide, dn_ref, xt, sem):
    parts, rows = pack_ref.shape[0], tok_ref.shape[0]
    nd, qrow, unit = wm.shape[1:]
    first = full_ref.shape[2] - qrow

    def fetch(t):
        return pltpu.make_async_copy(full_ref.at[:, t, pl.ds(first, qrow), :], wm.at[t], sem.at[t])

    for t in range(parts):
        fetch(t).start()
    widen(tok_ref, wide)
    dn_ref[...] = jnp.zeros_like(dn_ref)

    def part(t, carry):
        fetch(t).wait()
        for k in range(4):
            xt[:, k * LANES : (k + 1) * LANES] = pack_ref[t, k * rows : (k + 1) * rows, :]
        xt[:, 4 * LANES :] = unfold(pack_ref[t, 4 * rows :, :].astype(F32)).astype(BF)
        dn_ref[...] += nn(xt[...], wm[t].reshape(nd * qrow, unit))
        return carry

    lax.fori_loop(0, parts, part, 0)
    x = wide[...]
    s1, r = norm_stats(x, width + 1)
    grad = hid_ref[...] + norm_pull(x, s1, r, dn_ref[...], width + 1)
    out_ref[...] = grad[:, :width].astype(BF)


def final(tokens, hidgrad, pack, full):
    parts, nd = pack.shape[0], full.shape[0]
    rows, width = tokens.shape
    unit = full.shape[-1]
    return pl.pallas_call(
        partial(final_kernel, width),
        out_shape=jax.ShapeDtypeStruct((rows, width), BF),
        in_specs=[VMEM, VMEM, VMEM, ANY],
        out_specs=VMEM,
        scratch_shapes=[
            pltpu.VMEM((parts, nd, 640 // nd, unit), BF),
            pltpu.VMEM((rows, unit), F32),
            pltpu.VMEM((rows, unit), F32),
            pltpu.VMEM((rows, 5 * LANES), BF),
            pltpu.SemaphoreType.DMA((parts,)),
        ],
        compiler_params=pltpu.CompilerParams(vmem_limit_bytes=LIMIT),
    )(tokens, hidgrad, pack, full)


def swap(x):
    return lax.all_to_all(x, "tensor", 0, 0, tiled=True)


def pair_rows(w, axis):
    heads = [lax.slice_in_dim(w, k * HEAD, (k + 1) * HEAD, axis=axis) for k in range(9)]
    order = [heads[3 * (k % 2) + k // 2] for k in range(6)] + heads[6:] + [jnp.zeros_like(heads[0])]
    return jnp.concatenate(order, axis=axis)


def local(
    groups,
    tokens,
    cotangent,
    seq_length,
    live_rows,
    qkv_weight,
    qv_bias,
    out_weight,
    out_bias,
    up_weight,
    up_bias,
    down_weight,
    down_bias,
):
    parts = groups["tensor"]
    spread = groups["dp"] == 8
    nd = 8 if spread else 1
    rows, width = tokens.shape
    unit = width + 1
    piece = unit // nd
    as_row = lambda v: v.astype(F32)[None]

    w = jnp.transpose(qkv_weight, (1, 2, 0)).reshape(9 * HEAD, width)
    b = pair_rows(jnp.concatenate([qv_bias[0], jnp.zeros_like(qv_bias[0]), qv_bias[1]]).astype(F32), 0)[None]
    n1, qx, kx, vx, o, heads, full = enter(
        seq_length, live_rows, tokens, w, b, up_weight, down_weight, out_weight, as_row(up_bias), parts, spread
    )
    if not spread:
        wide = lambda v, tall=0: jnp.pad(v, ((0, tall), (0, unit - v.shape[1])))
        own = [jnp.concatenate([up_weight, up_bias[None]]), wide(down_weight), wide(out_weight, 64), wide(pair_rows(w, 0))]
        full = lax.all_gather(jnp.concatenate(own), "tensor", axis=0, tiled=False)[None]
    wide_row = lambda v: jnp.pad(as_row(v), ((0, 0), (0, 1)))
    mixed, hidgrad, hg, grads = middle(heads, tokens, cotangent, full, wide_row(out_bias), wide_row(down_bias))
    if spread:
        mine = lax.psum_scatter(grads, "dp", scatter_dimension=0, tiled=False)
        mine = lax.psum_scatter(mine, "tensor", scatter_dimension=0, tiled=False)
        mine = lax.all_gather(mine, "dp", axis=0, tiled=False)
    else:
        mine = lax.psum_scatter(grads[0].astype(F32), "tensor", scatter_dimension=0, tiled=False)
        mine = lax.psum(mine, "dp")[None]
    pack, wg = attend_back(live_rows, n1, qx, kx, vx, o, swap(hg))
    token_grad = final(tokens, hidgrad, swap(pack), full)
    wg = lax.psum(wg, "dp")
    up_grad = mine[:, :piece].reshape(unit, unit).astype(F32)
    down_grad = mine[:, piece : 2 * piece].reshape(unit, unit)[:, :width].astype(F32)
    rest = mine[:, 2 * piece :].reshape(256, unit).astype(F32)
    wg = jnp.concatenate(
        [wg[(2 * k if k < 3 else 2 * k - 5 if k < 6 else k) * HEAD :][:HEAD] for k in range(9)]
    )
    biases = wg[:, width].reshape(3, 3 * HEAD)
    return (
        mixed,
        token_grad,
        jnp.transpose(wg[:, :width].reshape(3, 3 * HEAD, width), (2, 0, 1)),
        jnp.stack([biases[0], biases[2]]),
        rest[: 3 * HEAD, :width],
        rest[3 * HEAD, :width],
        up_grad[:width],
        up_grad[width],
        down_grad,
        rest[3 * HEAD + 1, :width],
    )


def solution(mesh):
    placed = (
        P(BOTH, None),
        P(BOTH, None),
        P("dp"),
        P("dp"),
        P(None, None, "tensor"),
        P(None, "tensor"),
        P("tensor", None),
        P(),
        P(None, "tensor"),
        P("tensor"),
        P("tensor", None),
        P(),
    )
    return jax.shard_map(
        partial(local, dict(mesh.shape)),
        mesh=mesh,
        in_specs=placed,
        out_specs=(
            P(BOTH, None),
            P(BOTH, None),
            P(None, None, "tensor"),
            P(None, "tensor"),
            P("tensor", None),
            P(),
            P(None, "tensor"),
            P("tensor"),
            P("tensor", None),
            P(),
        ),
        check_vma=False,
    )
```

```python
from functools import partial

import jax
import jax.numpy as jnp
from jax import lax
from jax.experimental import pallas as pl
from jax.experimental.pallas import tpu as pltpu
from jax.sharding import PartitionSpec as P

HEAD = 64
LANES = 128
EPSILON = 1e-05
HIDE = -1e30
BF = jnp.bfloat16
F32 = jnp.float32
BOTH = ("dp", "tensor")
VMEM = pl.BlockSpec(memory_space=pltpu.VMEM)
SMEM = pl.BlockSpec(memory_space=pltpu.SMEM)
ANY = pl.BlockSpec(memory_space=pl.ANY)
LIMIT = 63 * 1024 * 1024
EARLY = 2


def nn(a, b):
    return lax.dot_general(a, b, (((1,), (0,)), ((), ())), preferred_element_type=F32)


def nt(a, b):
    return lax.dot_general(a, b, (((1,), (1,)), ((), ())), preferred_element_type=F32)


def tn(a, b):
    return lax.dot_general(a, b, (((0,), (0,)), ((), ())), preferred_element_type=F32)


def lane_ids(rows):
    return lax.broadcasted_iota(jnp.int32, (rows, LANES), 1)


def half_turn(x):
    return pltpu.roll(x, HEAD, 1)


def fold(x):
    half = x.shape[0] // 2
    return jnp.where(lane_ids(half) < HEAD, x[:half], half_turn(x[half:]))


def unfold(x):
    low = lane_ids(x.shape[0]) < HEAD
    zero = jnp.zeros_like(x)
    return jnp.concatenate(
        [jnp.where(low, x, zero), jnp.where(low, half_turn(x), zero)], axis=0
    )


def split3(x):
    high = x.astype(BF).astype(F32)
    rest = x - high
    mid = rest.astype(BF).astype(F32)
    return high, mid, rest - mid


def norm_stats(x, width):
    s1 = jnp.sum(x, axis=-1, keepdims=True)
    s2 = jnp.sum(x * x, axis=-1, keepdims=True)
    return s1, lax.rsqrt((s2 + s1 * s1) / width + EPSILON)


def norm_pull(x, s1, r, g, width):
    dot = jnp.sum(g * x, axis=-1, keepdims=True)
    return g * r - (r * r * r * dot / width) * (x + s1)


def widen(ref, scratch):
    rows, width = ref.shape
    wide = scratch.shape[1]
    scratch[:, wide - LANES :] = jnp.zeros((rows, LANES), F32)
    scratch[:, :width] = ref[...].astype(F32)


def diag_mask(first, rows, live, turned):
    q_dim, k_dim = (1, 0) if turned else (0, 1)
    q = lax.broadcasted_iota(jnp.int32, (rows, rows), q_dim)
    k = lax.broadcasted_iota(jnp.int32, (rows, rows), k_dim)
    seen = (k <= q) & ((k + first < live) | (k == q))
    return jnp.where(seen, 0.0, HIDE).astype(F32)


def at_rows(i, rows):
    return pl.ds(pl.multiple_of(i * rows, rows), rows)


def fill_rows(dst, src, first, rows, width):
    wide = dst.shape[1]
    dst[first : first + rows, wide - LANES :] = jnp.zeros((rows, LANES), dst.dtype)
    dst[first : first + rows, :width] = src


class Sends:
    def __init__(self):
        self.ends = []

    def start(self, copy, when=None):
        if when is None:
            copy().start()
        else:
            pl.when(when())(lambda: copy().start())
        self.ends.append((copy, when))

    def finish(self):
        for copy, when in self.ends:
            if when is None:
                copy().wait_send()
            else:
                pl.when(when())(lambda copy=copy: copy().wait_send())


def remote(src, dst, ssem, rsem, **where):
    return pltpu.make_async_remote_copy(
        src_ref=src,
        dst_ref=dst,
        send_sem=ssem,
        recv_sem=rsem,
        device_id=where,
        device_id_type=pl.DeviceIdType.MESH,
    )


def neighbours(d):
    core, x, y = d % 2, (d // 2) % 2, d // 4
    return d + 1 - 2 * core, d + 2 - 4 * x, d + 4 - 8 * y


def greet(d, t, parts, spread, corner=False):
    barrier = pltpu.get_barrier_semaphore()

    def signal(**where):
        pl.semaphore_signal(barrier, inc=1, device_id=where, device_id_type=pl.DeviceIdType.MESH)

    for k in range(1, parts):
        signal(tensor=lax.rem(t + k, parts))
    if spread:
        core_n, x_n, y_n = neighbours(d)
        for n in (core_n, x_n, y_n) + ((x_n + y_n - d,) if corner else ()):
            signal(dp=n)
    return lambda: pl.semaphore_wait(barrier, parts - 1 + (3 + corner) * spread)


class Spread:
    def __init__(self, d, t, parts, piece, full, zsem, xsem, csem, sends, times):
        self.d, self.t, self.parts, self.piece, self.full, self.times = d, t, parts, piece, full, times
        self.zsem, self.xsem, self.csem, self.sends = zsem, xsem, csem, sends
        self.core_n, self.x_n, self.y_n = neighbours(d)
        self.diag = self.x_n + self.y_n - d

    def slot(self, e, b):
        return self.full.at[e, b]

    def out(self, to, ok):
        self.sends.start(
            lambda: remote(self.piece, self.slot(self.d, self.t), self.zsem.at[0, to], self.zsem.at[1, self.t], tensor=to), ok
        )

    def plane(self, b, first, ok):
        d, xs = self.d, self.xsem
        src = lambda: self.piece if first else self.slot(d, b)
        self.sends.start(lambda: remote(src(), self.slot(d, b), xs.at[0, b], xs.at[1, b], dp=self.x_n), ok)
        self.sends.start(lambda: remote(src(), self.slot(d, b), xs.at[2, b], xs.at[3, b], dp=self.y_n), ok)
        self.sends.start(
            lambda: remote(src(), self.slot(d, b), self.csem.at[0, b], self.csem.at[4, b], dp=self.core_n), ok
        )

    def arrive(self, b, ok):
        def wait():
            remote(self.slot(self.d, b), self.slot(self.d, b), self.zsem.at[0, b], self.zsem.at[1, b], tensor=b).wait_recv()

        pl.when(ok())(wait)
        self.plane(b, False, ok)

    def across(self, b, ok):
        xs, cs = self.xsem, self.csem
        east = lambda: self.slot(self.x_n, b)
        north = lambda: self.slot(self.y_n, b)

        def wait():
            remote(east(), east(), xs.at[0, b], xs.at[1, b], dp=self.x_n).wait_recv()
            remote(north(), north(), xs.at[2, b], xs.at[3, b], dp=self.y_n).wait_recv()

        pl.when(ok())(wait)
        self.sends.start(
            lambda: remote(east(), east(), xs.at[4, b], xs.at[5, b], dp=self.y_n), lambda: ok() & (b % 2 == 0)
        )
        self.sends.start(
            lambda: remote(north(), north(), xs.at[4, b], xs.at[5, b], dp=self.x_n), lambda: ok() & (b % 2 == 1)
        )
        self.sends.start(lambda: remote(east(), east(), cs.at[1, b], cs.at[5, b], dp=self.core_n), ok)
        self.sends.start(lambda: remote(north(), north(), cs.at[2, b], cs.at[6, b], dp=self.core_n), ok)

    def corner(self, b, ok):
        far, xs, cs = (lambda: self.slot(self.diag, b)), self.xsem, self.csem
        pl.when(ok())(lambda: remote(far(), far(), xs.at[4, b], xs.at[5, b], dp=self.x_n).wait_recv())
        self.sends.start(lambda: remote(far(), far(), cs.at[3, b], cs.at[7, b], dp=self.core_n), ok)

    def at(self, point):
        own = lambda: self.t >= 0
        for job in ("out", "plane", "arrive", "across", "corner"):
            for (k, m), when in self.times[job].items():
                if when != point:
                    continue
                if k == m:
                    self.plane(self.t, True, own) if job == "plane" else getattr(self, job)(self.t, own)
                    continue
                for mirror in (False, True):
                    here, there = (self.parts - 1 - k, self.parts - 1 - m) if mirror else (k, m)
                    getattr(self, job)(there, lambda here=here: self.t == here)

    def ready(self, b):
        shift = self.core_n - self.d
        for k, e in enumerate((self.d, self.x_n, self.y_n, self.diag)):
            there = self.slot(e + shift, b)
            remote(there, there, self.csem.at[k, b], self.csem.at[4 + k, b], dp=self.core_n).wait_recv()


PAIRS = [(k, m) for k in range(4) for m in range(k)]
REST_TIMES = {
    "out": {(m, k): "p1" for k, m in PAIRS},
    "plane": {(0, 0): "p0"},
    "arrive": {pair: "p3" for pair in PAIRS},
    "across": {(0, 0): "p1", **{pair: "h0" for pair in PAIRS}},
    "corner": {(0, 0): "p2", **{pair: "h1" for pair in PAIRS}},
}
MAIN_TIMES = {
    "out": {(2, 3): "p0", (0, 1): "p1", (1, 2): "p2", (0, 2): "p2", (1, 3): "h2", (0, 3): "p3"},
    "plane": {(0, 0): "p0"},
    "arrive": {(3, 2): "p1", (1, 0): "p2", (2, 1): "h1", (2, 0): "h1", (3, 1): "h1", (3, 0): "h2"},
    "across": {(0, 0): "p1", (3, 2): "p3", (1, 0): "h0", (2, 0): "h2", (2, 1): "e", (3, 1): "e", (3, 0): "q0"},
    "corner": {(0, 0): "p2", (3, 2): "h0", (1, 0): "h1", (2, 0): "e", (3, 1): "q0", (2, 1): "q1", (3, 0): "q1"},
}
LATE_TIMES = {
    "out": {(m, k): "q0" for k, m in PAIRS},
    "plane": {(0, 0): "q0"},
    "arrive": {pair: "q2" for pair in PAIRS},
    "across": {(0, 0): "q2", **{pair: "q4" for pair in PAIRS}},
    "corner": {(0, 0): "q3", **{pair: "g" for pair in PAIRS}},
}


SERVE = {(0, 0): (2, 3), (1, 1): (3, 4), (2, 0): (4, None)}


def owner_order(d):
    return 4 * (d % 2) + d // 2


def layer_kernel(
    spread, seq_ref, live_ref, tok_ref, cot_any, w_any, b_ref, up_any, down_any, ow_any, ub_ref, ob_ref, db_ref, rest_in, main_in, late_in,
    mixed_ref, out_ref, o_any, fin_any, rest_out, main_out, late_out, r1_any,
    n1_ref, wq, piece, qx_ref, kx_ref, vx_ref, pack_ref, heads_in, hg_in, recv_ref, hid_ref, gbuf, r2, r3, fst, w1, w2,
    nsem, hsem, gsem, qsem, own_sem, lsem, wsem, s1, s2, s3, s4, s5, u1, u2, *gsems,
):
    rows, width = tok_ref.shape
    unit = n1_ref.shape[1]
    blocks = parts = heads_in.shape[0]
    nd = 8 if spread else 1
    share, tail, qrow = unit // nd, 256 // nd, 640 // nd
    d, t = lax.axis_index("dp"), lax.axis_index("tensor")
    core = d % 2
    barrier = greet(d, t, parts, spread, True)
    sends, heads_sends = Sends(), Sends()
    seq, live = seq_ref[0], live_ref[0]
    lane = lane_ids(rows)
    low = lane < HEAD
    row = lax.broadcasted_iota(jnp.int32, (rows, LANES), 0)
    spare = lax.broadcasted_iota(jnp.int32, (rows, unit), 1) == width
    rest_full, main_full, late_full = (rest_out, main_out, late_out) if spread else (rest_in, main_in, late_in)
    gathers = []
    if spread:
        main_piece, rest_piece = piece.at[pl.ds(0, 2 * share)], piece.at[pl.ds(2 * share, tail)]
        late_piece = piece.at[pl.ds(2 * share + tail, qrow)]
        for k, (own, full, times) in enumerate(
            ((rest_piece, rest_out, REST_TIMES), (main_piece, main_out, MAIN_TIMES), (late_piece, late_out, LATE_TIMES))
        ):
            gathers.append(Spread(d, t, parts, own, full, *gsems[3 * k : 3 * k + 3], sends, times))

    def point(name):
        for gather in gathers:
            gather.at(name)

    def when_point(cond, name):
        if spread:
            pl.when(cond)(lambda: point(name))

    def turn(k):
        a, b = (t + k - 2 * (t % 2) * (k % 2)) % 2, t // 2 + k // 2 - 2 * (t // 2) * (k // 2)
        return a + 2 * b

    def prologue(wide, w_sc, up_sc, down_sc, ow_sc):
        loads = [
            pltpu.make_async_copy(src, dst, lsem.at[k])
            for k, (src, dst) in enumerate(((w_any, w_sc), (up_any, up_sc), (down_any, down_sc), (ow_any, ow_sc)))
        ]
        for load in loads if spread else loads[:1]:
            load.start()
        widen(tok_ref, wide)
        x = wide[...]
        _, r = norm_stats(x, width + 1)
        n1_ref[at_rows(t, rows), :] = jnp.where(spare, 1.0, x * r).astype(BF)
        barrier()
        for up in (True, False):
            sends.start(lambda up=up: line(t, up), lambda up=up: edge(up))
        loads[0].wait()
        for k in range(9):
            take = 3 * (k % 2) + k // 2 if k < 6 else k
            fill_rows(wq, w_sc[take * HEAD : (take + 1) * HEAD, :], k * HEAD, HEAD, width)
        wq[9 * HEAD : 10 * HEAD, :] = jnp.zeros((HEAD, unit), BF)
        if not spread:
            return
        near = share - 16
        piece[:, unit - LANES :] = jnp.zeros((piece.shape[0], LANES), BF)
        for load in loads[1:]:
            load.wait()
        piece[:near, :] = up_sc[pl.ds(pl.multiple_of(d * share, 16), near), :]

        @pl.when(d < nd - 1)
        def _():
            piece[near:share, :] = up_sc[pl.ds(pl.multiple_of(d * share + near, 16), 16), :]

        @pl.when(d == nd - 1)
        def _():
            last = jnp.concatenate([up_sc[width - 15 :, :].astype(F32), ub_ref[...]], axis=0)
            piece[near:share, :] = last.astype(BF)

        piece[share : 2 * share, :width] = down_sc[pl.ds(pl.multiple_of(d * share, 16), share), :]

        @pl.when(d < 6)
        def _():
            piece[2 * share : 2 * share + tail, :width] = ow_sc[pl.ds(pl.multiple_of(d * tail, 16), tail), :]

        @pl.when(d >= 6)
        def _():
            piece[2 * share : 2 * share + tail, :] = jnp.zeros((tail, unit), BF)

        piece[2 * share + tail :, :] = wq[pl.ds(pl.multiple_of(d * qrow, 16), qrow), :]

    def line(b, up):
        block = n1_ref.at[at_rows(b, rows), :]
        return remote(block, block, nsem.at[1 if up else 2, b], nsem.at[0, b], tensor=t + 1 if up else t - 1)

    def edge(up):
        return t < parts - 1 if up else t > 0

    def place(s, up):
        b = t - s if up else t + s
        return b, (lambda: t - s >= 0) if up else (lambda: t + s < parts)

    places = {(s, up): place(s, up) for s in range(1, parts) for up in (True, False)}
    pl.run_scoped(
        prologue,
        pltpu.VMEM((rows, unit), F32),
        pltpu.VMEM(w_any.shape, BF),
        pltpu.VMEM(up_any.shape, BF),
        pltpu.VMEM(down_any.shape, BF),
        pltpu.VMEM(ow_any.shape, BF),
    )
    homes = []
    if spread:
        for k, gather in enumerate(gathers):
            homes.append(pltpu.make_async_copy(gather.piece, gather.slot(d, t), own_sem.at[k]))
            homes[-1].start()
        point("p0")

    def attend(o_ref, mask_ref, s_ref):
        def project(i):
            at = at_rows(i, rows)
            qkv = nt(n1_ref[at, :], wq[: 10 * HEAD, :]) + b_ref[...]
            qkv = qkv.astype(BF).astype(F32)
            key = row + i * rows
            m = lane - HEAD
            same = ((m * rows) ^ (i * rows)) < seq
            open_ = (m == i) | (same & (key < live))
            bias = jnp.where(m < blocks, jnp.where(open_, 0.0, HIDE), jnp.where(m < blocks + 3, 1.0, 0.0))
            hot = jnp.where(m == i, 1.0, 0.0)
            ones = jnp.where(m < 3, 1.0, 0.0)
            for h in range(3):
                pair = qkv[:, h * LANES : (h + 1) * LANES]
                qx_ref[h, at, :] = jnp.where(low, pair * HEAD**-0.5, hot).astype(BF)
                kx_ref[h, at, :] = jnp.where(low, half_turn(pair), bias).astype(BF)
                val = qkv[:, (3 + h // 2) * LANES : (4 + h // 2) * LANES]
                vx_ref[h, at, :] = jnp.where(low, half_turn(val) if h % 2 else val, ones).astype(BF)
            mask_ref[i] = diag_mask(i * rows, rows, live, False).astype(BF)

        for s in range(parts):
            if s:
                for up in (True, False):
                    b, ok = places[s, up]
                    pl.when(ok())(lambda b=b, up=up: line(b, up).wait_recv())
                    sends.start(lambda b=b, up=up: line(b, up), lambda ok=ok, up=up: ok() & edge(up))
                point(f"p{s}")

            def arrived(e, carry, s=s):
                b = t + (2 * e - 1) * s
                pl.when((b >= 0) & (b < parts))(lambda: project(b))
                return carry

            lax.fori_loop(0, 2 if s else 1, arrived, 0)

        def head(h, carry):
            for i in range(blocks):
                q = qx_ref[h, i * rows : (i + 1) * rows, :]
                top = None
                for j in range(i, -1, -1):
                    s = nt(q, kx_ref[h, j * rows : (j + 1) * rows, :])
                    if i == j:
                        s = s + mask_ref[i].astype(F32)
                    peak = jnp.max(s, axis=-1, keepdims=True)
                    top = peak if top is None else jnp.maximum(top, peak)
                    s_ref[j] = s
                acc = None
                for j in range(i + 1):
                    p = jnp.exp(s_ref[j] - top).astype(BF)
                    part = nn(p, vx_ref[h, j * rows : (j + 1) * rows, :])
                    acc = part if acc is None else acc + part
                mass = acc[:, HEAD : HEAD + 1]
                lse = top + jnp.log(mass)
                o_ref[h, i * rows : (i + 1) * rows, :] = acc / mass
                hi, mid, lo = split3(-lse)
                ext = jnp.where(
                    lane == HEAD + blocks,
                    hi,
                    jnp.where(lane == HEAD + blocks + 1, mid, jnp.where(lane == HEAD + blocks + 2, lo, q.astype(F32))),
                )
                qx_ref[h, i * rows : (i + 1) * rows, :] = ext.astype(BF)
            for k in range(3):
                when_point(h == k, f"h{k}")
            return carry

        lax.fori_loop(0, 3, head, 0)
        keep = pltpu.make_async_copy(o_ref, o_any, lsem.at[0])
        keep.start()

        def pack(i, carry):
            at = at_rows(i, rows)
            pack_ref[i, :rows, :] = jnp.where(low, o_ref[0, at, :], half_turn(o_ref[1, at, :])).astype(BF)
            pack_ref[i, rows:, :] = fold(o_ref[2, at, :]).astype(BF)
            return carry

        lax.fori_loop(0, blocks, pack, 0)
        swap_start(pack_ref, heads_in, hsem, heads_sends)
        point("e")
        keep.wait()

    def swap(src_ref, dst_ref, sems, k, taking):
        to = lax.rem(t + (parts - k if taking else k), parts)
        src, dst = (to, to) if taking else (to, t)
        return remote(src_ref.at[src], dst_ref.at[dst], sems.at[0, k], sems.at[1, k], tensor=to)

    def swap_home(src_ref, dst_ref, sems):
        return pltpu.make_async_copy(src_ref.at[t], dst_ref.at[t], sems.at[0, 0])

    def swap_start(src_ref, dst_ref, sems, sends):
        for k in (2, 1, 3):
            sends.start(lambda k=k: swap(src_ref, dst_ref, sems, k, False))
        swap_home(src_ref, dst_ref, sems).start()

    def swap_end(src_ref, dst_ref, sems):
        for k in range(1, parts):
            swap(src_ref, dst_ref, sems, k, True).wait_recv()
        swap_home(src_ref, dst_ref, sems).wait()

    pl.run_scoped(
        attend,
        pltpu.VMEM((3, rows * parts, LANES), F32),
        pltpu.VMEM((parts, rows, rows), BF),
        pltpu.VMEM((parts, rows, rows), F32),
    )

    core_n, x_n, y_n = neighbours(d)
    chips = (x_n, y_n, x_n + y_n - d)
    main_rows, rest_rows = pl.ds(0, 2 * share), pl.ds(2 * share, tail)
    half = gbuf.at[core] if spread else gbuf
    every = pl.ds(0, parts)

    def region(k):
        if isinstance(k, int) and k == parts:
            return every, rest_rows
        return turn(k), main_rows

    def to_core(k):
        which, at = region(k)
        return remote(gbuf.at[1 - core, :, which, at], r1_any.at[:, which, at], s1.at[0, k], s1.at[1, k], dp=core_n)

    def second(c, k):
        which, at = region(k)
        return remote(
            gbuf.at[core, chips[c] // 2, which, at], r2.at[c, which, at], s2.at[0, c, k], s2.at[1, c, k], dp=chips[c]
        )

    def add_core(k, stage, stage_rest):
        to_core(k).wait_recv()
        which, at = region(k)
        here = stage_rest if isinstance(k, int) and k == parts else stage
        load = pltpu.make_async_copy(r1_any.at[:, which, at], here, lsem.at[0])
        load.start()
        load.wait()
        for q in range(4):
            gbuf[core, q, which, at] = (gbuf[core, q, which, at].astype(F32) + here[q].astype(F32)).astype(BF)

    def third(k, m):
        b, at = turn(k), (main_rows, rest_rows)[m]
        return remote(gbuf.at[core, d // 2, b, at], r3.at[t, at], s3.at[0, m, b], s3.at[1, m, t], tensor=b)

    def send_second(k):
        for c in range(3):
            sends.start(lambda c=c: second(c, k))

    def sum_second(k):
        for c in range(3):
            second(c, k).wait_recv()
        which, at = region(k)
        total = gbuf[core, d // 2, which, at].astype(F32)
        for c in range(3):
            total = total + r2[c, which, at].astype(F32)
        gbuf[core, d // 2, which, at] = total.astype(BF)
        if k == parts:
            for j in range(1, parts):
                sends.start(lambda j=j: third(j, 1))
        elif k:
            sends.start(lambda: third(k, 0))

    def middle(wu, wd, wm, acts, ugs, xall, n2_ref, gb_ref, wide, dn_ref, stage):
        stage_rest = wm.at[pl.ds(0, 4)] if spread else None
        wo = wq

        def fetch(k, slot):
            return [
                pltpu.make_async_copy(main_full.at[:, turn(k), pl.ds(m * share, share), :], dst.at[slot], wsem.at[m, slot])
                for m, dst in enumerate((wu, wd))
            ]

        def fetch_start(k, slot):
            if spread:
                gathers[1].ready(turn(k))
            for copy in fetch(k, slot):
                copy.start()

        cot_load = pltpu.make_async_copy(cot_any, mixed_ref, lsem.at[1])
        cot_load.start()
        if spread:
            for home in homes[:2]:
                home.wait()
            for b in range(parts):
                gathers[0].ready(b)
        rest_load = pltpu.make_async_copy(rest_full, wm, lsem.at[0])
        rest_load.start()
        fetch_start(0, 0)
        cot_load.wait()
        widen(mixed_ref, wide)
        gb_ref[...] = wide[...].astype(BF)
        widen(tok_ref, wide)
        rest_load.wait()
        for b in range(parts):
            own = wm[:, b].reshape(tail * nd, unit)
            wo[b * LANES : (b + 1) * LANES, :] = own[:LANES]
            wo[parts * LANES + b * HEAD : parts * LANES + (b + 1) * HEAD, :] = own[LANES : LANES + HEAD]
        swap_end(pack_ref, heads_in, hsem)
        lows = []
        for b in range(parts):
            xall[:, b * LANES : (b + 1) * LANES] = heads_in[b, :rows, :]
            lows.append(unfold(heads_in[b, rows:, :].astype(F32)))
        for k in range(parts // 2):
            both = jnp.where(low, lows[2 * k], half_turn(lows[2 * k + 1]))
            xall[:, (parts + k) * LANES : (parts + k + 1) * LANES] = both.astype(BF)
        point("q0")
        hidden = wide[...] + nn(xall[...], wo[...]) + ob_ref[...]
        s1_, r = norm_stats(hidden, width + 1)
        n2_ref[...] = jnp.where(spare, 1.0, hidden * r).astype(BF)
        hid_ref[...] = hidden
        wide[...] = hidden + db_ref[...]
        dn_ref[...] = jnp.zeros_like(dn_ref)
        root = (2 / jnp.pi) ** 0.5

        def store_grads(k, act, ug):
            b = turn(k)
            up_g = tn(n2_ref[...], ug).astype(BF)
            down_g = tn(act, gb_ref[...]).astype(BF)
            if spread:
                gbuf[:, :, b, :share, :] = up_g.reshape(2, 4, share, unit)
                gbuf[:, :, b, share : 2 * share, :] = down_g.reshape(2, 4, share, unit)
                to_core(k).start()
            else:
                gbuf[0, b, :share, :] = up_g
                gbuf[0, b, share : 2 * share, :] = down_g

        def unit_block(k, carry):
            slot = k % 2
            for copy in fetch(k, slot):
                copy.wait()
            up = wu[slot].reshape(unit, unit)
            down = wd[slot].reshape(unit, unit)

            def some_rows(i, carry):
                at = at_rows(i, rows // 2)
                u = nn(n2_ref[at, :], up)
                th = jnp.tanh(root * (u + 0.044715 * (u * u * u)))
                act = (0.5 * u * (1 + th)).astype(BF)
                slope = 0.5 * (1 + th) + (0.5 * u) * (1 - th * th) * (root * (1 + 0.134145 * (u * u)))
                acts[slot, at, :] = act
                wide[at, :] += nn(act, down)
                ug = (nt(gb_ref[at, :], down) * slope).astype(BF)
                ugs[slot, at, :] = ug
                dn_ref[at, :] += nt(ug, up)
                return carry

            lax.fori_loop(0, 2, some_rows, 0)
            pl.when(k < parts - 1)(lambda: fetch_start(k + 1, (k + 1) % 2))
            pl.when(k < EARLY)(lambda: store_grads(k, acts[slot], ugs[slot]))

            if spread:
                for m in range(1, EARLY + 1):
                    pl.when(k == m)(lambda m=m: add_core(m - 1, stage, stage_rest))
                pl.when(k == 1)(lambda: send_second(0))
                pl.when(k == 3)(lambda: send_second(1))
            for m in range(parts):
                when_point(k == m, f"q{m + 1}")
            return carry

        lax.fori_loop(0, parts, unit_block, 0)
        hidden = hid_ref[...]
        gout = gb_ref[...].astype(F32)
        hidgrad = gout + norm_pull(hidden, s1_, r, dn_ref[...], width + 1)
        ag = hidgrad.astype(BF)
        hg = nt(ag, wo[...])
        heads_sends.finish()
        for b in range(parts):
            pack_ref[b, :rows, :] = hg[:, b * LANES : (b + 1) * LANES].astype(BF)
            pair = hg[:, (parts + b // 2) * LANES : (parts + b // 2 + 1) * LANES]
            pack_ref[b, rows:, :] = fold(half_turn(pair) if b % 2 else pair).astype(BF)
        swap_start(pack_ref, hg_in, gsem, sends)
        point("g")
        mixed_ref[...] = wide[:, :width].astype(BF)
        hid_ref[...] = hidgrad
        out_bias_grad = jnp.sum(hidgrad, axis=0, keepdims=True)
        down_bias_grad = jnp.sum(gout, axis=0, keepdims=True)
        wide[...] = tn(xall[:, : parts * LANES], ag)
        dn_ref[: parts * HEAD, :] = tn(xall[:, parts * LANES :], ag)
        extra = lax.broadcasted_iota(jnp.int32, (HEAD, unit), 0)
        extra = jnp.where(extra == 0, out_bias_grad, jnp.where(extra == 1, down_bias_grad, 0.0))
        for b in range(parts):
            pair = wide[b * LANES : (b + 1) * LANES, :]
            low_part = dn_ref[b * HEAD : (b + 1) * HEAD, :]
            misc = jnp.concatenate([pair, low_part, extra], axis=0).astype(BF)
            if spread:
                gbuf[:, :, b, 2 * share :, :] = misc.reshape(2, 4, tail, unit)
            else:
                gbuf[0, b, 2 * share :, :] = misc
        if spread:
            to_core(parts).start()

        def late(k, carry):
            store_grads(k, acts[k % 2], ugs[k % 2])
            return carry

        lax.fori_loop(EARLY, parts, late, 0)
        if spread:
            for k in [parts] + list(range(EARLY, parts)):
                add_core(k, stage, stage_rest)
            for k in range(EARLY):
                sum_second(k)
            send_second(2)
        else:
            out = pltpu.make_async_copy(gbuf, fin_any, lsem.at[0])
            out.start()
            out.wait()

    square, low_square = pltpu.VMEM((rows, unit), F32), pltpu.VMEM((rows, unit), BF)
    pl.run_scoped(
        middle,
        pltpu.VMEM((2, nd, share, unit), BF),
        pltpu.VMEM((2, nd, share, unit), BF),
        pltpu.VMEM((nd, parts, tail, unit), BF),
        pltpu.VMEM((parts - EARLY, rows, unit), BF),
        pltpu.VMEM((parts - EARLY, rows, unit), BF),
        low_square,
        low_square,
        low_square,
        square,
        square,
        pltpu.VMEM((4, 2 * share, unit) if spread else (16, LANES), BF),
    )

    def back(gpack, wgb, dox, dvs, dqt, dk_ref, mask_ref, xt, wg_acc, wmq, dn_ref):
        local = Sends()
        wide = wg_acc.at[pl.ds(0, rows)]

        def o_load(i):
            return pltpu.make_async_copy(o_any.at[:, pl.ds(i * rows, rows), :], dk_ref.at[pl.ds(0, 3)], lsem.at[0])

        def w_load(k):
            return pltpu.make_async_copy(late_full.at[:, k], wmq.at[k], wsem.at[0, k])

        def swap_grads(k, p, taking):
            to = lax.rem(t + (parts - k if taking else k), parts)
            src, dst = (to, to) if taking else (to, t)
            at = pl.ds(p * rows, rows if p < 4 else rows // 2)
            return remote(gpack.at[src].at[at], recv_ref.at[dst].at[at], qsem.at[0, k, p], qsem.at[1, k, p], tensor=to)

        def send_grads(p):
            for k in (2, 1, 3):
                local.start(lambda k=k: swap_grads(k, p, False))

        o_load(0).start()

        def masks(i, carry):
            mask_ref[i] = diag_mask(i * rows, rows, live, True).astype(BF)
            return carry

        lax.fori_loop(0, blocks, masks, 0)
        swap_end(pack_ref, hg_in, gsem)
        for i in range(blocks):
            o_load(i).wait()
            pair = hg_in[i, :rows, :].astype(F32)
            last = unfold(hg_in[i, rows:, :].astype(F32))
            for h, g in enumerate((pair, half_turn(pair), last)):
                g = jnp.where(low, g, 0.0)
                hi, mid, lo = split3(-jnp.sum(g * dk_ref[h], axis=-1, keepdims=True))
                g = jnp.where(lane == HEAD, hi, jnp.where(lane == HEAD + 1, mid, jnp.where(lane == HEAD + 2, lo, g)))
                dox[h, i * rows : (i + 1) * rows, :] = g.astype(BF)
            if i + 1 < blocks:
                o_load(i + 1).start()
        if spread:
            homes[2].wait()
            for k in range(parts):
                gathers[2].ready(k)
        for k in range(parts):
            w_load(k).start()

        def head(h, carry):
            spot = lax.rem(h, 2)
            for j in range(blocks):
                keys = kx_ref[h, j * rows : (j + 1) * rows, :]
                keys_t = jnp.transpose(keys.astype(F32)).astype(BF)
                vals = vx_ref[h, j * rows : (j + 1) * rows, :]
                dk = dv = None
                for i in range(j, blocks):
                    q = qx_ref[h, i * rows : (i + 1) * rows, :]
                    do = dox[h, i * rows : (i + 1) * rows, :]
                    s = nt(keys, q)
                    if i == j:
                        s = s + mask_ref[i].astype(F32)
                    p = jnp.exp(s)
                    ds = (p * nt(vals, do)).astype(BF)
                    dv_part = nn(p.astype(BF), do)
                    dk_part = nn(ds, q)
                    dq_part = nn(keys_t, ds)
                    dk = dk_part if dk is None else dk + dk_part
                    dv = dv_part if dv is None else dv + dv_part
                    if j == 0:
                        dqt[i] = dq_part
                    else:
                        dqt[i] += dq_part
                dk_ref[j] = dk
                dvs[spot, j * rows : (j + 1) * rows, :] = dv.astype(BF)
                if spread:
                    for step, (done, next_) in SERVE.items():
                        if step[1] == j:

                            @pl.when(h == step[0])
                            def _(done=done, next_=next_):
                                sum_second(done)
                                if next_ is not None:
                                    send_second(next_)

            at = pl.ds(pl.multiple_of(h * rows, rows), rows)
            for i in range(blocks):
                dq = jnp.transpose(dqt[i]) * HEAD**-0.5
                gpack[i, at, :] = jnp.where(low, dq, half_turn(dk_ref[i])).astype(BF)
            for p in range(3):
                pl.when(h == p)(lambda p=p: send_grads(p))

            @pl.when(h == 1)
            def _():
                for i in range(blocks):
                    mine = pl.ds(i * rows, rows)
                    gpack[i, 3 * rows : 4 * rows, :] = jnp.where(low, dvs[0, mine, :].astype(F32), half_turn(dvs[1, mine, :].astype(F32))).astype(BF)
                send_grads(3)

            @pl.when(h == 2)
            def _():
                for i in range(blocks):
                    gpack[i, 4 * rows :, :] = fold(dvs[0, i * rows : (i + 1) * rows, :].astype(F32)).astype(BF)
                send_grads(4)

            return carry

        lax.fori_loop(0, 3, head, 0)
        home = pltpu.make_async_copy(gpack.at[t], recv_ref.at[t], qsem.at[0, 0, 0])
        home.start()

        def spread_lanes(ref, i):
            for k in range(4):
                xt[:, k * LANES : (k + 1) * LANES] = ref[i, k * rows : (k + 1) * rows, :]
            xt[:, 4 * LANES :] = unfold(ref[i, 4 * rows :, :].astype(F32)).astype(BF)

        wg_acc[...] = jnp.zeros_like(wg_acc)

        def weigh(i, carry):
            spread_lanes(gpack, i)
            wg_acc[...] += tn(xt[...], n1_ref[at_rows(i, rows), :])
            return carry

        lax.fori_loop(0, blocks, weigh, 0)
        tall = 2 * share + tail
        if spread:
            wgb[...] = wg_acc[...].astype(BF).reshape(2, 4, qrow, unit)

            def w_first():
                return remote(wgb.at[1 - core], w1, u1.at[0], u1.at[1], dp=core_n)

            def w_second(c):
                return remote(wgb.at[core, chips[c] // 2], w2.at[c], u2.at[0, c], u2.at[1, c], dp=chips[c])

            local.start(w_first)
            w_first().wait_recv()
            for q in range(4):
                wgb[core, q] = (wgb[core, q].astype(F32) + w1[q].astype(F32)).astype(BF)
            for c in range(3):
                local.start(lambda c=c: w_second(c))
            total = wgb[core, d // 2].astype(F32)
            for c in range(3):
                w_second(c).wait_recv()
                total = total + w2[c].astype(F32)
            fst[tall:, :] = total.astype(BF)
            total = gbuf[core, d // 2, t].astype(F32)
            for k in range(1, parts):
                b = turn(k)
                for m, at in enumerate((main_rows, rest_rows)):
                    there = r3.at[b, at]
                    remote(there, there, s3.at[0, m, b], s3.at[1, m, b], tensor=b).wait_recv()
                total = total + r3[b].astype(F32)
            fst[:tall, :] = total.astype(BF)

            def give(c):
                return remote(fst, fin_any.at[owner_order(d)], s4.at[0, c], s4.at[1, c], dp=chips[c])

            def came(c):
                there = fin_any.at[owner_order(chips[c])]
                return remote(there, there, s4.at[0, c], s4.at[1, c], dp=chips[c])

            def give_core(c):
                if c == 3:
                    return remote(fst, fin_any.at[owner_order(d)], s5.at[0, c], s5.at[1, c], dp=core_n)
                there = fin_any.at[owner_order(chips[c])]
                return remote(there, there, s5.at[0, c], s5.at[1, c], dp=core_n)

            own = pltpu.make_async_copy(fst, fin_any.at[owner_order(d)], own_sem.at[3])
            own.start()
            for c in (2, 0, 1):
                sends.start(lambda c=c: give(c))
            sends.start(lambda: give_core(3))
        else:
            out = pltpu.make_async_copy(wg_acc, r1_any, own_sem.at[3])
            out.start()
            out.wait()
        widen(tok_ref, wide)
        dn_ref[...] = jnp.zeros_like(dn_ref)
        home.wait()
        for k in range(1, parts):
            for p in range(5):
                swap_grads(k, p, True).wait_recv()
        for k in range(parts):
            w_load(k).wait()

        def part(b, carry):
            spread_lanes(recv_ref, b)
            dn_ref[...] += nn(xt[...], wmq[b].reshape(nd * qrow, unit))
            return carry

        lax.fori_loop(0, parts, part, 0)
        x = wide[...]
        s1_, r = norm_stats(x, width + 1)
        grad = hid_ref[...] + norm_pull(x, s1_, r, dn_ref[...], width + 1)
        out_ref[...] = grad[:, :width].astype(BF)
        if spread:
            for c in range(3):
                came(c).wait_recv()
                sends.start(lambda c=c: give_core(c))
            for c in range(4):
                give_core(c).wait_recv()
            own.wait()
        local.finish()

    pack = (parts, 4 * rows + rows // 2, LANES)
    pl.run_scoped(
        back,
        pltpu.VMEM(pack, BF),
        pltpu.VMEM((2, 4, qrow, unit) if spread else (16, LANES), BF),
        pltpu.VMEM((3, rows * parts, LANES), BF),
        pltpu.VMEM((2, rows * parts, LANES), BF),
        pltpu.VMEM((parts, LANES, rows), F32),
        pltpu.VMEM((parts, rows, LANES), F32),
        pltpu.VMEM((parts, rows, rows), BF),
        pltpu.VMEM((rows, 5 * LANES), BF),
        pltpu.VMEM((5 * LANES, unit), F32),
        pltpu.VMEM((parts, nd, qrow, unit), BF),
        square,
    )
    if spread:
        for k in range(parts + 1):
            to_core(k).wait_send()
    sends.finish()


def layer(seq, live, tokens, cot, w, b, up, down, ow, ub, ob, db, rest, main, late, parts, spread):
    rows, width = tokens.shape
    unit = width + 1
    total = rows * parts
    nd = 8 if spread else 1
    share, tail, qrow = unit // nd, 256 // nd, 640 // nd
    tall = 2 * share + tail
    heads = (parts, rows + rows // 2, LANES)
    dma = lambda *shape: pltpu.SemaphoreType.DMA(shape)
    only = lambda *shape: shape if spread else (1, 1, 16, LANES)
    shape = jax.ShapeDtypeStruct
    vm = lambda *s: pltpu.VMEM(s, BF)
    return pl.pallas_call(
        partial(layer_kernel, spread),
        out_shape=(
            shape((rows, width), BF),
            shape((rows, width), BF),
            shape((3, total, LANES), F32),
            shape((8, tall + qrow, unit) if spread else (1, parts, tall, unit), BF),
            shape(only(8, parts, tail, unit), BF),
            shape(only(8, parts, 2 * share, unit), BF),
            shape(only(8, parts, qrow, unit), BF),
            shape((4, parts, tall, unit), BF) if spread else shape((640, unit), F32),
        ),
        in_specs=[SMEM, SMEM, VMEM, ANY, ANY, VMEM, ANY, ANY, ANY, VMEM, VMEM, VMEM, ANY, ANY, ANY],
        out_specs=(VMEM, VMEM) + (ANY,) * 6,
        scratch_shapes=[
            vm(total, unit),
            vm(unit, unit),
            vm(*(tall + qrow, unit) if spread else (16, LANES)),
            vm(3, total, LANES), vm(3, total, LANES), vm(3, total, LANES),
            vm(*heads), vm(*heads), vm(*heads),
            vm(parts, 4 * rows + rows // 2, LANES),
            pltpu.VMEM((rows, unit), F32),
            vm(*(2, 4, parts, tall, unit) if spread else (1, parts, tall, unit)),
            vm(*only(3, parts, tall, unit)),
            vm(*only(parts, tall, unit)),
            vm(*only(tall + qrow, unit)),
            vm(*only(4, qrow, unit)),
            vm(*only(3, qrow, unit)),
            dma(3, parts), dma(2, parts), dma(2, parts), dma(2, parts, 5), dma(4), dma(4), dma(2, parts),
            dma(2, parts + 1), dma(2, 3, parts + 1), dma(2, 2, parts), dma(2, 3), dma(2, 4), dma(2), dma(2, 3),
        ] + [dma(2, parts), dma(6, parts), dma(8, parts)] * 3,
        compiler_params=pltpu.CompilerParams(vmem_limit_bytes=LIMIT, collective_id=0, has_side_effects=True),
    )(seq, live, tokens, cot, w, b, up, down, ow, ub, ob, db, rest, main, late)


def pair_rows(w, axis):
    heads = [lax.slice_in_dim(w, k * HEAD, (k + 1) * HEAD, axis=axis) for k in range(9)]
    order = [heads[3 * (k % 2) + k // 2] for k in range(6)] + heads[6:] + [jnp.zeros_like(heads[0])]
    return jnp.concatenate(order, axis=axis)


def local(
    groups,
    tokens,
    cotangent,
    seq_length,
    live_rows,
    qkv_weight,
    qv_bias,
    out_weight,
    out_bias,
    up_weight,
    up_bias,
    down_weight,
    down_bias,
):
    parts = groups["tensor"]
    spread = groups["dp"] == 8
    nd = 8 if spread else 1
    rows, width = tokens.shape
    unit = width + 1
    piece = unit // nd
    as_row = lambda v: v.astype(F32)[None]

    w = jnp.transpose(qkv_weight, (1, 2, 0)).reshape(9 * HEAD, width)
    b = pair_rows(jnp.concatenate([qv_bias[0], jnp.zeros_like(qv_bias[0]), qv_bias[1]]).astype(F32), 0)[None]
    wide_row = lambda v: jnp.pad(as_row(v), ((0, 0), (0, 1)))
    if spread:
        full = [jnp.zeros((16, LANES), BF)] * 3
    else:
        wide = lambda v, tall=0: jnp.pad(v, ((0, tall), (0, unit - v.shape[1])))
        own = [wide(out_weight, 64), jnp.concatenate([up_weight, up_bias[None], wide(down_weight)]), wide(pair_rows(w, 0))]
        full = [lax.all_gather(v, "tensor", axis=0, tiled=False)[None] for v in own]
    mixed, token_grad, _, grads, _, _, _, wg = layer(
        seq_length, live_rows, tokens, cotangent, w, b, up_weight, down_weight, out_weight, as_row(up_bias),
        wide_row(out_bias), wide_row(down_bias), *full, parts, spread,
    )
    if spread:
        mine, wg = grads, grads[:, 2 * piece + 32 :].reshape(640, unit)
    else:
        mine = lax.psum_scatter(grads[0].astype(F32), "tensor", scatter_dimension=0, tiled=False)
        mine, wg = lax.psum((mine[None], wg), "dp")
    up_grad = mine[:, :piece].reshape(unit, unit).astype(F32)
    down_grad = mine[:, piece : 2 * piece].reshape(unit, unit)[:, :width].astype(F32)
    rest = mine[:, 2 * piece : 2 * piece + 256 // nd].reshape(256, unit).astype(F32)
    wg = jnp.concatenate(
        [wg[(2 * k if k < 3 else 2 * k - 5 if k < 6 else k) * HEAD :][:HEAD] for k in range(9)]
    ).astype(F32)
    biases = wg[:, width].reshape(3, 3 * HEAD)
    return (
        mixed,
        token_grad,
        jnp.transpose(wg[:, :width].reshape(3, 3 * HEAD, width), (2, 0, 1)),
        jnp.stack([biases[0], biases[2]]),
        rest[: 3 * HEAD, :width],
        rest[3 * HEAD, :width],
        up_grad[:width],
        up_grad[width],
        down_grad,
        rest[3 * HEAD + 1, :width],
    )


def solution(mesh):
    placed = (
        P(BOTH, None),
        P(BOTH, None),
        P("dp"),
        P("dp"),
        P(None, None, "tensor"),
        P(None, "tensor"),
        P("tensor", None),
        P(),
        P(None, "tensor"),
        P("tensor"),
        P("tensor", None),
        P(),
    )
    return jax.shard_map(
        partial(local, dict(mesh.shape)),
        mesh=mesh,
        in_specs=placed,
        out_specs=(
            P(BOTH, None),
            P(BOTH, None),
            P(None, None, "tensor"),
            P(None, "tensor"),
            P("tensor", None),
            P(),
            P(None, "tensor"),
            P("tensor"),
            P("tensor", None),
            P(),
        ),
        check_vma=False,
    )
```

```python
from functools import partial

import jax
import jax.numpy as jnp
from jax import lax
from jax.experimental import pallas as pl
from jax.experimental.pallas import tpu as pltpu
from jax.sharding import PartitionSpec as P

HEAD = 64
LANES = 128
EPSILON = 1e-05
HIDE = -1e30
BF = jnp.bfloat16
F32 = jnp.float32
BOTH = ("dp", "tensor")
VMEM = pl.BlockSpec(memory_space=pltpu.VMEM)
SMEM = pl.BlockSpec(memory_space=pltpu.SMEM)
ANY = pl.BlockSpec(memory_space=pl.ANY)
LIMIT = 63 * 1024 * 1024
EARLY = 2


def nn(a, b):
    return lax.dot_general(a, b, (((1,), (0,)), ((), ())), preferred_element_type=F32)


def nt(a, b):
    return lax.dot_general(a, b, (((1,), (1,)), ((), ())), preferred_element_type=F32)


def tn(a, b):
    return lax.dot_general(a, b, (((0,), (0,)), ((), ())), preferred_element_type=F32)


def lane_ids(rows):
    return lax.broadcasted_iota(jnp.int32, (rows, LANES), 1)


def half_turn(x):
    return pltpu.roll(x, HEAD, 1)


def fold(x):
    half = x.shape[0] // 2
    return jnp.where(lane_ids(half) < HEAD, x[:half], half_turn(x[half:]))


def unfold(x):
    low = lane_ids(x.shape[0]) < HEAD
    zero = jnp.zeros_like(x)
    return jnp.concatenate(
        [jnp.where(low, x, zero), jnp.where(low, half_turn(x), zero)], axis=0
    )


def split3(x):
    high = x.astype(BF).astype(F32)
    rest = x - high
    mid = rest.astype(BF).astype(F32)
    return high, mid, rest - mid


def norm_stats(x, width):
    s1 = jnp.sum(x, axis=-1, keepdims=True)
    s2 = jnp.sum(x * x, axis=-1, keepdims=True)
    return s1, lax.rsqrt((s2 + s1 * s1) / width + EPSILON)


def norm_pull(x, s1, r, g, width):
    dot = jnp.sum(g * x, axis=-1, keepdims=True)
    return g * r - (r * r * r * dot / width) * (x + s1)


def widen(ref, scratch):
    rows, width = ref.shape
    wide = scratch.shape[1]
    scratch[:, wide - LANES :] = jnp.zeros((rows, LANES), F32)
    scratch[:, :width] = ref[...].astype(F32)


def diag_mask(first, rows, live, turned):
    q_dim, k_dim = (1, 0) if turned else (0, 1)
    q = lax.broadcasted_iota(jnp.int32, (rows, rows), q_dim)
    k = lax.broadcasted_iota(jnp.int32, (rows, rows), k_dim)
    seen = (k <= q) & ((k + first < live) | (k == q))
    return jnp.where(seen, 0.0, HIDE).astype(F32)


def at_rows(i, rows):
    return pl.ds(pl.multiple_of(i * rows, rows), rows)


def fill_rows(dst, src, first, rows, width):
    wide = dst.shape[1]
    dst[first : first + rows, wide - LANES :] = jnp.zeros((rows, LANES), dst.dtype)
    dst[first : first + rows, :width] = src


class Sends:
    def __init__(self):
        self.ends = []

    def start(self, copy, when=None):
        if when is None:
            copy().start()
        else:
            pl.when(when())(lambda: copy().start())
        self.ends.append((copy, when))

    def finish(self):
        for copy, when in self.ends:
            if when is None:
                copy().wait_send()
            else:
                pl.when(when())(lambda copy=copy: copy().wait_send())


def remote(src, dst, ssem, rsem, **where):
    return pltpu.make_async_remote_copy(
        src_ref=src,
        dst_ref=dst,
        send_sem=ssem,
        recv_sem=rsem,
        device_id=where,
        device_id_type=pl.DeviceIdType.MESH,
    )


def neighbours(d):
    core, x, y = d % 2, (d // 2) % 2, d // 4
    return d + 1 - 2 * core, d + 2 - 4 * x, d + 4 - 8 * y


def greet(d, t, parts, spread, corner=False):
    barrier = pltpu.get_barrier_semaphore()

    def signal(**where):
        pl.semaphore_signal(barrier, inc=1, device_id=where, device_id_type=pl.DeviceIdType.MESH)

    for k in range(1, parts):
        signal(tensor=lax.rem(t + k, parts))
    if spread:
        core_n, x_n, y_n = neighbours(d)
        for n in (core_n, x_n, y_n) + ((x_n + y_n - d,) if corner else ()):
            signal(dp=n)
    return lambda: pl.semaphore_wait(barrier, parts - 1 + (3 + corner) * spread)


class Spread:
    def __init__(self, d, t, parts, piece, full, zsem, xsem, csem, sends, times):
        self.d, self.t, self.parts, self.piece, self.full, self.times = d, t, parts, piece, full, times
        self.zsem, self.xsem, self.csem, self.sends = zsem, xsem, csem, sends
        self.core_n, self.x_n, self.y_n = neighbours(d)
        self.diag = self.x_n + self.y_n - d

    def slot(self, e, b):
        return self.full.at[e, b]

    def out(self, to, ok):
        self.sends.start(
            lambda: remote(self.piece, self.slot(self.d, self.t), self.zsem.at[0, to], self.zsem.at[1, self.t], tensor=to), ok
        )

    def plane(self, b, first, ok):
        d, xs = self.d, self.xsem
        src = lambda: self.piece if first else self.slot(d, b)
        self.sends.start(lambda: remote(src(), self.slot(d, b), xs.at[0, b], xs.at[1, b], dp=self.x_n), ok)
        self.sends.start(lambda: remote(src(), self.slot(d, b), xs.at[2, b], xs.at[3, b], dp=self.y_n), ok)
        self.sends.start(
            lambda: remote(src(), self.slot(d, b), self.csem.at[0, b], self.csem.at[4, b], dp=self.core_n), ok
        )

    def arrive(self, b, ok):
        def wait():
            remote(self.slot(self.d, b), self.slot(self.d, b), self.zsem.at[0, b], self.zsem.at[1, b], tensor=b).wait_recv()

        pl.when(ok())(wait)
        self.plane(b, False, ok)

    def across(self, b, ok):
        xs, cs = self.xsem, self.csem
        east = lambda: self.slot(self.x_n, b)
        north = lambda: self.slot(self.y_n, b)

        def wait():
            remote(east(), east(), xs.at[0, b], xs.at[1, b], dp=self.x_n).wait_recv()
            remote(north(), north(), xs.at[2, b], xs.at[3, b], dp=self.y_n).wait_recv()

        pl.when(ok())(wait)
        self.sends.start(
            lambda: remote(east(), east(), xs.at[4, b], xs.at[5, b], dp=self.y_n), lambda: ok() & (b % 2 == 0)
        )
        self.sends.start(
            lambda: remote(north(), north(), xs.at[4, b], xs.at[5, b], dp=self.x_n), lambda: ok() & (b % 2 == 1)
        )
        self.sends.start(lambda: remote(east(), east(), cs.at[1, b], cs.at[5, b], dp=self.core_n), ok)
        self.sends.start(lambda: remote(north(), north(), cs.at[2, b], cs.at[6, b], dp=self.core_n), ok)

    def corner(self, b, ok):
        far, xs, cs = (lambda: self.slot(self.diag, b)), self.xsem, self.csem
        pl.when(ok())(lambda: remote(far(), far(), xs.at[4, b], xs.at[5, b], dp=self.x_n).wait_recv())
        self.sends.start(lambda: remote(far(), far(), cs.at[3, b], cs.at[7, b], dp=self.core_n), ok)

    def at(self, point):
        own = lambda: self.t >= 0
        for job in ("out", "plane", "arrive", "across", "corner"):
            for (k, m), when in self.times[job].items():
                if when != point:
                    continue
                if k == m:
                    self.plane(self.t, True, own) if job == "plane" else getattr(self, job)(self.t, own)
                    continue
                for mirror in (False, True):
                    here, there = (self.parts - 1 - k, self.parts - 1 - m) if mirror else (k, m)
                    getattr(self, job)(there, lambda here=here: self.t == here)

    def ready(self, b):
        shift = self.core_n - self.d
        for k, e in enumerate((self.d, self.x_n, self.y_n, self.diag)):
            there = self.slot(e + shift, b)
            remote(there, there, self.csem.at[k, b], self.csem.at[4 + k, b], dp=self.core_n).wait_recv()


PAIRS = [(k, m) for k in range(4) for m in range(k)]
REST_TIMES = {
    "out": {(m, k): "p1" for k, m in PAIRS},
    "plane": {(0, 0): "p0"},
    "arrive": {pair: "p3" for pair in PAIRS},
    "across": {(0, 0): "p1", **{pair: "h0" for pair in PAIRS}},
    "corner": {(0, 0): "p2", **{pair: "h1" for pair in PAIRS}},
}
MAIN_TIMES = {
    "out": {(2, 3): "p0", (0, 1): "p1", (1, 2): "p2", (0, 2): "p2", (1, 3): "h2", (0, 3): "p3"},
    "plane": {(0, 0): "p0"},
    "arrive": {(3, 2): "p1", (1, 0): "p2", (2, 1): "h1", (2, 0): "h1", (3, 1): "h1", (3, 0): "h2"},
    "across": {(0, 0): "p1", (3, 2): "p3", (1, 0): "h0", (2, 0): "h2", (2, 1): "e", (3, 1): "e", (3, 0): "q0"},
    "corner": {(0, 0): "p2", (3, 2): "h0", (1, 0): "h1", (2, 0): "e", (3, 1): "q0", (2, 1): "q1", (3, 0): "q1"},
}
LATE_TIMES = {
    "out": {(m, k): "e" for k, m in PAIRS},
    "plane": {(0, 0): "p0"},
    "arrive": {pair: "q0" for pair in PAIRS},
    "across": {(0, 0): "p1", **{pair: "q1" for pair in PAIRS}},
    "corner": {(0, 0): "p2", **{pair: "q2" for pair in PAIRS}},
}
SENT = (4, 2, 3)
SERVE = {(0, 0): ((), (0,)), (0, 1): ((), (1,)), (1, 1): ((), (4, 2)), (2, 2): ((), (3,))}


def owner_order(d):
    return 4 * (d % 2) + d // 2


def layer_kernel(
    spread, seq_ref, live_ref, tok_ref, cot_any, w_any, b_ref, up_any, down_any, ow_any, ub_ref, ob_ref, db_ref, rest_in, main_in, late_in,
    mixed_ref, out_ref, o_any, fin_any, fin_down, fin_rest, fin_wg, rest_out, main_out, late_out, r1_any,
    n1_ref, wq, piece, qx_ref, kx_ref, vx_ref, pack_ref, heads_in, hg_in, recv_ref, hid_ref, gbuf, r2, r3, fst, w1, w2,
    nsem, hsem, gsem, qsem, own_sem, lsem, wsem, s1, s2, s3, s4, s5, u1, u2, *gsems,
):
    rows, width = tok_ref.shape
    unit = n1_ref.shape[1]
    blocks = parts = heads_in.shape[0]
    nd = 8 if spread else 1
    share, tail, qrow = unit // nd, 256 // nd, 640 // nd
    d, t = lax.axis_index("dp"), lax.axis_index("tensor")
    core = d % 2
    barrier = greet(d, t, parts, spread, True)
    sends, heads_sends = Sends(), Sends()
    seq, live = seq_ref[0], live_ref[0]
    lane = lane_ids(rows)
    low = lane < HEAD
    row = lax.broadcasted_iota(jnp.int32, (rows, LANES), 0)
    spare = lax.broadcasted_iota(jnp.int32, (rows, unit), 1) == width
    rest_full, main_full, late_full = (rest_out, main_out, late_out) if spread else (rest_in, main_in, late_in)
    gathers = []
    if spread:
        main_piece, rest_piece = piece.at[pl.ds(0, 2 * share)], piece.at[pl.ds(2 * share, tail)]
        late_piece = piece.at[pl.ds(2 * share + tail, qrow)]
        for k, (own, full, times) in enumerate(
            ((rest_piece, rest_out, REST_TIMES), (main_piece, main_out, MAIN_TIMES), (late_piece, late_out, LATE_TIMES))
        ):
            gathers.append(Spread(d, t, parts, own, full, *gsems[3 * k : 3 * k + 3], sends, times))

    def point(name):
        for gather in gathers:
            gather.at(name)

    def when_point(cond, name):
        if spread:
            pl.when(cond)(lambda: point(name))

    def turn(k):
        a, b = (t + k - 2 * (t % 2) * (k % 2)) % 2, t // 2 + k // 2 - 2 * (t // 2) * (k // 2)
        return a + 2 * b

    def prologue(wide, w_sc, up_sc, down_sc, ow_sc):
        loads = [
            pltpu.make_async_copy(src, dst, lsem.at[k])
            for k, (src, dst) in enumerate(((w_any, w_sc), (up_any, up_sc), (down_any, down_sc), (ow_any, ow_sc)))
        ]
        for load in loads if spread else loads[:1]:
            load.start()
        widen(tok_ref, wide)
        x = wide[...]
        _, r = norm_stats(x, width + 1)
        n1_ref[at_rows(t, rows), :] = jnp.where(spare, 1.0, x * r).astype(BF)
        barrier()
        for up in (True, False):
            sends.start(lambda up=up: line(t, up), lambda up=up: edge(up))
        loads[0].wait()
        for k in range(9):
            take = 3 * (k % 2) + k // 2 if k < 6 else k
            fill_rows(wq, w_sc[take * HEAD : (take + 1) * HEAD, :], k * HEAD, HEAD, width)
        wq[9 * HEAD : 10 * HEAD, :] = jnp.zeros((HEAD, unit), BF)
        if not spread:
            return
        near = share - 16
        piece[:, unit - LANES :] = jnp.zeros((piece.shape[0], LANES), BF)
        for load in loads[1:]:
            load.wait()
        piece[:near, :] = up_sc[pl.ds(pl.multiple_of(d * share, 16), near), :]

        @pl.when(d < nd - 1)
        def _():
            piece[near:share, :] = up_sc[pl.ds(pl.multiple_of(d * share + near, 16), 16), :]

        @pl.when(d == nd - 1)
        def _():
            last = jnp.concatenate([up_sc[width - 15 :, :].astype(F32), ub_ref[...]], axis=0)
            piece[near:share, :] = last.astype(BF)

        piece[share : 2 * share, :width] = down_sc[pl.ds(pl.multiple_of(d * share, 16), share), :]

        @pl.when(d < 6)
        def _():
            piece[2 * share : 2 * share + tail, :width] = ow_sc[pl.ds(pl.multiple_of(d * tail, 16), tail), :]

        @pl.when(d >= 6)
        def _():
            piece[2 * share : 2 * share + tail, :] = jnp.zeros((tail, unit), BF)

        piece[2 * share + tail :, :] = wq[pl.ds(pl.multiple_of(d * qrow, 16), qrow), :]

    def line(b, up):
        block = n1_ref.at[at_rows(b, rows), :]
        return remote(block, block, nsem.at[1 if up else 2, b], nsem.at[0, b], tensor=t + 1 if up else t - 1)

    def edge(up):
        return t < parts - 1 if up else t > 0

    def place(s, up):
        b = t - s if up else t + s
        return b, (lambda: t - s >= 0) if up else (lambda: t + s < parts)

    places = {(s, up): place(s, up) for s in range(1, parts) for up in (True, False)}
    pl.run_scoped(
        prologue,
        pltpu.VMEM((rows, unit), F32),
        pltpu.VMEM(w_any.shape, BF),
        pltpu.VMEM(up_any.shape, BF),
        pltpu.VMEM(down_any.shape, BF),
        pltpu.VMEM(ow_any.shape, BF),
    )
    homes = []
    if spread:
        for k, gather in enumerate(gathers):
            homes.append(pltpu.make_async_copy(gather.piece, gather.slot(d, t), own_sem.at[k]))
            homes[-1].start()
        point("p0")

    def attend(o_ref, mask_ref, s_ref):
        def project(i):
            at = at_rows(i, rows)
            qkv = nt(n1_ref[at, :], wq[: 10 * HEAD, :]) + b_ref[...]
            qkv = qkv.astype(BF).astype(F32)
            key = row + i * rows
            m = lane - HEAD
            same = ((m * rows) ^ (i * rows)) < seq
            open_ = (m == i) | (same & (key < live))
            bias = jnp.where(m < blocks, jnp.where(open_, 0.0, HIDE), jnp.where(m < blocks + 3, 1.0, 0.0))
            hot = jnp.where(m == i, 1.0, 0.0)
            ones = jnp.where(m < 3, 1.0, 0.0)
            for h in range(3):
                pair = qkv[:, h * LANES : (h + 1) * LANES]
                qx_ref[h, at, :] = jnp.where(low, pair * HEAD**-0.5, hot).astype(BF)
                kx_ref[h, at, :] = jnp.where(low, half_turn(pair), bias).astype(BF)
                val = qkv[:, (3 + h // 2) * LANES : (4 + h // 2) * LANES]
                vx_ref[h, at, :] = jnp.where(low, half_turn(val) if h % 2 else val, ones).astype(BF)
            mask_ref[i] = diag_mask(i * rows, rows, live, False).astype(BF)

        for s in range(parts):
            if s:
                for up in (True, False):
                    b, ok = places[s, up]
                    pl.when(ok())(lambda b=b, up=up: line(b, up).wait_recv())
                    sends.start(lambda b=b, up=up: line(b, up), lambda ok=ok, up=up: ok() & edge(up))
                point(f"p{s}")

            def arrived(e, carry, s=s):
                b = t + (2 * e - 1) * s
                pl.when((b >= 0) & (b < parts))(lambda: project(b))
                return carry

            lax.fori_loop(0, 2 if s else 1, arrived, 0)

        def head(h, carry):
            for i in range(blocks):
                q = qx_ref[h, i * rows : (i + 1) * rows, :]
                top = None
                for j in range(i, -1, -1):
                    s = nt(q, kx_ref[h, j * rows : (j + 1) * rows, :])
                    if i == j:
                        s = s + mask_ref[i].astype(F32)
                    peak = jnp.max(s, axis=-1, keepdims=True)
                    top = peak if top is None else jnp.maximum(top, peak)
                    s_ref[j] = s
                acc = None
                for j in range(i + 1):
                    p = jnp.exp(s_ref[j] - top).astype(BF)
                    part = nn(p, vx_ref[h, j * rows : (j + 1) * rows, :])
                    acc = part if acc is None else acc + part
                mass = acc[:, HEAD : HEAD + 1]
                lse = top + jnp.log(mass)
                o_ref[h, i * rows : (i + 1) * rows, :] = acc / mass
                hi, mid, lo = split3(-lse)
                ext = jnp.where(
                    lane == HEAD + blocks,
                    hi,
                    jnp.where(lane == HEAD + blocks + 1, mid, jnp.where(lane == HEAD + blocks + 2, lo, q.astype(F32))),
                )
                qx_ref[h, i * rows : (i + 1) * rows, :] = ext.astype(BF)
            for k in range(3):
                when_point(h == k, f"h{k}")
            return carry

        lax.fori_loop(0, 3, head, 0)
        keep = pltpu.make_async_copy(o_ref, o_any, lsem.at[0])
        keep.start()

        def pack(i, carry):
            at = at_rows(i, rows)
            pack_ref[i, :rows, :] = jnp.where(low, o_ref[0, at, :], half_turn(o_ref[1, at, :])).astype(BF)
            pack_ref[i, rows:, :] = fold(o_ref[2, at, :]).astype(BF)
            return carry

        lax.fori_loop(0, blocks, pack, 0)
        swap_start(pack_ref, heads_in, hsem, heads_sends)
        point("e")
        keep.wait()

    def swap(src_ref, dst_ref, sems, k, taking):
        to = lax.rem(t + (parts - k if taking else k), parts)
        src, dst = (to, to) if taking else (to, t)
        return remote(src_ref.at[src], dst_ref.at[dst], sems.at[0, k], sems.at[1, k], tensor=to)

    def swap_home(src_ref, dst_ref, sems):
        return pltpu.make_async_copy(src_ref.at[t], dst_ref.at[t], sems.at[0, 0])

    def swap_start(src_ref, dst_ref, sems, sends):
        for k in (2, 1, 3):
            sends.start(lambda k=k: swap(src_ref, dst_ref, sems, k, False))
        swap_home(src_ref, dst_ref, sems).start()

    def swap_end(src_ref, dst_ref, sems):
        for k in range(1, parts):
            swap(src_ref, dst_ref, sems, k, True).wait_recv()
        swap_home(src_ref, dst_ref, sems).wait()

    pl.run_scoped(
        attend,
        pltpu.VMEM((3, rows * parts, LANES), F32),
        pltpu.VMEM((parts, rows, rows), BF),
        pltpu.VMEM((parts, rows, rows), F32),
    )

    core_n, x_n, y_n = neighbours(d)
    chips = (x_n, y_n, x_n + y_n - d)
    main_rows, rest_rows = pl.ds(0, 2 * share), pl.ds(2 * share, tail)
    half = gbuf.at[core] if spread else gbuf
    every = pl.ds(0, parts)

    def region(k):
        if isinstance(k, int) and k == parts:
            return every, rest_rows
        return turn(k), main_rows

    def to_core(k):
        which, at = region(k)
        return remote(gbuf.at[1 - core, :, which, at], r1_any.at[:, which, at], s1.at[0, k], s1.at[1, k], dp=core_n)

    def second(c, k):
        which, at = region(k)
        return remote(
            gbuf.at[core, chips[c] // 2, which, at], r2.at[c, which, at], s2.at[0, c, k], s2.at[1, c, k], dp=chips[c]
        )

    def add_core(k, stage, stage_rest):
        to_core(k).wait_recv()
        which, at = region(k)
        here = stage_rest if isinstance(k, int) and k == parts else stage
        load = pltpu.make_async_copy(r1_any.at[:, which, at], here, lsem.at[0])
        load.start()
        load.wait()
        for q in range(4):
            gbuf[core, q, which, at] = (gbuf[core, q, which, at].astype(F32) + here[q].astype(F32)).astype(BF)

    def third(k, m):
        b, at = turn(k), (main_rows, rest_rows)[m]
        return remote(gbuf.at[core, d // 2, b, at], r3.at[t, at], s3.at[0, m, b], s3.at[1, m, t], tensor=b)

    def send_second(k):
        for c in range(3):
            sends.start(lambda c=c: second(c, k))

    def sum_second(k):
        for c in range(3):
            second(c, k).wait_recv()
        which, at = region(k)
        total = gbuf[core, d // 2, which, at].astype(F32)
        for c in range(3):
            total = total + r2[c, which, at].astype(F32)
        gbuf[core, d // 2, which, at] = total.astype(BF)
        if k == parts:
            for j in range(1, parts):
                sends.start(lambda j=j: third(j, 1))
        elif k:
            sends.start(lambda: third(k, 0))

    def middle(wu, wd, wm, acts, ugs, xall, n2_ref, gb_ref, wide, dn_ref, stage):
        stage_rest = wm.at[pl.ds(0, 4)] if spread else None
        wo = wq

        def fetch(k, slot):
            return [
                pltpu.make_async_copy(main_full.at[:, turn(k), pl.ds(m * share, share), :], dst.at[slot], wsem.at[m, slot])
                for m, dst in enumerate((wu, wd))
            ]

        def fetch_start(k, slot):
            if spread:
                gathers[1].ready(turn(k))
            for copy in fetch(k, slot):
                copy.start()

        cot_load = pltpu.make_async_copy(cot_any, mixed_ref, lsem.at[1])
        cot_load.start()
        if spread:
            for home in homes[:2]:
                home.wait()
            for b in range(parts):
                gathers[0].ready(b)
        rest_load = pltpu.make_async_copy(rest_full, wm, lsem.at[0])
        rest_load.start()
        fetch_start(0, 0)
        cot_load.wait()
        widen(mixed_ref, wide)
        gb_ref[...] = wide[...].astype(BF)
        widen(tok_ref, wide)
        rest_load.wait()
        for b in range(parts):
            own = wm[:, b].reshape(tail * nd, unit)
            wo[b * LANES : (b + 1) * LANES, :] = own[:LANES]
            wo[parts * LANES + b * HEAD : parts * LANES + (b + 1) * HEAD, :] = own[LANES : LANES + HEAD]
        swap_end(pack_ref, heads_in, hsem)
        lows = []
        for b in range(parts):
            xall[:, b * LANES : (b + 1) * LANES] = heads_in[b, :rows, :]
            lows.append(unfold(heads_in[b, rows:, :].astype(F32)))
        for k in range(parts // 2):
            both = jnp.where(low, lows[2 * k], half_turn(lows[2 * k + 1]))
            xall[:, (parts + k) * LANES : (parts + k + 1) * LANES] = both.astype(BF)
        point("q0")
        hidden = wide[...] + nn(xall[...], wo[...]) + ob_ref[...]
        s1_, r = norm_stats(hidden, width + 1)
        n2_ref[...] = jnp.where(spare, 1.0, hidden * r).astype(BF)
        hid_ref[...] = hidden
        wide[...] = hidden + db_ref[...]
        dn_ref[...] = jnp.zeros_like(dn_ref)
        root = (2 / jnp.pi) ** 0.5

        def store_grads(k, act, ug):
            b = turn(k)
            up_g = tn(n2_ref[...], ug).astype(BF)
            down_g = tn(act, gb_ref[...]).astype(BF)
            if spread:
                gbuf[:, :, b, :share, :] = up_g.reshape(2, 4, share, unit)
                gbuf[:, :, b, share : 2 * share, :] = down_g.reshape(2, 4, share, unit)
                to_core(k).start()
            else:
                gbuf[0, b, :share, :] = up_g
                gbuf[0, b, share : 2 * share, :] = down_g

        def unit_block(k, carry):
            slot = k % 2
            for copy in fetch(k, slot):
                copy.wait()
            up = wu[slot].reshape(unit, unit)
            down = wd[slot].reshape(unit, unit)

            def some_rows(i, carry):
                at = at_rows(i, rows // 2)
                u = nn(n2_ref[at, :], up)
                th = jnp.tanh(root * (u + 0.044715 * (u * u * u)))
                act = (0.5 * u * (1 + th)).astype(BF)
                slope = 0.5 * (1 + th) + (0.5 * u) * (1 - th * th) * (root * (1 + 0.134145 * (u * u)))
                acts[slot, at, :] = act
                wide[at, :] += nn(act, down)
                ug = (nt(gb_ref[at, :], down) * slope).astype(BF)
                ugs[slot, at, :] = ug
                dn_ref[at, :] += nt(ug, up)
                return carry

            lax.fori_loop(0, 2, some_rows, 0)
            pl.when(k < parts - 1)(lambda: fetch_start(k + 1, (k + 1) % 2))
            pl.when(k < EARLY)(lambda: store_grads(k, acts[slot], ugs[slot]))

            if spread:
                for m in range(1, EARLY + 1):
                    pl.when(k == m)(lambda m=m: add_core(m - 1, stage, stage_rest))
                pl.when(k == 1)(lambda: send_second(0))
                pl.when(k == 3)(lambda: send_second(1))
            for m in range(parts):
                when_point(k == m, f"q{m + 1}")
            return carry

        lax.fori_loop(0, parts, unit_block, 0)
        hidden = hid_ref[...]
        gout = gb_ref[...].astype(F32)
        hidgrad = gout + norm_pull(hidden, s1_, r, dn_ref[...], width + 1)
        ag = hidgrad.astype(BF)
        hg = nt(ag, wo[...])
        heads_sends.finish()
        for b in range(parts):
            pack_ref[b, :rows, :] = hg[:, b * LANES : (b + 1) * LANES].astype(BF)
            pair = hg[:, (parts + b // 2) * LANES : (parts + b // 2 + 1) * LANES]
            pack_ref[b, rows:, :] = fold(half_turn(pair) if b % 2 else pair).astype(BF)
        swap_start(pack_ref, hg_in, gsem, sends)
        point("g")
        mixed_ref[...] = wide[:, :width].astype(BF)
        hid_ref[...] = hidgrad
        out_bias_grad = jnp.sum(hidgrad, axis=0, keepdims=True)
        down_bias_grad = jnp.sum(gout, axis=0, keepdims=True)
        wide[...] = tn(xall[:, : parts * LANES], ag)
        dn_ref[: parts * HEAD, :] = tn(xall[:, parts * LANES :], ag)
        extra = lax.broadcasted_iota(jnp.int32, (HEAD, unit), 0)
        extra = jnp.where(extra == 0, out_bias_grad, jnp.where(extra == 1, down_bias_grad, 0.0))
        for b in range(parts):
            pair = wide[b * LANES : (b + 1) * LANES, :]
            low_part = dn_ref[b * HEAD : (b + 1) * HEAD, :]
            misc = jnp.concatenate([pair, low_part, extra], axis=0).astype(BF)
            if spread:
                gbuf[:, :, b, 2 * share :, :] = misc.reshape(2, 4, tail, unit)
            else:
                gbuf[0, b, 2 * share :, :] = misc
        if spread:
            to_core(parts).start()

        def late(k, carry):
            store_grads(k, acts[k % 2], ugs[k % 2])
            return carry

        lax.fori_loop(EARLY, parts, late, 0)
        if spread:
            for k in [parts] + list(range(EARLY, parts)):
                add_core(k, stage, stage_rest)
            for k in SENT:
                send_second(k)
        else:
            out = pltpu.make_async_copy(gbuf, fin_any, lsem.at[0])
            out.start()
            out.wait()

    square, low_square = pltpu.VMEM((rows, unit), F32), pltpu.VMEM((rows, unit), BF)
    pl.run_scoped(
        middle,
        pltpu.VMEM((2, nd, share, unit), BF),
        pltpu.VMEM((2, nd, share, unit), BF),
        pltpu.VMEM((nd, parts, tail, unit), BF),
        pltpu.VMEM((parts - EARLY, rows, unit), BF),
        pltpu.VMEM((parts - EARLY, rows, unit), BF),
        low_square,
        low_square,
        low_square,
        square,
        square,
        pltpu.VMEM((4, 2 * share, unit) if spread else (16, LANES), BF),
    )

    def back(gpack, wgb, dox, dvs, dqt, dk_ref, mask_ref, xt, wg_acc, wmq, dn_ref):
        local = Sends()
        wide = wg_acc.at[pl.ds(0, rows)]

        def o_load(i):
            return pltpu.make_async_copy(o_any.at[:, pl.ds(i * rows, rows), :], dk_ref.at[pl.ds(0, 3)], lsem.at[0])

        def w_load(k):
            return pltpu.make_async_copy(late_full.at[:, k], wmq.at[k], wsem.at[0, k])

        def swap_grads(k, p, taking):
            to = lax.rem(t + (parts - k if taking else k), parts)
            src, dst = (to, to) if taking else (to, t)
            at = pl.ds(p * rows, rows if p < 4 else rows // 2)
            return remote(gpack.at[src].at[at], recv_ref.at[dst].at[at], qsem.at[0, k, p], qsem.at[1, k, p], tensor=to)

        def send_grads(p):
            for k in (2, 1, 3):
                local.start(lambda k=k: swap_grads(k, p, False))

        o_load(0).start()

        def masks(i, carry):
            mask_ref[i] = diag_mask(i * rows, rows, live, True).astype(BF)
            return carry

        lax.fori_loop(0, blocks, masks, 0)
        swap_end(pack_ref, hg_in, gsem)
        for i in range(blocks):
            o_load(i).wait()
            pair = hg_in[i, :rows, :].astype(F32)
            last = unfold(hg_in[i, rows:, :].astype(F32))
            for h, g in enumerate((pair, half_turn(pair), last)):
                g = jnp.where(low, g, 0.0)
                hi, mid, lo = split3(-jnp.sum(g * dk_ref[h], axis=-1, keepdims=True))
                g = jnp.where(lane == HEAD, hi, jnp.where(lane == HEAD + 1, mid, jnp.where(lane == HEAD + 2, lo, g)))
                dox[h, i * rows : (i + 1) * rows, :] = g.astype(BF)
            if i + 1 < blocks:
                o_load(i + 1).start()
        if spread:
            homes[2].wait()
            for k in range(parts):
                gathers[2].ready(k)
        for k in range(parts):
            w_load(k).start()

        def head(h, carry):
            spot = lax.rem(h, 2)
            for j in range(blocks):
                keys = kx_ref[h, j * rows : (j + 1) * rows, :]
                keys_t = jnp.transpose(keys.astype(F32)).astype(BF)
                vals = vx_ref[h, j * rows : (j + 1) * rows, :]
                dk = dv = None
                for i in range(j, blocks):
                    q = qx_ref[h, i * rows : (i + 1) * rows, :]
                    do = dox[h, i * rows : (i + 1) * rows, :]
                    s = nt(keys, q)
                    if i == j:
                        s = s + mask_ref[i].astype(F32)
                    p = jnp.exp(s)
                    ds = (p * nt(vals, do)).astype(BF)
                    dv_part = nn(p.astype(BF), do)
                    dk_part = nn(ds, q)
                    dq_part = nn(keys_t, ds)
                    dk = dk_part if dk is None else dk + dk_part
                    dv = dv_part if dv is None else dv + dv_part
                    if j == 0:
                        dqt[i] = dq_part
                    else:
                        dqt[i] += dq_part
                dk_ref[j] = dk
                dvs[spot, j * rows : (j + 1) * rows, :] = dv.astype(BF)
                if spread:
                    for step, (sent, summed) in SERVE.items():
                        if step[1] == j:

                            @pl.when(h == step[0])
                            def _(sent=sent, summed=summed):
                                for k in sent:
                                    send_second(k)
                                for k in summed:
                                    sum_second(k)

            at = pl.ds(pl.multiple_of(h * rows, rows), rows)
            for i in range(blocks):
                dq = jnp.transpose(dqt[i]) * HEAD**-0.5
                gpack[i, at, :] = jnp.where(low, dq, half_turn(dk_ref[i])).astype(BF)
            for p in range(3):
                pl.when(h == p)(lambda p=p: send_grads(p))

            @pl.when(h == 1)
            def _():
                for i in range(blocks):
                    mine = pl.ds(i * rows, rows)
                    gpack[i, 3 * rows : 4 * rows, :] = jnp.where(low, dvs[0, mine, :].astype(F32), half_turn(dvs[1, mine, :].astype(F32))).astype(BF)
                send_grads(3)

            @pl.when(h == 2)
            def _():
                for i in range(blocks):
                    gpack[i, 4 * rows :, :] = fold(dvs[0, i * rows : (i + 1) * rows, :].astype(F32)).astype(BF)
                send_grads(4)

            return carry

        lax.fori_loop(0, 3, head, 0)
        home = pltpu.make_async_copy(gpack.at[t], recv_ref.at[t], qsem.at[0, 0, 0])
        home.start()

        def spread_lanes(ref, i):
            for k in range(4):
                xt[:, k * LANES : (k + 1) * LANES] = ref[i, k * rows : (k + 1) * rows, :]
            xt[:, 4 * LANES :] = unfold(ref[i, 4 * rows :, :].astype(F32)).astype(BF)

        wg_acc[...] = jnp.zeros_like(wg_acc)

        def weigh(i, carry):
            spread_lanes(gpack, i)
            wg_acc[...] += tn(xt[...], n1_ref[at_rows(i, rows), :])
            return carry

        lax.fori_loop(0, blocks, weigh, 0)
        tall = 2 * share + tail
        if spread:
            order = [2 * k if k < 3 else 2 * k - 5 if k < 6 else k for k in range(10)]
            natural = jnp.concatenate([wg_acc[k * HEAD : (k + 1) * HEAD, :] for k in order], axis=0)
            wgb[...] = natural.astype(BF).reshape(2, 4, qrow, unit)

            def w_first():
                return remote(wgb.at[1 - core], w1, u1.at[0], u1.at[1], dp=core_n)

            def w_second(c):
                return remote(wgb.at[core, chips[c] // 2], w2.at[c], u2.at[0, c], u2.at[1, c], dp=chips[c])

            local.start(w_first)
            w_first().wait_recv()
            for q in range(4):
                wgb[core, q] = (wgb[core, q].astype(F32) + w1[q].astype(F32)).astype(BF)
            for c in range(3):
                local.start(lambda c=c: w_second(c))
            total = wgb[core, d // 2].astype(F32)
            for c in range(3):
                w_second(c).wait_recv()
                total = total + w2[c].astype(F32)
            fst[tall:, :] = total.astype(BF)
            total = gbuf[core, d // 2, t].astype(F32)
            for k in range(1, parts):
                b = turn(k)
                for m, at in enumerate((main_rows, rest_rows)):
                    there = r3.at[b, at]
                    remote(there, there, s3.at[0, m, b], s3.at[1, m, b], tensor=b).wait_recv()
                total = total + r3[b].astype(F32)
            fst[:tall, :] = total.astype(BF)

            cuts = ((fin_any, 0, share), (fin_down, share, share), (fin_rest, 2 * share, tail), (fin_wg, tall, qrow))

            def piece_of(m, e):
                return cuts[m][0].at[e]

            def sum_of(m):
                return fst.at[pl.ds(cuts[m][1], cuts[m][2])]

            def give(c, m):
                return remote(sum_of(m), piece_of(m, owner_order(d)), s4.at[0, c, m], s4.at[1, c, m], dp=chips[c])

            def came(c, m):
                there = piece_of(m, owner_order(chips[c]))
                return remote(there, there, s4.at[0, c, m], s4.at[1, c, m], dp=chips[c])

            def give_core(c, m):
                there = piece_of(m, owner_order(d if c == 3 else chips[c]))
                return remote(sum_of(m) if c == 3 else there, there, s5.at[0, c, m], s5.at[1, c, m], dp=core_n)

            owns = [
                pltpu.make_async_copy(sum_of(m), piece_of(m, owner_order(d)), lsem.at[m]) for m in range(4)
            ]
            for m in range(4):
                owns[m].start()
                for c in (2, 0, 1):
                    sends.start(lambda c=c, m=m: give(c, m))
                sends.start(lambda m=m: give_core(3, m))
        else:
            out = pltpu.make_async_copy(wg_acc, r1_any, own_sem.at[3])
            out.start()
            out.wait()
        widen(tok_ref, wide)
        dn_ref[...] = jnp.zeros_like(dn_ref)
        home.wait()
        for k in range(1, parts):
            for p in range(5):
                swap_grads(k, p, True).wait_recv()
        for k in range(parts):
            w_load(k).wait()

        def part(b, carry):
            spread_lanes(recv_ref, b)
            dn_ref[...] += nn(xt[...], wmq[b].reshape(nd * qrow, unit))
            return carry

        lax.fori_loop(0, parts, part, 0)
        x = wide[...]
        s1_, r = norm_stats(x, width + 1)
        grad = hid_ref[...] + norm_pull(x, s1_, r, dn_ref[...], width + 1)
        out_ref[...] = grad[:, :width].astype(BF)
        if spread:
            for c in range(3):
                for m in range(4):
                    came(c, m).wait_recv()
                    sends.start(lambda c=c, m=m: give_core(c, m))
            for c in range(4):
                for m in range(4):
                    give_core(c, m).wait_recv()
            for own in owns:
                own.wait()
        local.finish()

    pack = (parts, 4 * rows + rows // 2, LANES)
    pl.run_scoped(
        back,
        pltpu.VMEM(pack, BF),
        pltpu.VMEM((2, 4, qrow, unit) if spread else (16, LANES), BF),
        pltpu.VMEM((3, rows * parts, LANES), BF),
        pltpu.VMEM((2, rows * parts, LANES), BF),
        pltpu.VMEM((parts, LANES, rows), F32),
        pltpu.VMEM((parts, rows, LANES), F32),
        pltpu.VMEM((parts, rows, rows), BF),
        pltpu.VMEM((rows, 5 * LANES), BF),
        pltpu.VMEM((5 * LANES, unit), F32),
        pltpu.VMEM((parts, nd, qrow, unit), BF),
        square,
    )
    if spread:
        for k in range(parts + 1):
            to_core(k).wait_send()
    sends.finish()


def layer(seq, live, tokens, cot, w, b, up, down, ow, ub, ob, db, rest, main, late, parts, spread):
    rows, width = tokens.shape
    unit = width + 1
    total = rows * parts
    nd = 8 if spread else 1
    share, tail, qrow = unit // nd, 256 // nd, 640 // nd
    tall = 2 * share + tail
    heads = (parts, rows + rows // 2, LANES)
    dma = lambda *shape: pltpu.SemaphoreType.DMA(shape)
    only = lambda *shape: shape if spread else (1, 1, 16, LANES)
    shape = jax.ShapeDtypeStruct
    vm = lambda *s: pltpu.VMEM(s, BF)
    return pl.pallas_call(
        partial(layer_kernel, spread),
        out_shape=(
            shape((rows, width), BF),
            shape((rows, width), BF),
            shape((3, total, LANES), F32),
            shape((8, share, unit) if spread else (1, parts, tall, unit), BF),
            shape(only(8, share, unit), BF),
            shape(only(8, tail, unit), BF),
            shape(only(8, qrow, unit), BF),
            shape(only(8, parts, tail, unit), BF),
            shape(only(8, parts, 2 * share, unit), BF),
            shape(only(8, parts, qrow, unit), BF),
            shape((4, parts, tall, unit), BF) if spread else shape((640, unit), F32),
        ),
        in_specs=[SMEM, SMEM, VMEM, ANY, ANY, VMEM, ANY, ANY, ANY, VMEM, VMEM, VMEM, ANY, ANY, ANY],
        out_specs=(VMEM, VMEM) + (ANY,) * 9,
        scratch_shapes=[
            vm(total, unit),
            vm(unit, unit),
            vm(*(tall + qrow, unit) if spread else (16, LANES)),
            vm(3, total, LANES), vm(3, total, LANES), vm(3, total, LANES),
            vm(*heads), vm(*heads), vm(*heads),
            vm(parts, 4 * rows + rows // 2, LANES),
            pltpu.VMEM((rows, unit), F32),
            vm(*(2, 4, parts, tall, unit) if spread else (1, parts, tall, unit)),
            vm(*only(3, parts, tall, unit)),
            vm(*only(parts, tall, unit)),
            vm(*only(tall + qrow, unit)),
            vm(*only(4, qrow, unit)),
            vm(*only(3, qrow, unit)),
            dma(3, parts), dma(2, parts), dma(2, parts), dma(2, parts, 5), dma(4), dma(4), dma(2, parts),
            dma(2, parts + 1), dma(2, 3, parts + 1), dma(2, 2, parts), dma(2, 3, 4), dma(2, 4, 4), dma(2), dma(2, 3),
        ] + [dma(2, parts), dma(6, parts), dma(8, parts)] * 3,
        compiler_params=pltpu.CompilerParams(vmem_limit_bytes=LIMIT, collective_id=0, has_side_effects=True),
    )(seq, live, tokens, cot, w, b, up, down, ow, ub, ob, db, rest, main, late)


def pair_rows(w, axis):
    heads = [lax.slice_in_dim(w, k * HEAD, (k + 1) * HEAD, axis=axis) for k in range(9)]
    order = [heads[3 * (k % 2) + k // 2] for k in range(6)] + heads[6:] + [jnp.zeros_like(heads[0])]
    return jnp.concatenate(order, axis=axis)


def local(
    groups,
    tokens,
    cotangent,
    seq_length,
    live_rows,
    qkv_weight,
    qv_bias,
    out_weight,
    out_bias,
    up_weight,
    up_bias,
    down_weight,
    down_bias,
):
    parts = groups["tensor"]
    spread = groups["dp"] == 8
    nd = 8 if spread else 1
    rows, width = tokens.shape
    unit = width + 1
    piece = unit // nd
    as_row = lambda v: v.astype(F32)[None]

    w = jnp.transpose(qkv_weight, (1, 2, 0)).reshape(9 * HEAD, width)
    b = pair_rows(jnp.concatenate([qv_bias[0], jnp.zeros_like(qv_bias[0]), qv_bias[1]]).astype(F32), 0)[None]
    wide_row = lambda v: jnp.pad(as_row(v), ((0, 0), (0, 1)))
    if spread:
        full = [tokens] * 3
    else:
        wide = lambda v, tall=0: jnp.pad(v, ((0, tall), (0, unit - v.shape[1])))
        own = [wide(out_weight, 64), jnp.concatenate([up_weight, up_bias[None], wide(down_weight)]), wide(pair_rows(w, 0))]
        full = [lax.all_gather(v, "tensor", axis=0, tiled=False)[None] for v in own]
    mixed, token_grad, _, up_sum, down_sum, rest_sum, wg_sum, _, _, _, wg = layer(
        seq_length, live_rows, tokens, cotangent, w, b, up_weight, down_weight, out_weight, as_row(up_bias),
        wide_row(out_bias), wide_row(down_bias), *full, parts, spread,
    )
    if spread:
        up_sum, down_sum, rest_sum = up_sum.reshape(unit, unit), down_sum.reshape(unit, unit), rest_sum.reshape(256, unit)
        wg = wg_sum.reshape(640, unit)[: 9 * HEAD].astype(F32)
    else:
        mine = lax.psum_scatter(up_sum[0].astype(F32), "tensor", scatter_dimension=0, tiled=False)
        mine, wg = lax.psum((mine, wg), "dp")
        up_sum, down_sum, rest_sum = mine[:unit], mine[unit : 2 * unit], mine[2 * unit :]
        wg = jnp.concatenate([wg[(2 * k if k < 3 else 2 * k - 5 if k < 6 else k) * HEAD :][:HEAD] for k in range(9)])
    up_grad = up_sum.astype(F32)
    down_grad = down_sum[:, :width].astype(F32)
    rest = rest_sum.astype(F32)
    biases = wg[:, width].reshape(3, 3 * HEAD)
    return (
        mixed,
        token_grad,
        jnp.transpose(wg[:, :width].reshape(3, 3 * HEAD, width), (2, 0, 1)),
        jnp.stack([biases[0], biases[2]]),
        rest[: 3 * HEAD, :width],
        rest[3 * HEAD, :width],
        up_grad[:width],
        up_grad[width],
        down_grad,
        rest[3 * HEAD + 1, :width],
    )


def solution(mesh):
    placed = (
        P(BOTH, None),
        P(BOTH, None),
        P("dp"),
        P("dp"),
        P(None, None, "tensor"),
        P(None, "tensor"),
        P("tensor", None),
        P(),
        P(None, "tensor"),
        P("tensor"),
        P("tensor", None),
        P(),
    )
    return jax.shard_map(
        partial(local, dict(mesh.shape)),
        mesh=mesh,
        in_specs=placed,
        out_specs=(
            P(BOTH, None),
            P(BOTH, None),
            P(None, None, "tensor"),
            P(None, "tensor"),
            P("tensor", None),
            P(),
            P(None, "tensor"),
            P("tensor"),
            P("tensor", None),
            P(),
        ),
        check_vma=False,
    )
```

```python
from functools import partial

import jax
import jax.numpy as jnp
from jax import lax
from jax.experimental import pallas as pl
from jax.experimental.pallas import tpu as pltpu
from jax.sharding import PartitionSpec as P

HEAD = 64
LANES = 128
EPSILON = 1e-05
HIDE = -1e30
BF = jnp.bfloat16
F32 = jnp.float32
BOTH = ("dp", "tensor")
VMEM = pl.BlockSpec(memory_space=pltpu.VMEM)
SMEM = pl.BlockSpec(memory_space=pltpu.SMEM)
ANY = pl.BlockSpec(memory_space=pl.ANY)
LIMIT = 63 * 1024 * 1024
EARLY = 2


def nn(a, b):
    return lax.dot_general(a, b, (((1,), (0,)), ((), ())), preferred_element_type=F32)


def nt(a, b):
    return lax.dot_general(a, b, (((1,), (1,)), ((), ())), preferred_element_type=F32)


def tn(a, b):
    return lax.dot_general(a, b, (((0,), (0,)), ((), ())), preferred_element_type=F32)


def lane_ids(rows):
    return lax.broadcasted_iota(jnp.int32, (rows, LANES), 1)


def half_turn(x):
    return pltpu.roll(x, HEAD, 1)


def fold(x):
    half = x.shape[0] // 2
    return jnp.where(lane_ids(half) < HEAD, x[:half], half_turn(x[half:]))


def unfold(x):
    low = lane_ids(x.shape[0]) < HEAD
    zero = jnp.zeros_like(x)
    return jnp.concatenate(
        [jnp.where(low, x, zero), jnp.where(low, half_turn(x), zero)], axis=0
    )


def split3(x):
    high = x.astype(BF).astype(F32)
    rest = x - high
    mid = rest.astype(BF).astype(F32)
    return high, mid, rest - mid


def norm_stats(x, width):
    s1 = jnp.sum(x, axis=-1, keepdims=True)
    s2 = jnp.sum(x * x, axis=-1, keepdims=True)
    return s1, lax.rsqrt((s2 + s1 * s1) / width + EPSILON)


def norm_pull(x, s1, r, g, width):
    dot = jnp.sum(g * x, axis=-1, keepdims=True)
    return g * r - (r * r * r * dot / width) * (x + s1)


def widen(ref, scratch):
    rows, width = ref.shape
    wide = scratch.shape[1]
    scratch[:, wide - LANES :] = jnp.zeros((rows, LANES), F32)
    scratch[:, :width] = ref[...].astype(F32)


def diag_mask(first, rows, live, turned):
    q_dim, k_dim = (1, 0) if turned else (0, 1)
    q = lax.broadcasted_iota(jnp.int32, (rows, rows), q_dim)
    k = lax.broadcasted_iota(jnp.int32, (rows, rows), k_dim)
    seen = (k <= q) & ((k + first < live) | (k == q))
    return jnp.where(seen, 0.0, HIDE).astype(F32)


def at_rows(i, rows):
    return pl.ds(pl.multiple_of(i * rows, rows), rows)


def fill_rows(dst, src, first, rows, width):
    wide = dst.shape[1]
    dst[first : first + rows, wide - LANES :] = jnp.zeros((rows, LANES), dst.dtype)
    dst[first : first + rows, :width] = src


class Sends:
    def __init__(self):
        self.ends = []

    def start(self, copy, when=None):
        if when is None:
            copy().start()
        else:
            pl.when(when())(lambda: copy().start())
        self.ends.append((copy, when))

    def finish(self):
        for copy, when in self.ends:
            if when is None:
                copy().wait_send()
            else:
                pl.when(when())(lambda copy=copy: copy().wait_send())


def remote(src, dst, ssem, rsem, **where):
    return pltpu.make_async_remote_copy(
        src_ref=src,
        dst_ref=dst,
        send_sem=ssem,
        recv_sem=rsem,
        device_id=where,
        device_id_type=pl.DeviceIdType.MESH,
    )


def neighbours(d):
    core, x, y = d % 2, (d // 2) % 2, d // 4
    return d + 1 - 2 * core, d + 2 - 4 * x, d + 4 - 8 * y


def greet(d, t, parts, spread, corner=False):
    barrier = pltpu.get_barrier_semaphore()

    def signal(**where):
        pl.semaphore_signal(barrier, inc=1, device_id=where, device_id_type=pl.DeviceIdType.MESH)

    for k in range(1, parts):
        signal(tensor=lax.rem(t + k, parts))
    if spread:
        core_n, x_n, y_n = neighbours(d)
        for n in (core_n, x_n, y_n) + ((x_n + y_n - d,) if corner else ()):
            signal(dp=n)
    return lambda: pl.semaphore_wait(barrier, parts - 1 + (3 + corner) * spread)


class Spread:
    def __init__(self, d, t, parts, piece, full, zsem, xsem, csem, sends, times):
        self.d, self.t, self.parts, self.piece, self.full, self.times = d, t, parts, piece, full, times
        self.zsem, self.xsem, self.csem, self.sends = zsem, xsem, csem, sends
        self.core_n, self.x_n, self.y_n = neighbours(d)
        self.diag = self.x_n + self.y_n - d

    def slot(self, e, b):
        return self.full.at[e, b]

    def out(self, to, ok):
        self.sends.start(
            lambda: remote(self.piece, self.slot(self.d, self.t), self.zsem.at[0, to], self.zsem.at[1, self.t], tensor=to), ok
        )

    def plane(self, b, first, ok):
        d, xs = self.d, self.xsem
        src = lambda: self.piece if first else self.slot(d, b)
        self.sends.start(lambda: remote(src(), self.slot(d, b), xs.at[0, b], xs.at[1, b], dp=self.x_n), ok)
        self.sends.start(lambda: remote(src(), self.slot(d, b), xs.at[2, b], xs.at[3, b], dp=self.y_n), ok)
        self.sends.start(
            lambda: remote(src(), self.slot(d, b), self.csem.at[0, b], self.csem.at[4, b], dp=self.core_n), ok
        )

    def arrive(self, b, ok):
        def wait():
            remote(self.slot(self.d, b), self.slot(self.d, b), self.zsem.at[0, b], self.zsem.at[1, b], tensor=b).wait_recv()

        pl.when(ok())(wait)
        self.plane(b, False, ok)

    def across(self, b, ok):
        xs, cs = self.xsem, self.csem
        east = lambda: self.slot(self.x_n, b)
        north = lambda: self.slot(self.y_n, b)

        def wait():
            remote(east(), east(), xs.at[0, b], xs.at[1, b], dp=self.x_n).wait_recv()
            remote(north(), north(), xs.at[2, b], xs.at[3, b], dp=self.y_n).wait_recv()

        pl.when(ok())(wait)
        self.sends.start(
            lambda: remote(east(), east(), xs.at[4, b], xs.at[5, b], dp=self.y_n), lambda: ok() & (b % 2 == 0)
        )
        self.sends.start(
            lambda: remote(north(), north(), xs.at[4, b], xs.at[5, b], dp=self.x_n), lambda: ok() & (b % 2 == 1)
        )
        self.sends.start(lambda: remote(east(), east(), cs.at[1, b], cs.at[5, b], dp=self.core_n), ok)
        self.sends.start(lambda: remote(north(), north(), cs.at[2, b], cs.at[6, b], dp=self.core_n), ok)

    def corner(self, b, ok):
        far, xs, cs = (lambda: self.slot(self.diag, b)), self.xsem, self.csem
        pl.when(ok())(lambda: remote(far(), far(), xs.at[4, b], xs.at[5, b], dp=self.x_n).wait_recv())
        self.sends.start(lambda: remote(far(), far(), cs.at[3, b], cs.at[7, b], dp=self.core_n), ok)

    def at(self, point):
        own = lambda: self.t >= 0
        for job in ("out", "plane", "arrive", "across", "corner"):
            for (k, m), when in self.times[job].items():
                if when != point:
                    continue
                if k == m:
                    self.plane(self.t, True, own) if job == "plane" else getattr(self, job)(self.t, own)
                    continue
                for mirror in (False, True):
                    here, there = (self.parts - 1 - k, self.parts - 1 - m) if mirror else (k, m)
                    getattr(self, job)(there, lambda here=here: self.t == here)

    def ready(self, b):
        shift = self.core_n - self.d
        for k, e in enumerate((self.d, self.x_n, self.y_n, self.diag)):
            there = self.slot(e + shift, b)
            remote(there, there, self.csem.at[k, b], self.csem.at[4 + k, b], dp=self.core_n).wait_recv()


PAIRS = [(k, m) for k in range(4) for m in range(k)]
REST_TIMES = {
    "out": {(m, k): "p1" for k, m in PAIRS},
    "plane": {(0, 0): "p0"},
    "arrive": {pair: "p3" for pair in PAIRS},
    "across": {(0, 0): "p1", **{pair: "h0" for pair in PAIRS}},
    "corner": {(0, 0): "p2", **{pair: "h1" for pair in PAIRS}},
}
MAIN_TIMES = {
    "out": {(2, 3): "p0", (0, 1): "p1", (1, 2): "p2", (0, 2): "p2", (1, 3): "h2", (0, 3): "p3"},
    "plane": {(0, 0): "p0"},
    "arrive": {(3, 2): "p1", (1, 0): "p2", (2, 1): "h1", (2, 0): "h1", (3, 1): "h1", (3, 0): "h2"},
    "across": {(0, 0): "p1", (3, 2): "p3", (1, 0): "h0", (2, 0): "h2", (2, 1): "e", (3, 1): "e", (3, 0): "q0"},
    "corner": {(0, 0): "p2", (3, 2): "h0", (1, 0): "h1", (2, 0): "e", (3, 1): "q0", (2, 1): "q1", (3, 0): "q1"},
}
LATE_TIMES = {
    "out": {(m, k): "e" for k, m in PAIRS},
    "plane": {(0, 0): "p0"},
    "arrive": {pair: "q0" for pair in PAIRS},
    "across": {(0, 0): "p1", **{pair: "q1" for pair in PAIRS}},
    "corner": {(0, 0): "p2", **{pair: "q2" for pair in PAIRS}},
}
SENT = (4, 2, 3)
SERVE = {(0, 0): ((), (0,)), (0, 1): ((), (1,)), (1, 1): ((), (4, 2)), (2, 2): ((), (3,))}


def owner_order(d):
    return 4 * (d % 2) + d // 2


def layer_kernel(
    spread, seq_ref, live_ref, tok_ref, cot_any, w_any, bias_ref, up_any, down_any, ow_any, rest_in, main_in, late_in,
    mixed_ref, out_ref, o_any, fin_any, fin_down, fin_rest, fin_wg, rest_out, main_out, late_out, r1_any,
    n1_ref, wq, piece, qx_ref, kx_ref, vx_ref, pack_ref, heads_in, hg_in, recv_ref, hid_ref, gbuf, r2, r3, fst, w1, w2,
    nsem, hsem, gsem, qsem, own_sem, lsem, wsem, s1, s2, s3, s4, s5, u1, u2, *gsems,
):
    rows, width = tok_ref.shape
    unit = n1_ref.shape[1]
    blocks = parts = heads_in.shape[0]
    nd = 8 if spread else 1
    share, tail, qrow = unit // nd, 256 // nd, 640 // nd
    d, t = lax.axis_index("dp"), lax.axis_index("tensor")
    core = d % 2
    barrier = greet(d, t, parts, spread, True)
    sends, heads_sends = Sends(), Sends()
    seq, live = seq_ref[0], live_ref[0]
    lane = lane_ids(rows)
    low = lane < HEAD
    row = lax.broadcasted_iota(jnp.int32, (rows, LANES), 0)
    spare = lax.broadcasted_iota(jnp.int32, (rows, unit), 1) == width
    rest_full, main_full, late_full = (rest_out, main_out, late_out) if spread else (rest_in, main_in, late_in)
    gathers = []
    if spread:
        main_piece, rest_piece = piece.at[pl.ds(0, 2 * share)], piece.at[pl.ds(2 * share, tail)]
        late_piece = piece.at[pl.ds(2 * share + tail, qrow)]
        for k, (own, full, times) in enumerate(
            ((rest_piece, rest_out, REST_TIMES), (main_piece, main_out, MAIN_TIMES), (late_piece, late_out, LATE_TIMES))
        ):
            gathers.append(Spread(d, t, parts, own, full, *gsems[3 * k : 3 * k + 3], sends, times))

    def point(name):
        for gather in gathers:
            gather.at(name)

    def when_point(cond, name):
        if spread:
            pl.when(cond)(lambda: point(name))

    def turn(k):
        a, b = (t + k - 2 * (t % 2) * (k % 2)) % 2, t // 2 + k // 2 - 2 * (t // 2) * (k // 2)
        return a + 2 * b

    def prologue(wide, w_sc, up_sc, down_sc, ow_sc):
        loads = [
            pltpu.make_async_copy(src, dst, lsem.at[k])
            for k, (src, dst) in enumerate(((w_any, w_sc), (up_any, up_sc), (down_any, down_sc), (ow_any, ow_sc)))
        ]
        for load in loads if spread else loads[:1]:
            load.start()
        widen(tok_ref, wide)
        x = wide[...]
        _, r = norm_stats(x, width + 1)
        n1_ref[at_rows(t, rows), :] = jnp.where(spare, 1.0, x * r).astype(BF)
        barrier()
        for up in (True, False):
            sends.start(lambda up=up: line(t, up), lambda up=up: edge(up))
        loads[0].wait()
        for k in range(9):
            take = 3 * (k % 2) + k // 2 if k < 6 else k
            fill_rows(wq, w_sc[take * HEAD : (take + 1) * HEAD, :], k * HEAD, HEAD, width)
        wq[9 * HEAD : 10 * HEAD, :] = jnp.zeros((HEAD, unit), BF)
        if not spread:
            return
        near = share - 16
        piece[:, unit - LANES :] = jnp.zeros((piece.shape[0], LANES), BF)
        for load in loads[1:]:
            load.wait()
        piece[:near, :] = up_sc[pl.ds(pl.multiple_of(d * share, 16), near), :]

        @pl.when(d < nd - 1)
        def _():
            piece[near:share, :] = up_sc[pl.ds(pl.multiple_of(d * share + near, 16), 16), :]

        @pl.when(d == nd - 1)
        def _():
            last = jnp.concatenate([up_sc[width - 15 :, :].astype(F32), bias_ref[1:2, :]], axis=0)
            piece[near:share, :] = last.astype(BF)

        piece[share : 2 * share, :width] = down_sc[pl.ds(pl.multiple_of(d * share, 16), share), :]

        @pl.when(d < 6)
        def _():
            piece[2 * share : 2 * share + tail, :width] = ow_sc[pl.ds(pl.multiple_of(d * tail, 16), tail), :]

        @pl.when(d >= 6)
        def _():
            piece[2 * share : 2 * share + tail, :] = jnp.zeros((tail, unit), BF)

        piece[2 * share + tail :, :] = wq[pl.ds(pl.multiple_of(d * qrow, 16), qrow), :]

    def line(b, up):
        block = n1_ref.at[at_rows(b, rows), :]
        return remote(block, block, nsem.at[1 if up else 2, b], nsem.at[0, b], tensor=t + 1 if up else t - 1)

    def edge(up):
        return t < parts - 1 if up else t > 0

    def place(s, up):
        b = t - s if up else t + s
        return b, (lambda: t - s >= 0) if up else (lambda: t + s < parts)

    places = {(s, up): place(s, up) for s in range(1, parts) for up in (True, False)}
    pl.run_scoped(
        prologue,
        pltpu.VMEM((rows, unit), F32),
        pltpu.VMEM(w_any.shape, BF),
        pltpu.VMEM(up_any.shape, BF),
        pltpu.VMEM(down_any.shape, BF),
        pltpu.VMEM(ow_any.shape, BF),
    )
    homes = []
    if spread:
        for k, gather in enumerate(gathers):
            homes.append(pltpu.make_async_copy(gather.piece, gather.slot(d, t), own_sem.at[k]))
            homes[-1].start()
        point("p0")

    def attend(o_ref, mask_ref, s_ref):
        def project(i):
            at = at_rows(i, rows)
            qkv = nt(n1_ref[at, :], wq[: 10 * HEAD, :]) + bias_ref[:1, : 10 * HEAD]
            qkv = qkv.astype(BF).astype(F32)
            key = row + i * rows
            m = lane - HEAD
            same = ((m * rows) ^ (i * rows)) < seq
            open_ = (m == i) | (same & (key < live))
            bias = jnp.where(m < blocks, jnp.where(open_, 0.0, HIDE), jnp.where(m < blocks + 3, 1.0, 0.0))
            hot = jnp.where(m == i, 1.0, 0.0)
            ones = jnp.where(m < 3, 1.0, 0.0)
            for h in range(3):
                pair = qkv[:, h * LANES : (h + 1) * LANES]
                qx_ref[h, at, :] = jnp.where(low, pair * HEAD**-0.5, hot).astype(BF)
                kx_ref[h, at, :] = jnp.where(low, half_turn(pair), bias).astype(BF)
                val = qkv[:, (3 + h // 2) * LANES : (4 + h // 2) * LANES]
                vx_ref[h, at, :] = jnp.where(low, half_turn(val) if h % 2 else val, ones).astype(BF)
            mask_ref[i] = diag_mask(i * rows, rows, live, False).astype(BF)

        for s in range(parts):
            if s:
                for up in (True, False):
                    b, ok = places[s, up]
                    pl.when(ok())(lambda b=b, up=up: line(b, up).wait_recv())
                    sends.start(lambda b=b, up=up: line(b, up), lambda ok=ok, up=up: ok() & edge(up))
                point(f"p{s}")

            def arrived(e, carry, s=s):
                b = t + (2 * e - 1) * s
                pl.when((b >= 0) & (b < parts))(lambda: project(b))
                return carry

            lax.fori_loop(0, 2 if s else 1, arrived, 0)

        def head(h, carry):
            for i in range(blocks):
                q = qx_ref[h, i * rows : (i + 1) * rows, :]
                top = None
                for j in range(i, -1, -1):
                    s = nt(q, kx_ref[h, j * rows : (j + 1) * rows, :])
                    if i == j:
                        s = s + mask_ref[i].astype(F32)
                    peak = jnp.max(s, axis=-1, keepdims=True)
                    top = peak if top is None else jnp.maximum(top, peak)
                    s_ref[j] = s
                acc = None
                for j in range(i + 1):
                    p = jnp.exp(s_ref[j] - top).astype(BF)
                    part = nn(p, vx_ref[h, j * rows : (j + 1) * rows, :])
                    acc = part if acc is None else acc + part
                mass = acc[:, HEAD : HEAD + 1]
                lse = top + jnp.log(mass)
                o_ref[h, i * rows : (i + 1) * rows, :] = acc / mass
                hi, mid, lo = split3(-lse)
                ext = jnp.where(
                    lane == HEAD + blocks,
                    hi,
                    jnp.where(lane == HEAD + blocks + 1, mid, jnp.where(lane == HEAD + blocks + 2, lo, q.astype(F32))),
                )
                qx_ref[h, i * rows : (i + 1) * rows, :] = ext.astype(BF)
            for k in range(3):
                when_point(h == k, f"h{k}")
            return carry

        lax.fori_loop(0, 3, head, 0)
        keep = pltpu.make_async_copy(o_ref, o_any, lsem.at[0])
        keep.start()

        def pack(i, carry):
            at = at_rows(i, rows)
            pack_ref[i, :rows, :] = jnp.where(low, o_ref[0, at, :], half_turn(o_ref[1, at, :])).astype(BF)
            pack_ref[i, rows:, :] = fold(o_ref[2, at, :]).astype(BF)
            return carry

        lax.fori_loop(0, blocks, pack, 0)
        swap_start(pack_ref, heads_in, hsem, heads_sends)
        point("e")
        keep.wait()

    def swap(src_ref, dst_ref, sems, k, taking):
        to = lax.rem(t + (parts - k if taking else k), parts)
        src, dst = (to, to) if taking else (to, t)
        return remote(src_ref.at[src], dst_ref.at[dst], sems.at[0, k], sems.at[1, k], tensor=to)

    def swap_home(src_ref, dst_ref, sems):
        return pltpu.make_async_copy(src_ref.at[t], dst_ref.at[t], sems.at[0, 0])

    def swap_start(src_ref, dst_ref, sems, sends):
        for k in (2, 1, 3):
            sends.start(lambda k=k: swap(src_ref, dst_ref, sems, k, False))
        swap_home(src_ref, dst_ref, sems).start()

    def swap_end(src_ref, dst_ref, sems):
        for k in range(1, parts):
            swap(src_ref, dst_ref, sems, k, True).wait_recv()
        swap_home(src_ref, dst_ref, sems).wait()

    pl.run_scoped(
        attend,
        pltpu.VMEM((3, rows * parts, LANES), F32),
        pltpu.VMEM((parts, rows, rows), BF),
        pltpu.VMEM((parts, rows, rows), F32),
    )

    core_n, x_n, y_n = neighbours(d)
    chips = (x_n, y_n, x_n + y_n - d)
    main_rows, rest_rows = pl.ds(0, 2 * share), pl.ds(2 * share, tail)
    half = gbuf.at[core] if spread else gbuf
    every = pl.ds(0, parts)

    def region(k):
        if isinstance(k, int) and k == parts:
            return every, rest_rows
        return turn(k), main_rows

    def to_core(k):
        which, at = region(k)
        return remote(gbuf.at[1 - core, :, which, at], r1_any.at[:, which, at], s1.at[0, k], s1.at[1, k], dp=core_n)

    def second(c, k):
        which, at = region(k)
        return remote(
            gbuf.at[core, chips[c] // 2, which, at], r2.at[c, which, at], s2.at[0, c, k], s2.at[1, c, k], dp=chips[c]
        )

    def add_core(k, stage, stage_rest):
        to_core(k).wait_recv()
        which, at = region(k)
        here = stage_rest if isinstance(k, int) and k == parts else stage
        load = pltpu.make_async_copy(r1_any.at[:, which, at], here, lsem.at[0])
        load.start()
        load.wait()
        for q in range(4):
            gbuf[core, q, which, at] = (gbuf[core, q, which, at].astype(F32) + here[q].astype(F32)).astype(BF)

    def third(k, m):
        b, at = turn(k), (main_rows, rest_rows)[m]
        return remote(gbuf.at[core, d // 2, b, at], r3.at[t, at], s3.at[0, m, b], s3.at[1, m, t], tensor=b)

    def send_second(k):
        for c in range(3):
            sends.start(lambda c=c: second(c, k))

    def sum_second(k):
        for c in range(3):
            second(c, k).wait_recv()
        which, at = region(k)
        total = gbuf[core, d // 2, which, at].astype(F32)
        for c in range(3):
            total = total + r2[c, which, at].astype(F32)
        gbuf[core, d // 2, which, at] = total.astype(BF)
        if k == parts:
            for j in range(1, parts):
                sends.start(lambda j=j: third(j, 1))
        elif k:
            sends.start(lambda: third(k, 0))

    def middle(wu, wd, wm, acts, ugs, xall, n2_ref, gb_ref, wide, dn_ref, stage):
        stage_rest = wm.at[pl.ds(0, 4)] if spread else None
        wo = wq

        def fetch(k, slot):
            return [
                pltpu.make_async_copy(main_full.at[:, turn(k), pl.ds(m * share, share), :], dst.at[slot], wsem.at[m, slot])
                for m, dst in enumerate((wu, wd))
            ]

        def fetch_start(k, slot):
            if spread:
                gathers[1].ready(turn(k))
            for copy in fetch(k, slot):
                copy.start()

        cot_load = pltpu.make_async_copy(cot_any, mixed_ref, lsem.at[1])
        cot_load.start()
        if spread:
            for home in homes[:2]:
                home.wait()
            for b in range(parts):
                gathers[0].ready(b)
        rest_load = pltpu.make_async_copy(rest_full, wm, lsem.at[0])
        rest_load.start()
        fetch_start(0, 0)
        cot_load.wait()
        widen(mixed_ref, wide)
        gb_ref[...] = wide[...].astype(BF)
        widen(tok_ref, wide)
        rest_load.wait()
        for b in range(parts):
            own = wm[:, b].reshape(tail * nd, unit)
            wo[b * LANES : (b + 1) * LANES, :] = own[:LANES]
            wo[parts * LANES + b * HEAD : parts * LANES + (b + 1) * HEAD, :] = own[LANES : LANES + HEAD]
        swap_end(pack_ref, heads_in, hsem)
        lows = []
        for b in range(parts):
            xall[:, b * LANES : (b + 1) * LANES] = heads_in[b, :rows, :]
            lows.append(unfold(heads_in[b, rows:, :].astype(F32)))
        for k in range(parts // 2):
            both = jnp.where(low, lows[2 * k], half_turn(lows[2 * k + 1]))
            xall[:, (parts + k) * LANES : (parts + k + 1) * LANES] = both.astype(BF)
        point("q0")
        hidden = wide[...] + nn(xall[...], wo[...]) + bias_ref[2:3, :]
        s1_, r = norm_stats(hidden, width + 1)
        n2_ref[...] = jnp.where(spare, 1.0, hidden * r).astype(BF)
        hid_ref[...] = hidden
        wide[...] = hidden + bias_ref[3:4, :]
        dn_ref[...] = jnp.zeros_like(dn_ref)
        root = (2 / jnp.pi) ** 0.5

        def store_grads(k, act, ug):
            b = turn(k)
            up_g = tn(n2_ref[...], ug).astype(BF)
            down_g = tn(act, gb_ref[...]).astype(BF)
            if spread:
                gbuf[:, :, b, :share, :] = up_g.reshape(2, 4, share, unit)
                gbuf[:, :, b, share : 2 * share, :] = down_g.reshape(2, 4, share, unit)
                to_core(k).start()
            else:
                gbuf[0, b, :share, :] = up_g
                gbuf[0, b, share : 2 * share, :] = down_g

        def unit_block(k, carry):
            slot = k % 2
            for copy in fetch(k, slot):
                copy.wait()
            up = wu[slot].reshape(unit, unit)
            down = wd[slot].reshape(unit, unit)

            def some_rows(i, carry):
                at = at_rows(i, rows // 2)
                u = nn(n2_ref[at, :], up)
                th = jnp.tanh(root * (u + 0.044715 * (u * u * u)))
                act = (0.5 * u * (1 + th)).astype(BF)
                slope = 0.5 * (1 + th) + (0.5 * u) * (1 - th * th) * (root * (1 + 0.134145 * (u * u)))
                acts[slot, at, :] = act
                wide[at, :] += nn(act, down)
                ug = (nt(gb_ref[at, :], down) * slope).astype(BF)
                ugs[slot, at, :] = ug
                dn_ref[at, :] += nt(ug, up)
                return carry

            lax.fori_loop(0, 2, some_rows, 0)
            pl.when(k < parts - 1)(lambda: fetch_start(k + 1, (k + 1) % 2))
            pl.when(k < EARLY)(lambda: store_grads(k, acts[slot], ugs[slot]))

            if spread:
                for m in range(1, EARLY + 1):
                    pl.when(k == m)(lambda m=m: add_core(m - 1, stage, stage_rest))
                pl.when(k == 1)(lambda: send_second(0))
                pl.when(k == 3)(lambda: send_second(1))
            for m in range(parts):
                when_point(k == m, f"q{m + 1}")
            return carry

        lax.fori_loop(0, parts, unit_block, 0)
        hidden = hid_ref[...]
        gout = gb_ref[...].astype(F32)
        hidgrad = gout + norm_pull(hidden, s1_, r, dn_ref[...], width + 1)
        ag = hidgrad.astype(BF)
        hg = nt(ag, wo[...])
        heads_sends.finish()
        for b in range(parts):
            pack_ref[b, :rows, :] = hg[:, b * LANES : (b + 1) * LANES].astype(BF)
            pair = hg[:, (parts + b // 2) * LANES : (parts + b // 2 + 1) * LANES]
            pack_ref[b, rows:, :] = fold(half_turn(pair) if b % 2 else pair).astype(BF)
        swap_start(pack_ref, hg_in, gsem, sends)
        point("g")
        mixed_ref[...] = wide[:, :width].astype(BF)
        hid_ref[...] = hidgrad
        out_bias_grad = jnp.sum(hidgrad, axis=0, keepdims=True)
        down_bias_grad = jnp.sum(gout, axis=0, keepdims=True)
        wide[...] = tn(xall[:, : parts * LANES], ag)
        dn_ref[: parts * HEAD, :] = tn(xall[:, parts * LANES :], ag)
        extra = lax.broadcasted_iota(jnp.int32, (HEAD, unit), 0)
        extra = jnp.where(extra == 0, out_bias_grad, jnp.where(extra == 1, down_bias_grad, 0.0))
        for b in range(parts):
            pair = wide[b * LANES : (b + 1) * LANES, :]
            low_part = dn_ref[b * HEAD : (b + 1) * HEAD, :]
            misc = jnp.concatenate([pair, low_part, extra], axis=0).astype(BF)
            if spread:
                gbuf[:, :, b, 2 * share :, :] = misc.reshape(2, 4, tail, unit)
            else:
                gbuf[0, b, 2 * share :, :] = misc
        if spread:
            to_core(parts).start()

        def late(k, carry):
            store_grads(k, acts[k % 2], ugs[k % 2])
            return carry

        lax.fori_loop(EARLY, parts, late, 0)
        if spread:
            for k in [parts] + list(range(EARLY, parts)):
                add_core(k, stage, stage_rest)
            for k in SENT:
                send_second(k)
        else:
            out = pltpu.make_async_copy(gbuf, fin_any, lsem.at[0])
            out.start()
            out.wait()

    square, low_square = pltpu.VMEM((rows, unit), F32), pltpu.VMEM((rows, unit), BF)
    pl.run_scoped(
        middle,
        pltpu.VMEM((2, nd, share, unit), BF),
        pltpu.VMEM((2, nd, share, unit), BF),
        pltpu.VMEM((nd, parts, tail, unit), BF),
        pltpu.VMEM((parts - EARLY, rows, unit), BF),
        pltpu.VMEM((parts - EARLY, rows, unit), BF),
        low_square,
        low_square,
        low_square,
        square,
        square,
        pltpu.VMEM((4, 2 * share, unit) if spread else (16, LANES), BF),
    )

    def back(gpack, wgb, dox, dvs, dqt, dk_ref, mask_ref, xt, wg_acc, wmq, dn_ref):
        local = Sends()
        wide = wg_acc.at[pl.ds(0, rows)]

        def o_load(i):
            return pltpu.make_async_copy(o_any.at[:, pl.ds(i * rows, rows), :], dk_ref.at[pl.ds(0, 3)], lsem.at[0])

        def w_load(k):
            return pltpu.make_async_copy(late_full.at[:, k], wmq.at[k], wsem.at[0, k])

        def swap_grads(k, p, taking):
            to = lax.rem(t + (parts - k if taking else k), parts)
            src, dst = (to, to) if taking else (to, t)
            at = pl.ds(p * rows, rows if p < 4 else rows // 2)
            return remote(gpack.at[src].at[at], recv_ref.at[dst].at[at], qsem.at[0, k, p], qsem.at[1, k, p], tensor=to)

        def send_grads(p):
            for k in (2, 1, 3):
                local.start(lambda k=k: swap_grads(k, p, False))

        o_load(0).start()

        def masks(i, carry):
            mask_ref[i] = diag_mask(i * rows, rows, live, True).astype(BF)
            return carry

        lax.fori_loop(0, blocks, masks, 0)
        swap_end(pack_ref, hg_in, gsem)
        for i in range(blocks):
            o_load(i).wait()
            pair = hg_in[i, :rows, :].astype(F32)
            last = unfold(hg_in[i, rows:, :].astype(F32))
            for h, g in enumerate((pair, half_turn(pair), last)):
                g = jnp.where(low, g, 0.0)
                hi, mid, lo = split3(-jnp.sum(g * dk_ref[h], axis=-1, keepdims=True))
                g = jnp.where(lane == HEAD, hi, jnp.where(lane == HEAD + 1, mid, jnp.where(lane == HEAD + 2, lo, g)))
                dox[h, i * rows : (i + 1) * rows, :] = g.astype(BF)
            if i + 1 < blocks:
                o_load(i + 1).start()
        if spread:
            homes[2].wait()
            for k in range(parts):
                gathers[2].ready(k)
        for k in range(parts):
            w_load(k).start()

        def head(h, carry):
            spot = lax.rem(h, 2)
            for j in range(blocks):
                keys = kx_ref[h, j * rows : (j + 1) * rows, :]
                keys_t = jnp.transpose(keys.astype(F32)).astype(BF)
                vals = vx_ref[h, j * rows : (j + 1) * rows, :]
                dk = dv = None
                for i in range(j, blocks):
                    q = qx_ref[h, i * rows : (i + 1) * rows, :]
                    do = dox[h, i * rows : (i + 1) * rows, :]
                    s = nt(keys, q)
                    if i == j:
                        s = s + mask_ref[i].astype(F32)
                    p = jnp.exp(s)
                    ds = (p * nt(vals, do)).astype(BF)
                    dv_part = nn(p.astype(BF), do)
                    dk_part = nn(ds, q)
                    dq_part = nn(keys_t, ds)
                    dk = dk_part if dk is None else dk + dk_part
                    dv = dv_part if dv is None else dv + dv_part
                    if j == 0:
                        dqt[i] = dq_part
                    else:
                        dqt[i] += dq_part
                dk_ref[j] = dk
                dvs[spot, j * rows : (j + 1) * rows, :] = dv.astype(BF)
                if spread:
                    for step, (sent, summed) in SERVE.items():
                        if step[1] == j:

                            @pl.when(h == step[0])
                            def _(sent=sent, summed=summed):
                                for k in sent:
                                    send_second(k)
                                for k in summed:
                                    sum_second(k)

            at = pl.ds(pl.multiple_of(h * rows, rows), rows)
            for i in range(blocks):
                dq = jnp.transpose(dqt[i]) * HEAD**-0.5
                gpack[i, at, :] = jnp.where(low, dq, half_turn(dk_ref[i])).astype(BF)
            for p in range(3):
                pl.when(h == p)(lambda p=p: send_grads(p))

            @pl.when(h == 1)
            def _():
                for i in range(blocks):
                    mine = pl.ds(i * rows, rows)
                    gpack[i, 3 * rows : 4 * rows, :] = jnp.where(low, dvs[0, mine, :].astype(F32), half_turn(dvs[1, mine, :].astype(F32))).astype(BF)
                send_grads(3)

            @pl.when(h == 2)
            def _():
                for i in range(blocks):
                    gpack[i, 4 * rows :, :] = fold(dvs[0, i * rows : (i + 1) * rows, :].astype(F32)).astype(BF)
                send_grads(4)

            return carry

        lax.fori_loop(0, 3, head, 0)
        home = pltpu.make_async_copy(gpack.at[t], recv_ref.at[t], qsem.at[0, 0, 0])
        home.start()

        def spread_lanes(ref, i):
            for k in range(4):
                xt[:, k * LANES : (k + 1) * LANES] = ref[i, k * rows : (k + 1) * rows, :]
            xt[:, 4 * LANES :] = unfold(ref[i, 4 * rows :, :].astype(F32)).astype(BF)

        wg_acc[...] = jnp.zeros_like(wg_acc)

        def weigh(i, carry):
            spread_lanes(gpack, i)
            wg_acc[...] += tn(xt[...], n1_ref[at_rows(i, rows), :])
            return carry

        lax.fori_loop(0, blocks, weigh, 0)
        tall = 2 * share + tail
        if spread:
            order = [2 * k if k < 3 else 2 * k - 5 if k < 6 else k for k in range(10)]
            natural = jnp.concatenate([wg_acc[k * HEAD : (k + 1) * HEAD, :] for k in order], axis=0)
            wgb[...] = natural.astype(BF).reshape(2, 4, qrow, unit)

            def w_first():
                return remote(wgb.at[1 - core], w1, u1.at[0], u1.at[1], dp=core_n)

            def w_second(c):
                return remote(wgb.at[core, chips[c] // 2], w2.at[c], u2.at[0, c], u2.at[1, c], dp=chips[c])

            local.start(w_first)
            w_first().wait_recv()
            for q in range(4):
                wgb[core, q] = (wgb[core, q].astype(F32) + w1[q].astype(F32)).astype(BF)
            for c in range(3):
                local.start(lambda c=c: w_second(c))
            total = wgb[core, d // 2].astype(F32)
            for c in range(3):
                w_second(c).wait_recv()
                total = total + w2[c].astype(F32)
            fst[tall:, :] = total.astype(BF)
            total = gbuf[core, d // 2, t].astype(F32)
            for k in range(1, parts):
                b = turn(k)
                for m, at in enumerate((main_rows, rest_rows)):
                    there = r3.at[b, at]
                    remote(there, there, s3.at[0, m, b], s3.at[1, m, b], tensor=b).wait_recv()
                total = total + r3[b].astype(F32)
            fst[:tall, :] = total.astype(BF)

            cuts = ((fin_any, 0, share), (fin_down, share, share), (fin_rest, 2 * share, tail), (fin_wg, tall, qrow))

            def piece_of(m, e):
                return cuts[m][0].at[e]

            def sum_of(m):
                return fst.at[pl.ds(cuts[m][1], cuts[m][2])]

            def give(c, m):
                return remote(sum_of(m), piece_of(m, owner_order(d)), s4.at[0, c, m], s4.at[1, c, m], dp=chips[c])

            def came(c, m):
                there = piece_of(m, owner_order(chips[c]))
                return remote(there, there, s4.at[0, c, m], s4.at[1, c, m], dp=chips[c])

            def give_core(c, m):
                there = piece_of(m, owner_order(d if c == 3 else chips[c]))
                return remote(sum_of(m) if c == 3 else there, there, s5.at[0, c, m], s5.at[1, c, m], dp=core_n)

            owns = [
                pltpu.make_async_copy(sum_of(m), piece_of(m, owner_order(d)), lsem.at[m]) for m in range(4)
            ]
            for m in range(4):
                owns[m].start()
                for c in (2, 0, 1):
                    sends.start(lambda c=c, m=m: give(c, m))
                sends.start(lambda m=m: give_core(3, m))
        else:
            out = pltpu.make_async_copy(wg_acc, r1_any, own_sem.at[3])
            out.start()
            out.wait()
        widen(tok_ref, wide)
        dn_ref[...] = jnp.zeros_like(dn_ref)
        home.wait()
        for k in range(1, parts):
            for p in range(5):
                swap_grads(k, p, True).wait_recv()
        for k in range(parts):
            w_load(k).wait()

        def part(b, carry):
            spread_lanes(recv_ref, b)
            dn_ref[...] += nn(xt[...], wmq[b].reshape(nd * qrow, unit))
            return carry

        lax.fori_loop(0, parts, part, 0)
        x = wide[...]
        s1_, r = norm_stats(x, width + 1)
        grad = hid_ref[...] + norm_pull(x, s1_, r, dn_ref[...], width + 1)
        out_ref[...] = grad[:, :width].astype(BF)
        if spread:
            for c in range(3):
                for m in range(4):
                    came(c, m).wait_recv()
                    sends.start(lambda c=c, m=m: give_core(c, m))
            for c in range(4):
                for m in range(4):
                    give_core(c, m).wait_recv()
            for own in owns:
                own.wait()
        local.finish()

    pack = (parts, 4 * rows + rows // 2, LANES)
    pl.run_scoped(
        back,
        pltpu.VMEM(pack, BF),
        pltpu.VMEM((2, 4, qrow, unit) if spread else (16, LANES), BF),
        pltpu.VMEM((3, rows * parts, LANES), BF),
        pltpu.VMEM((2, rows * parts, LANES), BF),
        pltpu.VMEM((parts, LANES, rows), F32),
        pltpu.VMEM((parts, rows, LANES), F32),
        pltpu.VMEM((parts, rows, rows), BF),
        pltpu.VMEM((rows, 5 * LANES), BF),
        pltpu.VMEM((5 * LANES, unit), F32),
        pltpu.VMEM((parts, nd, qrow, unit), BF),
        square,
    )
    if spread:
        for k in range(parts + 1):
            to_core(k).wait_send()
    sends.finish()


def layer(seq, live, tokens, cot, w, biases, up, down, ow, rest, main, late, parts, spread):
    rows, width = tokens.shape
    unit = width + 1
    total = rows * parts
    nd = 8 if spread else 1
    share, tail, qrow = unit // nd, 256 // nd, 640 // nd
    tall = 2 * share + tail
    heads = (parts, rows + rows // 2, LANES)
    dma = lambda *shape: pltpu.SemaphoreType.DMA(shape)
    only = lambda *shape: shape if spread else (1, 1, 16, LANES)
    shape = jax.ShapeDtypeStruct
    vm = lambda *s: pltpu.VMEM(s, BF)
    return pl.pallas_call(
        partial(layer_kernel, spread),
        out_shape=(
            shape((rows, width), BF),
            shape((rows, width), BF),
            shape((3, total, LANES), F32),
            shape((8, share, unit) if spread else (1, parts, tall, unit), BF),
            shape(only(8, share, unit), BF),
            shape(only(8, tail, unit), BF),
            shape(only(8, qrow, unit), BF),
            shape(only(8, parts, tail, unit), BF),
            shape(only(8, parts, 2 * share, unit), BF),
            shape(only(8, parts, qrow, unit), BF),
            shape((4, parts, tall, unit), BF) if spread else shape((640, unit), F32),
        ),
        in_specs=[SMEM, SMEM, VMEM, ANY, ANY, VMEM] + [ANY] * 6,
        out_specs=(VMEM, VMEM) + (ANY,) * 9,
        scratch_shapes=[
            vm(total, unit),
            vm(unit, unit),
            vm(*(tall + qrow, unit) if spread else (16, LANES)),
            vm(3, total, LANES), vm(3, total, LANES), vm(3, total, LANES),
            vm(*heads), vm(*heads), vm(*heads),
            vm(parts, 4 * rows + rows // 2, LANES),
            pltpu.VMEM((rows, unit), F32),
            vm(*(2, 4, parts, tall, unit) if spread else (1, parts, tall, unit)),
            vm(*only(3, parts, tall, unit)),
            vm(*only(parts, tall, unit)),
            vm(*only(tall + qrow, unit)),
            vm(*only(4, qrow, unit)),
            vm(*only(3, qrow, unit)),
            dma(3, parts), dma(2, parts), dma(2, parts), dma(2, parts, 5), dma(4), dma(4), dma(2, parts),
            dma(2, parts + 1), dma(2, 3, parts + 1), dma(2, 2, parts), dma(2, 3, 4), dma(2, 4, 4), dma(2), dma(2, 3),
        ] + [dma(2, parts), dma(6, parts), dma(8, parts)] * 3,
        compiler_params=pltpu.CompilerParams(vmem_limit_bytes=LIMIT, collective_id=0, has_side_effects=True),
    )(seq, live, tokens, cot, w, biases, up, down, ow, rest, main, late)


def pair_rows(w, axis):
    heads = [lax.slice_in_dim(w, k * HEAD, (k + 1) * HEAD, axis=axis) for k in range(9)]
    order = [heads[3 * (k % 2) + k // 2] for k in range(6)] + heads[6:] + [jnp.zeros_like(heads[0])]
    return jnp.concatenate(order, axis=axis)


def local(
    groups,
    tokens,
    cotangent,
    seq_length,
    live_rows,
    qkv_weight,
    qv_bias,
    out_weight,
    out_bias,
    up_weight,
    up_bias,
    down_weight,
    down_bias,
):
    parts = groups["tensor"]
    spread = groups["dp"] == 8
    nd = 8 if spread else 1
    rows, width = tokens.shape
    unit = width + 1
    piece = unit // nd

    w = jnp.transpose(qkv_weight, (1, 2, 0)).reshape(9 * HEAD, width)
    b = pair_rows(jnp.concatenate([qv_bias[0], jnp.zeros_like(qv_bias[0]), qv_bias[1]]), 0)
    flat = [v if v.shape[0] == unit else jnp.pad(v, (0, unit - v.shape[0])) for v in (b, up_bias, out_bias, down_bias)]
    biases = jnp.stack(flat).astype(F32)
    if spread:
        full = [tokens] * 3
    else:
        wide = lambda v, tall=0: jnp.pad(v, ((0, tall), (0, unit - v.shape[1])))
        own = [wide(out_weight, 64), jnp.concatenate([up_weight, up_bias[None], wide(down_weight)]), wide(pair_rows(w, 0))]
        full = [lax.all_gather(v, "tensor", axis=0, tiled=False)[None] for v in own]
    mixed, token_grad, _, up_sum, down_sum, rest_sum, wg_sum, _, _, _, wg = layer(
        seq_length, live_rows, tokens, cotangent, w, biases, up_weight, down_weight, out_weight, *full, parts, spread
    )
    if spread:
        up_sum, down_sum, rest_sum = up_sum.reshape(unit, unit), down_sum.reshape(unit, unit), rest_sum.reshape(256, unit)
        wg = wg_sum.reshape(640, unit)[: 9 * HEAD].astype(F32)
    else:
        mine = lax.psum_scatter(up_sum[0].astype(F32), "tensor", scatter_dimension=0, tiled=False)
        mine, wg = lax.psum((mine, wg), "dp")
        up_sum, down_sum, rest_sum = mine[:unit], mine[unit : 2 * unit], mine[2 * unit :]
        wg = jnp.concatenate([wg[(2 * k if k < 3 else 2 * k - 5 if k < 6 else k) * HEAD :][:HEAD] for k in range(9)])
    up_grad = up_sum.astype(F32)
    down_grad = down_sum[:, :width].astype(F32)
    rest = rest_sum.astype(F32)
    biases = wg[:, width].reshape(3, 3 * HEAD)
    return (
        mixed,
        token_grad,
        jnp.transpose(wg[:, :width].reshape(3, 3 * HEAD, width), (2, 0, 1)),
        jnp.stack([biases[0], biases[2]]),
        rest[: 3 * HEAD, :width],
        rest[3 * HEAD, :width],
        up_grad[:width],
        up_grad[width],
        down_grad,
        rest[3 * HEAD + 1, :width],
    )


def solution(mesh):
    placed = (
        P(BOTH, None),
        P(BOTH, None),
        P("dp"),
        P("dp"),
        P(None, None, "tensor"),
        P(None, "tensor"),
        P("tensor", None),
        P(),
        P(None, "tensor"),
        P("tensor"),
        P("tensor", None),
        P(),
    )
    return jax.shard_map(
        partial(local, dict(mesh.shape)),
        mesh=mesh,
        in_specs=placed,
        out_specs=(
            P(BOTH, None),
            P(BOTH, None),
            P(None, None, "tensor"),
            P(None, "tensor"),
            P("tensor", None),
            P(),
            P(None, "tensor"),
            P("tensor"),
            P("tensor", None),
            P(),
        ),
        check_vma=False,
    )
```

```python
from functools import partial

import jax
import jax.numpy as jnp
from jax import lax
from jax.experimental import pallas as pl
from jax.experimental.pallas import tpu as pltpu
from jax.sharding import PartitionSpec as P

HEAD = 64
LANES = 128
EPSILON = 1e-05
HIDE = -1e30
BF = jnp.bfloat16
F32 = jnp.float32
BOTH = ("dp", "tensor")
VMEM = pl.BlockSpec(memory_space=pltpu.VMEM)
SMEM = pl.BlockSpec(memory_space=pltpu.SMEM)
ANY = pl.BlockSpec(memory_space=pl.ANY)
LIMIT = 63 * 1024 * 1024
EARLY = 2


def nn(a, b):
    return lax.dot_general(a, b, (((1,), (0,)), ((), ())), preferred_element_type=F32)


def nt(a, b):
    return lax.dot_general(a, b, (((1,), (1,)), ((), ())), preferred_element_type=F32)


def tn(a, b):
    return lax.dot_general(a, b, (((0,), (0,)), ((), ())), preferred_element_type=F32)


def lane_ids(rows):
    return lax.broadcasted_iota(jnp.int32, (rows, LANES), 1)


def half_turn(x):
    return pltpu.roll(x, HEAD, 1)


def fold(x):
    half = x.shape[0] // 2
    return jnp.where(lane_ids(half) < HEAD, x[:half], half_turn(x[half:]))


def unfold(x):
    low = lane_ids(x.shape[0]) < HEAD
    zero = jnp.zeros_like(x)
    return jnp.concatenate(
        [jnp.where(low, x, zero), jnp.where(low, half_turn(x), zero)], axis=0
    )


def split3(x):
    high = x.astype(BF).astype(F32)
    rest = x - high
    mid = rest.astype(BF).astype(F32)
    return high, mid, rest - mid


def norm_stats(x, width):
    s1 = jnp.sum(x, axis=-1, keepdims=True)
    s2 = jnp.sum(x * x, axis=-1, keepdims=True)
    return s1, lax.rsqrt((s2 + s1 * s1) / width + EPSILON)


def norm_pull(x, s1, r, g, width):
    dot = jnp.sum(g * x, axis=-1, keepdims=True)
    return g * r - (r * r * r * dot / width) * (x + s1)


def widen(ref, scratch):
    rows, width = ref.shape
    wide = scratch.shape[1]
    scratch[:, wide - LANES :] = jnp.zeros((rows, LANES), F32)
    scratch[:, :width] = ref[...].astype(F32)


def diag_mask(first, rows, live, turned):
    q_dim, k_dim = (1, 0) if turned else (0, 1)
    q = lax.broadcasted_iota(jnp.int32, (rows, rows), q_dim)
    k = lax.broadcasted_iota(jnp.int32, (rows, rows), k_dim)
    seen = (k <= q) & ((k + first < live) | (k == q))
    return jnp.where(seen, 0.0, HIDE).astype(F32)


def at_rows(i, rows):
    return pl.ds(pl.multiple_of(i * rows, rows), rows)


def fill_rows(dst, src, first, rows, width):
    wide = dst.shape[1]
    dst[first : first + rows, wide - LANES :] = jnp.zeros((rows, LANES), dst.dtype)
    dst[first : first + rows, :width] = src


class Sends:
    def __init__(self):
        self.ends = []

    def start(self, copy, when=None):
        if when is None:
            copy().start()
        else:
            pl.when(when())(lambda: copy().start())
        self.ends.append((copy, when))

    def finish(self):
        for copy, when in self.ends:
            if when is None:
                copy().wait_send()
            else:
                pl.when(when())(lambda copy=copy: copy().wait_send())


def remote(src, dst, ssem, rsem, **where):
    return pltpu.make_async_remote_copy(
        src_ref=src,
        dst_ref=dst,
        send_sem=ssem,
        recv_sem=rsem,
        device_id=where,
        device_id_type=pl.DeviceIdType.MESH,
    )


def neighbours(d):
    core, x, y = d % 2, (d // 2) % 2, d // 4
    return d + 1 - 2 * core, d + 2 - 4 * x, d + 4 - 8 * y


def greet(d, t, parts, spread, corner=False):
    barrier = pltpu.get_barrier_semaphore()

    def signal(**where):
        pl.semaphore_signal(barrier, inc=1, device_id=where, device_id_type=pl.DeviceIdType.MESH)

    for k in range(1, parts):
        signal(tensor=lax.rem(t + k, parts))
    if spread:
        core_n, x_n, y_n = neighbours(d)
        for n in (core_n, x_n, y_n) + ((x_n + y_n - d,) if corner else ()):
            signal(dp=n)
    return lambda: pl.semaphore_wait(barrier, parts - 1 + (3 + corner) * spread)


class Spread:
    def __init__(self, d, t, parts, piece, full, zsem, xsem, csem, sends, times):
        self.d, self.t, self.parts, self.piece, self.full, self.times = d, t, parts, piece, full, times
        self.zsem, self.xsem, self.csem, self.sends = zsem, xsem, csem, sends
        self.core_n, self.x_n, self.y_n = neighbours(d)
        self.diag = self.x_n + self.y_n - d

    def slot(self, e, b):
        return self.full.at[e, b]

    def out(self, to, ok):
        self.sends.start(
            lambda: remote(self.piece, self.slot(self.d, self.t), self.zsem.at[0, to], self.zsem.at[1, self.t], tensor=to), ok
        )

    def plane(self, b, first, ok):
        d, xs = self.d, self.xsem
        src = lambda: self.piece if first else self.slot(d, b)
        self.sends.start(lambda: remote(src(), self.slot(d, b), xs.at[0, b], xs.at[1, b], dp=self.x_n), ok)
        self.sends.start(lambda: remote(src(), self.slot(d, b), xs.at[2, b], xs.at[3, b], dp=self.y_n), ok)
        self.sends.start(
            lambda: remote(src(), self.slot(d, b), self.csem.at[0, b], self.csem.at[4, b], dp=self.core_n), ok
        )

    def arrive(self, b, ok):
        def wait():
            remote(self.slot(self.d, b), self.slot(self.d, b), self.zsem.at[0, b], self.zsem.at[1, b], tensor=b).wait_recv()

        pl.when(ok())(wait)
        self.plane(b, False, ok)

    def across(self, b, ok):
        xs, cs = self.xsem, self.csem
        east = lambda: self.slot(self.x_n, b)
        north = lambda: self.slot(self.y_n, b)

        def wait():
            remote(east(), east(), xs.at[0, b], xs.at[1, b], dp=self.x_n).wait_recv()
            remote(north(), north(), xs.at[2, b], xs.at[3, b], dp=self.y_n).wait_recv()

        pl.when(ok())(wait)
        self.sends.start(
            lambda: remote(east(), east(), xs.at[4, b], xs.at[5, b], dp=self.y_n), lambda: ok() & (b % 2 == 0)
        )
        self.sends.start(
            lambda: remote(north(), north(), xs.at[4, b], xs.at[5, b], dp=self.x_n), lambda: ok() & (b % 2 == 1)
        )
        self.sends.start(lambda: remote(east(), east(), cs.at[1, b], cs.at[5, b], dp=self.core_n), ok)
        self.sends.start(lambda: remote(north(), north(), cs.at[2, b], cs.at[6, b], dp=self.core_n), ok)

    def corner(self, b, ok):
        far, xs, cs = (lambda: self.slot(self.diag, b)), self.xsem, self.csem
        pl.when(ok())(lambda: remote(far(), far(), xs.at[4, b], xs.at[5, b], dp=self.x_n).wait_recv())
        self.sends.start(lambda: remote(far(), far(), cs.at[3, b], cs.at[7, b], dp=self.core_n), ok)

    def at(self, point):
        own = lambda: self.t >= 0
        for job in ("out", "plane", "arrive", "across", "corner"):
            for (k, m), when in self.times[job].items():
                if when != point:
                    continue
                if k == m:
                    self.plane(self.t, True, own) if job == "plane" else getattr(self, job)(self.t, own)
                    continue
                for mirror in (False, True):
                    here, there = (self.parts - 1 - k, self.parts - 1 - m) if mirror else (k, m)
                    getattr(self, job)(there, lambda here=here: self.t == here)

    def ready(self, b):
        shift = self.core_n - self.d
        for k, e in enumerate((self.d, self.x_n, self.y_n, self.diag)):
            there = self.slot(e + shift, b)
            remote(there, there, self.csem.at[k, b], self.csem.at[4 + k, b], dp=self.core_n).wait_recv()


PAIRS = [(k, m) for k in range(4) for m in range(k)]
REST_TIMES = {
    "out": {(m, k): "p1" for k, m in PAIRS},
    "plane": {(0, 0): "p0"},
    "arrive": {pair: "p3" for pair in PAIRS},
    "across": {(0, 0): "p1", **{pair: "h0" for pair in PAIRS}},
    "corner": {(0, 0): "p2", **{pair: "h1" for pair in PAIRS}},
}
MAIN_TIMES = {
    "out": {(2, 3): "p0", (0, 1): "p1", (1, 2): "p2", (0, 2): "p2", (1, 3): "h2", (0, 3): "p3"},
    "plane": {(0, 0): "p0"},
    "arrive": {(3, 2): "p1", (1, 0): "p2", (2, 1): "h1", (2, 0): "h1", (3, 1): "h1", (3, 0): "h2"},
    "across": {(0, 0): "p1", (3, 2): "p3", (1, 0): "h0", (2, 0): "h2", (2, 1): "e", (3, 1): "e", (3, 0): "q0"},
    "corner": {(0, 0): "p2", (3, 2): "h0", (1, 0): "h1", (2, 0): "e", (3, 1): "q0", (2, 1): "q1", (3, 0): "q1"},
}
LATE_TIMES = {
    "out": {(m, k): "e" for k, m in PAIRS},
    "plane": {(0, 0): "p0"},
    "arrive": {pair: "q0" for pair in PAIRS},
    "across": {(0, 0): "p1", **{pair: "q1" for pair in PAIRS}},
    "corner": {(0, 0): "p2", **{pair: "q2" for pair in PAIRS}},
}
SENT = (2,)
SERVE = {(0, 0): ((), (0, 1)), (0, 1): ((3, 4), ()), (1, 0): ((), (2,)), (2, 1): ((), (3, 4))}


def owner_order(d):
    return 4 * (d % 2) + d // 2


def layer_kernel(
    spread, seq_ref, live_ref, tok_ref, cot_any, w_any, bias_ref, up_any, down_any, ow_any, rest_in, main_in, late_in,
    mixed_ref, out_ref, o_any, fin_any, fin_down, fin_rest, fin_wg, rest_out, main_out, late_out, r1_any,
    n1_ref, wq, piece, qx_ref, kx_ref, vx_ref, pack_ref, heads_in, hg_in, recv_ref, hid_ref, gbuf, r2, r3, fst, w1, w2,
    nsem, hsem, gsem, qsem, own_sem, lsem, wsem, s1, s2, s3, s4, s5, u1, u2, *gsems,
):
    rows, width = tok_ref.shape
    unit = n1_ref.shape[1]
    blocks = parts = heads_in.shape[0]
    nd = 8 if spread else 1
    share, tail, qrow = unit // nd, 256 // nd, 640 // nd
    d, t = lax.axis_index("dp"), lax.axis_index("tensor")
    core = d % 2
    barrier = greet(d, t, parts, spread, True)
    sends, heads_sends = Sends(), Sends()
    seq, live = seq_ref[0], live_ref[0]
    lane = lane_ids(rows)
    low = lane < HEAD
    row = lax.broadcasted_iota(jnp.int32, (rows, LANES), 0)
    spare = lax.broadcasted_iota(jnp.int32, (rows, unit), 1) == width
    rest_full, main_full, late_full = (rest_out, main_out, late_out) if spread else (rest_in, main_in, late_in)
    gathers = []
    if spread:
        main_piece, rest_piece = piece.at[pl.ds(0, 2 * share)], piece.at[pl.ds(2 * share, tail)]
        late_piece = piece.at[pl.ds(2 * share + tail, qrow)]
        for k, (own, full, times) in enumerate(
            ((rest_piece, rest_out, REST_TIMES), (main_piece, main_out, MAIN_TIMES), (late_piece, late_out, LATE_TIMES))
        ):
            gathers.append(Spread(d, t, parts, own, full, *gsems[3 * k : 3 * k + 3], sends, times))

    def point(name):
        for gather in gathers:
            gather.at(name)

    def when_point(cond, name):
        if spread:
            pl.when(cond)(lambda: point(name))

    def turn(k):
        a, b = (t + k - 2 * (t % 2) * (k % 2)) % 2, t // 2 + k // 2 - 2 * (t // 2) * (k // 2)
        return a + 2 * b

    def prologue(wide, w_sc, up_sc, down_sc, ow_sc):
        loads = [
            pltpu.make_async_copy(src, dst, lsem.at[k])
            for k, (src, dst) in enumerate(((w_any, w_sc), (up_any, up_sc), (down_any, down_sc), (ow_any, ow_sc)))
        ]
        for load in loads if spread else loads[:1]:
            load.start()
        widen(tok_ref, wide)
        x = wide[...]
        _, r = norm_stats(x, width + 1)
        n1_ref[at_rows(t, rows), :] = jnp.where(spare, 1.0, x * r).astype(BF)
        barrier()
        for up in (True, False):
            sends.start(lambda up=up: line(t, up), lambda up=up: edge(up))
        loads[0].wait()
        for k in range(9):
            take = 3 * (k % 2) + k // 2 if k < 6 else k
            fill_rows(wq, w_sc[take * HEAD : (take + 1) * HEAD, :], k * HEAD, HEAD, width)
        wq[9 * HEAD : 10 * HEAD, :] = jnp.zeros((HEAD, unit), BF)
        if not spread:
            return
        near = share - 16
        piece[:, unit - LANES :] = jnp.zeros((piece.shape[0], LANES), BF)
        for load in loads[1:]:
            load.wait()
        piece[:near, :] = up_sc[pl.ds(pl.multiple_of(d * share, 16), near), :]

        @pl.when(d < nd - 1)
        def _():
            piece[near:share, :] = up_sc[pl.ds(pl.multiple_of(d * share + near, 16), 16), :]

        @pl.when(d == nd - 1)
        def _():
            last = jnp.concatenate([up_sc[width - 15 :, :].astype(F32), bias_ref[1:2, :]], axis=0)
            piece[near:share, :] = last.astype(BF)

        piece[share : 2 * share, :width] = down_sc[pl.ds(pl.multiple_of(d * share, 16), share), :]

        @pl.when(d < 6)
        def _():
            piece[2 * share : 2 * share + tail, :width] = ow_sc[pl.ds(pl.multiple_of(d * tail, 16), tail), :]

        @pl.when(d >= 6)
        def _():
            piece[2 * share : 2 * share + tail, :] = jnp.zeros((tail, unit), BF)

        piece[2 * share + tail :, :] = wq[pl.ds(pl.multiple_of(d * qrow, 16), qrow), :]

    def line(b, up):
        block = n1_ref.at[at_rows(b, rows), :]
        return remote(block, block, nsem.at[1 if up else 2, b], nsem.at[0, b], tensor=t + 1 if up else t - 1)

    def edge(up):
        return t < parts - 1 if up else t > 0

    def place(s, up):
        b = t - s if up else t + s
        return b, (lambda: t - s >= 0) if up else (lambda: t + s < parts)

    places = {(s, up): place(s, up) for s in range(1, parts) for up in (True, False)}
    pl.run_scoped(
        prologue,
        pltpu.VMEM((rows, unit), F32),
        pltpu.VMEM(w_any.shape, BF),
        pltpu.VMEM(up_any.shape, BF),
        pltpu.VMEM(down_any.shape, BF),
        pltpu.VMEM(ow_any.shape, BF),
    )
    homes = []
    if spread:
        for k, gather in enumerate(gathers):
            homes.append(pltpu.make_async_copy(gather.piece, gather.slot(d, t), own_sem.at[k]))
            homes[-1].start()
        point("p0")

    def attend(o_ref, mask_ref, s_ref):
        def project(i):
            at = at_rows(i, rows)
            qkv = nt(n1_ref[at, :], wq[: 10 * HEAD, :]) + bias_ref[:1, : 10 * HEAD]
            qkv = qkv.astype(BF).astype(F32)
            key = row + i * rows
            m = lane - HEAD
            same = ((m * rows) ^ (i * rows)) < seq
            open_ = (m == i) | (same & (key < live))
            bias = jnp.where(m < blocks, jnp.where(open_, 0.0, HIDE), jnp.where(m < blocks + 3, 1.0, 0.0))
            hot = jnp.where(m == i, 1.0, 0.0)
            ones = jnp.where(m < 3, 1.0, 0.0)
            for h in range(3):
                pair = qkv[:, h * LANES : (h + 1) * LANES]
                qx_ref[h, at, :] = jnp.where(low, pair * HEAD**-0.5, hot).astype(BF)
                kx_ref[h, at, :] = jnp.where(low, half_turn(pair), bias).astype(BF)
                val = qkv[:, (3 + h // 2) * LANES : (4 + h // 2) * LANES]
                vx_ref[h, at, :] = jnp.where(low, half_turn(val) if h % 2 else val, ones).astype(BF)
            mask_ref[i] = diag_mask(i * rows, rows, live, False).astype(BF)

        for s in range(parts):
            if s:
                for up in (True, False):
                    b, ok = places[s, up]
                    pl.when(ok())(lambda b=b, up=up: line(b, up).wait_recv())
                    sends.start(lambda b=b, up=up: line(b, up), lambda ok=ok, up=up: ok() & edge(up))
                point(f"p{s}")

            def arrived(e, carry, s=s):
                b = t + (2 * e - 1) * s
                pl.when((b >= 0) & (b < parts))(lambda: project(b))
                return carry

            lax.fori_loop(0, 2 if s else 1, arrived, 0)

        def head(h, carry):
            for i in range(blocks):
                q = qx_ref[h, i * rows : (i + 1) * rows, :]
                top = None
                for j in range(i, -1, -1):
                    s = nt(q, kx_ref[h, j * rows : (j + 1) * rows, :])
                    if i == j:
                        s = s + mask_ref[i].astype(F32)
                    peak = jnp.max(s, axis=-1, keepdims=True)
                    top = peak if top is None else jnp.maximum(top, peak)
                    s_ref[j] = s
                acc = None
                for j in range(i + 1):
                    p = jnp.exp(s_ref[j] - top).astype(BF)
                    part = nn(p, vx_ref[h, j * rows : (j + 1) * rows, :])
                    acc = part if acc is None else acc + part
                mass = acc[:, HEAD : HEAD + 1]
                lse = top + jnp.log(mass)
                o_ref[h, i * rows : (i + 1) * rows, :] = acc / mass
                hi, mid, lo = split3(-lse)
                ext = jnp.where(
                    lane == HEAD + blocks,
                    hi,
                    jnp.where(lane == HEAD + blocks + 1, mid, jnp.where(lane == HEAD + blocks + 2, lo, q.astype(F32))),
                )
                qx_ref[h, i * rows : (i + 1) * rows, :] = ext.astype(BF)
            for k in range(3):
                when_point(h == k, f"h{k}")
            return carry

        lax.fori_loop(0, 3, head, 0)
        keep = pltpu.make_async_copy(o_ref, o_any, lsem.at[0])
        keep.start()

        def pack(i, carry):
            at = at_rows(i, rows)
            pack_ref[i, :rows, :] = jnp.where(low, o_ref[0, at, :], half_turn(o_ref[1, at, :])).astype(BF)
            pack_ref[i, rows:, :] = fold(o_ref[2, at, :]).astype(BF)
            return carry

        lax.fori_loop(0, blocks, pack, 0)
        swap_start(pack_ref, heads_in, hsem, heads_sends)
        point("e")
        keep.wait()

    def swap(src_ref, dst_ref, sems, k, taking):
        to = lax.rem(t + (parts - k if taking else k), parts)
        src, dst = (to, to) if taking else (to, t)
        return remote(src_ref.at[src], dst_ref.at[dst], sems.at[0, k], sems.at[1, k], tensor=to)

    def swap_home(src_ref, dst_ref, sems):
        return pltpu.make_async_copy(src_ref.at[t], dst_ref.at[t], sems.at[0, 0])

    def swap_start(src_ref, dst_ref, sems, sends):
        for k in (2, 1, 3):
            sends.start(lambda k=k: swap(src_ref, dst_ref, sems, k, False))
        swap_home(src_ref, dst_ref, sems).start()

    def swap_end(src_ref, dst_ref, sems):
        for k in range(1, parts):
            swap(src_ref, dst_ref, sems, k, True).wait_recv()
        swap_home(src_ref, dst_ref, sems).wait()

    pl.run_scoped(
        attend,
        pltpu.VMEM((3, rows * parts, LANES), F32),
        pltpu.VMEM((parts, rows, rows), BF),
        pltpu.VMEM((parts, rows, rows), F32),
    )

    core_n, x_n, y_n = neighbours(d)
    chips = (x_n, y_n, x_n + y_n - d)
    main_rows, rest_rows = pl.ds(0, 2 * share), pl.ds(2 * share, tail)
    half = gbuf.at[core] if spread else gbuf
    every = pl.ds(0, parts)

    def region(k):
        if isinstance(k, int) and k == parts:
            return every, rest_rows
        return turn(k), main_rows

    def to_core(k):
        which, at = region(k)
        return remote(gbuf.at[1 - core, :, which, at], r1_any.at[:, which, at], s1.at[0, k], s1.at[1, k], dp=core_n)

    def second(c, k):
        which, at = region(k)
        return remote(
            gbuf.at[core, chips[c] // 2, which, at], r2.at[c, which, at], s2.at[0, c, k], s2.at[1, c, k], dp=chips[c]
        )

    def add_core(k, stage, stage_rest):
        to_core(k).wait_recv()
        which, at = region(k)
        here = stage_rest if isinstance(k, int) and k == parts else stage
        load = pltpu.make_async_copy(r1_any.at[:, which, at], here, lsem.at[0])
        load.start()
        load.wait()
        for q in range(4):
            gbuf[core, q, which, at] = (gbuf[core, q, which, at].astype(F32) + here[q].astype(F32)).astype(BF)

    def third(k, m):
        b, at = turn(k), (main_rows, rest_rows)[m]
        return remote(gbuf.at[core, d // 2, b, at], r3.at[t, at], s3.at[0, m, b], s3.at[1, m, t], tensor=b)

    def send_second(k):
        for c in range(3):
            sends.start(lambda c=c: second(c, k))

    def sum_second(k):
        for c in range(3):
            second(c, k).wait_recv()
        which, at = region(k)
        total = gbuf[core, d // 2, which, at].astype(F32)
        for c in range(3):
            total = total + r2[c, which, at].astype(F32)
        gbuf[core, d // 2, which, at] = total.astype(BF)
        if k == parts:
            for j in range(1, parts):
                sends.start(lambda j=j: third(j, 1))
        elif k:
            sends.start(lambda: third(k, 0))

    def middle(wu, wd, wm, acts, ugs, xall, n2_ref, gb_ref, wide, dn_ref, stage):
        stage_rest = wm.at[pl.ds(0, 4)] if spread else None
        wo = wq

        def fetch(k, slot):
            return [
                pltpu.make_async_copy(main_full.at[:, turn(k), pl.ds(m * share, share), :], dst.at[slot], wsem.at[m, slot])
                for m, dst in enumerate((wu, wd))
            ]

        def fetch_start(k, slot):
            if spread:
                gathers[1].ready(turn(k))
            for copy in fetch(k, slot):
                copy.start()

        cot_load = pltpu.make_async_copy(cot_any, mixed_ref, lsem.at[1])
        cot_load.start()
        if spread:
            for home in homes[:2]:
                home.wait()
            for b in range(parts):
                gathers[0].ready(b)
        rest_load = pltpu.make_async_copy(rest_full, wm, lsem.at[0])
        rest_load.start()
        fetch_start(0, 0)
        cot_load.wait()
        widen(mixed_ref, wide)
        gb_ref[...] = wide[...].astype(BF)
        widen(tok_ref, wide)
        rest_load.wait()
        for b in range(parts):
            own = wm[:, b].reshape(tail * nd, unit)
            wo[b * LANES : (b + 1) * LANES, :] = own[:LANES]
            wo[parts * LANES + b * HEAD : parts * LANES + (b + 1) * HEAD, :] = own[LANES : LANES + HEAD]
        swap_end(pack_ref, heads_in, hsem)
        lows = []
        for b in range(parts):
            xall[:, b * LANES : (b + 1) * LANES] = heads_in[b, :rows, :]
            lows.append(unfold(heads_in[b, rows:, :].astype(F32)))
        for k in range(parts // 2):
            both = jnp.where(low, lows[2 * k], half_turn(lows[2 * k + 1]))
            xall[:, (parts + k) * LANES : (parts + k + 1) * LANES] = both.astype(BF)
        point("q0")
        hidden = wide[...] + nn(xall[...], wo[...]) + bias_ref[2:3, :]
        s1_, r = norm_stats(hidden, width + 1)
        n2_ref[...] = jnp.where(spare, 1.0, hidden * r).astype(BF)
        hid_ref[...] = hidden
        wide[...] = hidden + bias_ref[3:4, :]
        dn_ref[...] = jnp.zeros_like(dn_ref)
        root = (2 / jnp.pi) ** 0.5

        def store_grads(k, act, ug):
            b = turn(k)
            up_g = tn(n2_ref[...], ug).astype(BF)
            down_g = tn(act, gb_ref[...]).astype(BF)
            if spread:
                gbuf[:, :, b, :share, :] = up_g.reshape(2, 4, share, unit)
                gbuf[:, :, b, share : 2 * share, :] = down_g.reshape(2, 4, share, unit)
                to_core(k).start()
            else:
                gbuf[0, b, :share, :] = up_g
                gbuf[0, b, share : 2 * share, :] = down_g

        def unit_block(k, carry):
            slot = k % 2
            for copy in fetch(k, slot):
                copy.wait()
            up = wu[slot].reshape(unit, unit)
            down = wd[slot].reshape(unit, unit)

            def some_rows(i, carry):
                at = at_rows(i, rows // 2)
                u = nn(n2_ref[at, :], up)
                th = jnp.tanh(root * (u + 0.044715 * (u * u * u)))
                act = (0.5 * u * (1 + th)).astype(BF)
                slope = 0.5 * (1 + th) + (0.5 * u) * (1 - th * th) * (root * (1 + 0.134145 * (u * u)))
                acts[slot, at, :] = act
                wide[at, :] += nn(act, down)
                ug = (nt(gb_ref[at, :], down) * slope).astype(BF)
                ugs[slot, at, :] = ug
                dn_ref[at, :] += nt(ug, up)
                return carry

            lax.fori_loop(0, 2, some_rows, 0)
            pl.when(k < parts - 1)(lambda: fetch_start(k + 1, (k + 1) % 2))
            pl.when(k < EARLY)(lambda: store_grads(k, acts[slot], ugs[slot]))

            if spread:
                for m in range(1, EARLY + 1):
                    pl.when(k == m)(lambda m=m: add_core(m - 1, stage, stage_rest))
                pl.when(k == 1)(lambda: send_second(0))
                pl.when(k == 3)(lambda: send_second(1))
            for m in range(parts):
                when_point(k == m, f"q{m + 1}")
            return carry

        lax.fori_loop(0, parts, unit_block, 0)
        hidden = hid_ref[...]
        gout = gb_ref[...].astype(F32)
        hidgrad = gout + norm_pull(hidden, s1_, r, dn_ref[...], width + 1)
        ag = hidgrad.astype(BF)
        hg = nt(ag, wo[...])
        heads_sends.finish()
        for b in range(parts):
            pack_ref[b, :rows, :] = hg[:, b * LANES : (b + 1) * LANES].astype(BF)
            pair = hg[:, (parts + b // 2) * LANES : (parts + b // 2 + 1) * LANES]
            pack_ref[b, rows:, :] = fold(half_turn(pair) if b % 2 else pair).astype(BF)
        swap_start(pack_ref, hg_in, gsem, sends)
        point("g")
        mixed_ref[...] = wide[:, :width].astype(BF)
        hid_ref[...] = hidgrad
        out_bias_grad = jnp.sum(hidgrad, axis=0, keepdims=True)
        down_bias_grad = jnp.sum(gout, axis=0, keepdims=True)
        wide[...] = tn(xall[:, : parts * LANES], ag)
        dn_ref[: parts * HEAD, :] = tn(xall[:, parts * LANES :], ag)
        extra = lax.broadcasted_iota(jnp.int32, (HEAD, unit), 0)
        extra = jnp.where(extra == 0, out_bias_grad, jnp.where(extra == 1, down_bias_grad, 0.0))
        for b in range(parts):
            pair = wide[b * LANES : (b + 1) * LANES, :]
            low_part = dn_ref[b * HEAD : (b + 1) * HEAD, :]
            misc = jnp.concatenate([pair, low_part, extra], axis=0).astype(BF)
            if spread:
                gbuf[:, :, b, 2 * share :, :] = misc.reshape(2, 4, tail, unit)
            else:
                gbuf[0, b, 2 * share :, :] = misc
        if spread:
            to_core(parts).start()

        def late(k, carry):
            store_grads(k, acts[k % 2], ugs[k % 2])
            return carry

        lax.fori_loop(EARLY, parts, late, 0)
        if spread:
            for k in [parts] + list(range(EARLY, parts)):
                add_core(k, stage, stage_rest)
            for k in SENT:
                send_second(k)
        else:
            out = pltpu.make_async_copy(gbuf, fin_any, lsem.at[0])
            out.start()
            out.wait()

    square, low_square = pltpu.VMEM((rows, unit), F32), pltpu.VMEM((rows, unit), BF)
    pl.run_scoped(
        middle,
        pltpu.VMEM((2, nd, share, unit), BF),
        pltpu.VMEM((2, nd, share, unit), BF),
        pltpu.VMEM((nd, parts, tail, unit), BF),
        pltpu.VMEM((parts - EARLY, rows, unit), BF),
        pltpu.VMEM((parts - EARLY, rows, unit), BF),
        low_square,
        low_square,
        low_square,
        square,
        square,
        pltpu.VMEM((4, 2 * share, unit) if spread else (16, LANES), BF),
    )

    def back(gpack, wgb, dox, dvs, dqt, dk_ref, mask_ref, xt, wg_acc, wmq, dn_ref):
        local = Sends()
        wide = wg_acc.at[pl.ds(0, rows)]

        def o_load(i):
            return pltpu.make_async_copy(o_any.at[:, pl.ds(i * rows, rows), :], dk_ref.at[pl.ds(0, 3)], lsem.at[0])

        def w_load(k):
            return pltpu.make_async_copy(late_full.at[:, k], wmq.at[k], wsem.at[0, k])

        def swap_grads(k, p, taking):
            to = lax.rem(t + (parts - k if taking else k), parts)
            src, dst = (to, to) if taking else (to, t)
            at = pl.ds(p * rows, rows if p < 4 else rows // 2)
            return remote(gpack.at[src].at[at], recv_ref.at[dst].at[at], qsem.at[0, k, p], qsem.at[1, k, p], tensor=to)

        def send_grads(p):
            for k in (2, 1, 3):
                local.start(lambda k=k: swap_grads(k, p, False))

        o_load(0).start()

        def masks(i, carry):
            mask_ref[i] = diag_mask(i * rows, rows, live, True).astype(BF)
            return carry

        lax.fori_loop(0, blocks, masks, 0)
        swap_end(pack_ref, hg_in, gsem)
        for i in range(blocks):
            o_load(i).wait()
            pair = hg_in[i, :rows, :].astype(F32)
            last = unfold(hg_in[i, rows:, :].astype(F32))
            for h, g in enumerate((pair, half_turn(pair), last)):
                g = jnp.where(low, g, 0.0)
                hi, mid, lo = split3(-jnp.sum(g * dk_ref[h], axis=-1, keepdims=True))
                g = jnp.where(lane == HEAD, hi, jnp.where(lane == HEAD + 1, mid, jnp.where(lane == HEAD + 2, lo, g)))
                dox[h, i * rows : (i + 1) * rows, :] = g.astype(BF)
            if i + 1 < blocks:
                o_load(i + 1).start()
        if spread:
            homes[2].wait()
            for k in range(parts):
                gathers[2].ready(k)
        for k in range(parts):
            w_load(k).start()

        def head(h, carry):
            spot = lax.rem(h, 2)
            for j in range(blocks):
                keys = kx_ref[h, j * rows : (j + 1) * rows, :]
                keys_t = jnp.transpose(keys.astype(F32)).astype(BF)
                vals = vx_ref[h, j * rows : (j + 1) * rows, :]
                dk = dv = None
                for i in range(j, blocks):
                    q = qx_ref[h, i * rows : (i + 1) * rows, :]
                    do = dox[h, i * rows : (i + 1) * rows, :]
                    s = nt(keys, q)
                    if i == j:
                        s = s + mask_ref[i].astype(F32)
                    p = jnp.exp(s)
                    ds = (p * nt(vals, do)).astype(BF)
                    dv_part = nn(p.astype(BF), do)
                    dk_part = nn(ds, q)
                    dq_part = nn(keys_t, ds)
                    dk = dk_part if dk is None else dk + dk_part
                    dv = dv_part if dv is None else dv + dv_part
                    if j == 0:
                        dqt[i] = dq_part
                    else:
                        dqt[i] += dq_part
                dk_ref[j] = dk
                dvs[spot, j * rows : (j + 1) * rows, :] = dv.astype(BF)
                if spread:
                    for step, (sent, summed) in SERVE.items():
                        if step[1] == j:

                            @pl.when(h == step[0])
                            def _(sent=sent, summed=summed):
                                for k in sent:
                                    send_second(k)
                                for k in summed:
                                    sum_second(k)

            at = pl.ds(pl.multiple_of(h * rows, rows), rows)
            for i in range(blocks):
                dq = jnp.transpose(dqt[i]) * HEAD**-0.5
                gpack[i, at, :] = jnp.where(low, dq, half_turn(dk_ref[i])).astype(BF)
            for p in range(3):
                pl.when(h == p)(lambda p=p: send_grads(p))

            @pl.when(h == 1)
            def _():
                for i in range(blocks):
                    mine = pl.ds(i * rows, rows)
                    gpack[i, 3 * rows : 4 * rows, :] = jnp.where(low, dvs[0, mine, :].astype(F32), half_turn(dvs[1, mine, :].astype(F32))).astype(BF)
                send_grads(3)

            @pl.when(h == 2)
            def _():
                for i in range(blocks):
                    gpack[i, 4 * rows :, :] = fold(dvs[0, i * rows : (i + 1) * rows, :].astype(F32)).astype(BF)
                send_grads(4)

            return carry

        lax.fori_loop(0, 3, head, 0)
        home = pltpu.make_async_copy(gpack.at[t], recv_ref.at[t], qsem.at[0, 0, 0])
        home.start()

        def spread_lanes(ref, i):
            for k in range(4):
                xt[:, k * LANES : (k + 1) * LANES] = ref[i, k * rows : (k + 1) * rows, :]
            xt[:, 4 * LANES :] = unfold(ref[i, 4 * rows :, :].astype(F32)).astype(BF)

        wg_acc[...] = jnp.zeros_like(wg_acc)

        def weigh(i, carry):
            spread_lanes(gpack, i)
            wg_acc[...] += tn(xt[...], n1_ref[at_rows(i, rows), :])
            return carry

        lax.fori_loop(0, blocks, weigh, 0)
        tall = 2 * share + tail
        if spread:
            order = [2 * k if k < 3 else 2 * k - 5 if k < 6 else k for k in range(10)]
            natural = jnp.concatenate([wg_acc[k * HEAD : (k + 1) * HEAD, :] for k in order], axis=0)
            wgb[...] = natural.astype(BF).reshape(2, 4, qrow, unit)

            def w_first():
                return remote(wgb.at[1 - core], w1, u1.at[0], u1.at[1], dp=core_n)

            def w_second(c):
                return remote(wgb.at[core, chips[c] // 2], w2.at[c], u2.at[0, c], u2.at[1, c], dp=chips[c])

            local.start(w_first)
            w_first().wait_recv()
            for q in range(4):
                wgb[core, q] = (wgb[core, q].astype(F32) + w1[q].astype(F32)).astype(BF)
            for c in range(3):
                local.start(lambda c=c: w_second(c))
            total = wgb[core, d // 2].astype(F32)
            for c in range(3):
                w_second(c).wait_recv()
                total = total + w2[c].astype(F32)
            fst[tall:, :] = total.astype(BF)
            total = gbuf[core, d // 2, t].astype(F32)
            for k in range(1, parts):
                b = turn(k)
                for m, at in enumerate((main_rows, rest_rows)):
                    there = r3.at[b, at]
                    remote(there, there, s3.at[0, m, b], s3.at[1, m, b], tensor=b).wait_recv()
                total = total + r3[b].astype(F32)
            fst[:tall, :] = total.astype(BF)

            cuts = ((fin_any, 0, share), (fin_down, share, share), (fin_rest, 2 * share, tail), (fin_wg, tall, qrow))

            def piece_of(m, e):
                return cuts[m][0].at[e]

            def sum_of(m):
                return fst.at[pl.ds(cuts[m][1], cuts[m][2])]

            def give(c, m):
                return remote(sum_of(m), piece_of(m, owner_order(d)), s4.at[0, c, m], s4.at[1, c, m], dp=chips[c])

            def came(c, m):
                there = piece_of(m, owner_order(chips[c]))
                return remote(there, there, s4.at[0, c, m], s4.at[1, c, m], dp=chips[c])

            def give_core(c, m):
                there = piece_of(m, owner_order(d if c == 3 else chips[c]))
                return remote(sum_of(m) if c == 3 else there, there, s5.at[0, c, m], s5.at[1, c, m], dp=core_n)

            owns = [
                pltpu.make_async_copy(sum_of(m), piece_of(m, owner_order(d)), lsem.at[m]) for m in range(4)
            ]
            for m in range(4):
                owns[m].start()
                for c in (2, 0, 1):
                    sends.start(lambda c=c, m=m: give(c, m))
                sends.start(lambda m=m: give_core(3, m))
        else:
            out = pltpu.make_async_copy(wg_acc, r1_any, own_sem.at[3])
            out.start()
            out.wait()
        widen(tok_ref, wide)
        dn_ref[...] = jnp.zeros_like(dn_ref)
        home.wait()
        for k in range(1, parts):
            for p in range(5):
                swap_grads(k, p, True).wait_recv()
        for k in range(parts):
            w_load(k).wait()

        def part(b, carry):
            spread_lanes(recv_ref, b)
            dn_ref[...] += nn(xt[...], wmq[b].reshape(nd * qrow, unit))
            return carry

        lax.fori_loop(0, parts, part, 0)
        x = wide[...]
        s1_, r = norm_stats(x, width + 1)
        grad = hid_ref[...] + norm_pull(x, s1_, r, dn_ref[...], width + 1)
        out_ref[...] = grad[:, :width].astype(BF)
        if spread:
            for c in range(3):
                for m in range(4):
                    came(c, m).wait_recv()
                    sends.start(lambda c=c, m=m: give_core(c, m))
            for c in range(4):
                for m in range(4):
                    give_core(c, m).wait_recv()
            for own in owns:
                own.wait()
        local.finish()

    pack = (parts, 4 * rows + rows // 2, LANES)
    pl.run_scoped(
        back,
        pltpu.VMEM(pack, BF),
        pltpu.VMEM((2, 4, qrow, unit) if spread else (16, LANES), BF),
        pltpu.VMEM((3, rows * parts, LANES), BF),
        pltpu.VMEM((2, rows * parts, LANES), BF),
        pltpu.VMEM((parts, LANES, rows), F32),
        pltpu.VMEM((parts, rows, LANES), F32),
        pltpu.VMEM((parts, rows, rows), BF),
        pltpu.VMEM((rows, 5 * LANES), BF),
        pltpu.VMEM((5 * LANES, unit), F32),
        pltpu.VMEM((parts, nd, qrow, unit), BF),
        square,
    )
    if spread:
        for k in range(parts + 1):
            to_core(k).wait_send()
    sends.finish()


def layer(seq, live, tokens, cot, w, biases, up, down, ow, rest, main, late, parts, spread):
    rows, width = tokens.shape
    unit = width + 1
    total = rows * parts
    nd = 8 if spread else 1
    share, tail, qrow = unit // nd, 256 // nd, 640 // nd
    tall = 2 * share + tail
    heads = (parts, rows + rows // 2, LANES)
    dma = lambda *shape: pltpu.SemaphoreType.DMA(shape)
    only = lambda *shape: shape if spread else (1, 1, 16, LANES)
    shape = jax.ShapeDtypeStruct
    vm = lambda *s: pltpu.VMEM(s, BF)
    return pl.pallas_call(
        partial(layer_kernel, spread),
        out_shape=(
            shape((rows, width), BF),
            shape((rows, width), BF),
            shape((3, total, LANES), F32),
            shape((8, share, unit) if spread else (1, parts, tall, unit), BF),
            shape(only(8, share, unit), BF),
            shape(only(8, tail, unit), BF),
            shape(only(8, qrow, unit), BF),
            shape(only(8, parts, tail, unit), BF),
            shape(only(8, parts, 2 * share, unit), BF),
            shape(only(8, parts, qrow, unit), BF),
            shape((4, parts, tall, unit), BF) if spread else shape((640, unit), F32),
        ),
        in_specs=[SMEM, SMEM, VMEM, ANY, ANY, VMEM] + [ANY] * 6,
        out_specs=(VMEM, VMEM) + (ANY,) * 9,
        scratch_shapes=[
            vm(total, unit),
            vm(unit, unit),
            vm(*(tall + qrow, unit) if spread else (16, LANES)),
            vm(3, total, LANES), vm(3, total, LANES), vm(3, total, LANES),
            vm(*heads), vm(*heads), vm(*heads),
            vm(parts, 4 * rows + rows // 2, LANES),
            pltpu.VMEM((rows, unit), F32),
            vm(*(2, 4, parts, tall, unit) if spread else (1, parts, tall, unit)),
            vm(*only(3, parts, tall, unit)),
            vm(*only(parts, tall, unit)),
            vm(*only(tall + qrow, unit)),
            vm(*only(4, qrow, unit)),
            vm(*only(3, qrow, unit)),
            dma(3, parts), dma(2, parts), dma(2, parts), dma(2, parts, 5), dma(4), dma(4), dma(2, parts),
            dma(2, parts + 1), dma(2, 3, parts + 1), dma(2, 2, parts), dma(2, 3, 4), dma(2, 4, 4), dma(2), dma(2, 3),
        ] + [dma(2, parts), dma(6, parts), dma(8, parts)] * 3,
        compiler_params=pltpu.CompilerParams(vmem_limit_bytes=LIMIT, collective_id=0, has_side_effects=True),
    )(seq, live, tokens, cot, w, biases, up, down, ow, rest, main, late)


def pair_rows(w, axis):
    heads = [lax.slice_in_dim(w, k * HEAD, (k + 1) * HEAD, axis=axis) for k in range(9)]
    order = [heads[3 * (k % 2) + k // 2] for k in range(6)] + heads[6:] + [jnp.zeros_like(heads[0])]
    return jnp.concatenate(order, axis=axis)


def local(
    groups,
    tokens,
    cotangent,
    seq_length,
    live_rows,
    qkv_weight,
    qv_bias,
    out_weight,
    out_bias,
    up_weight,
    up_bias,
    down_weight,
    down_bias,
):
    parts = groups["tensor"]
    spread = groups["dp"] == 8
    nd = 8 if spread else 1
    rows, width = tokens.shape
    unit = width + 1
    piece = unit // nd

    w = jnp.transpose(qkv_weight, (1, 2, 0)).reshape(9 * HEAD, width)
    b = pair_rows(jnp.concatenate([qv_bias[0], jnp.zeros_like(qv_bias[0]), qv_bias[1]]), 0)
    flat = [v if v.shape[0] == unit else jnp.pad(v, (0, unit - v.shape[0])) for v in (b, up_bias, out_bias, down_bias)]
    biases = jnp.stack(flat).astype(F32)
    if spread:
        full = [tokens] * 3
    else:
        wide = lambda v, tall=0: jnp.pad(v, ((0, tall), (0, unit - v.shape[1])))
        own = [wide(out_weight, 64), jnp.concatenate([up_weight, up_bias[None], wide(down_weight)]), wide(pair_rows(w, 0))]
        full = [lax.all_gather(v, "tensor", axis=0, tiled=False)[None] for v in own]
    mixed, token_grad, _, up_sum, down_sum, rest_sum, wg_sum, _, _, _, wg = layer(
        seq_length, live_rows, tokens, cotangent, w, biases, up_weight, down_weight, out_weight, *full, parts, spread
    )
    if spread:
        up_sum, down_sum, rest_sum = up_sum.reshape(unit, unit), down_sum.reshape(unit, unit), rest_sum.reshape(256, unit)
        wg = wg_sum.reshape(640, unit)[: 9 * HEAD].astype(F32)
    else:
        mine = lax.psum_scatter(up_sum[0].astype(F32), "tensor", scatter_dimension=0, tiled=False)
        mine, wg = lax.psum((mine, wg), "dp")
        up_sum, down_sum, rest_sum = mine[:unit], mine[unit : 2 * unit], mine[2 * unit :]
        wg = jnp.concatenate([wg[(2 * k if k < 3 else 2 * k - 5 if k < 6 else k) * HEAD :][:HEAD] for k in range(9)])
    up_grad = up_sum.astype(F32)
    down_grad = down_sum[:, :width].astype(F32)
    rest = rest_sum.astype(F32)
    biases = wg[:, width].reshape(3, 3 * HEAD)
    return (
        mixed,
        token_grad,
        jnp.transpose(wg[:, :width].reshape(3, 3 * HEAD, width), (2, 0, 1)),
        jnp.stack([biases[0], biases[2]]),
        rest[: 3 * HEAD, :width],
        rest[3 * HEAD, :width],
        up_grad[:width],
        up_grad[width],
        down_grad,
        rest[3 * HEAD + 1, :width],
    )


def solution(mesh):
    placed = (
        P(BOTH, None),
        P(BOTH, None),
        P("dp"),
        P("dp"),
        P(None, None, "tensor"),
        P(None, "tensor"),
        P("tensor", None),
        P(),
        P(None, "tensor"),
        P("tensor"),
        P("tensor", None),
        P(),
    )
    return jax.shard_map(
        partial(local, dict(mesh.shape)),
        mesh=mesh,
        in_specs=placed,
        out_specs=(
            P(BOTH, None),
            P(BOTH, None),
            P(None, None, "tensor"),
            P(None, "tensor"),
            P("tensor", None),
            P(),
            P(None, "tensor"),
            P("tensor"),
            P("tensor", None),
            P(),
        ),
        check_vma=False,
    )
```
